32 devices in a mesh: sx: 2 (over core), sy: 2 (over x), fsdp: 8 (over z, y).
Axes of the slice: x: 2, y: 2, z: 4, core: 2. Of those that a mesh axis runs over, the one named last changes fastest.
Arguments:
- x_code: bfloat16 [8, 16, 32, 1536], P('fsdp', 'sx', 'sy'), may hold values from -6 to 6
- x_exp: int32 [8, 16, 32, 12], P('fsdp', 'sx', 'sy'), may hold values from -2 to 2
- dw_kernel: float32 [7, 7, 1536], replicated, may hold values from -1.2 to 1.2
- dw_bias: float32 [1536], replicated, may hold values from -4 to 4
- ln_gain: float32 [1536], replicated, may hold values from 0.1 to 1.9
- ln_bias: float32 [1536], replicated, may hold values from -3 to 3
- w_up: bfloat16 [1536, 3072], P('fsdp'), may hold values from -0.15625 to 0.15625
- b_up: float32 [3072], replicated, may hold values from -3 to 3
- w_down: bfloat16 [3072, 1536], P(None, 'fsdp'), may hold values from -0.109375 to 0.109375
- b_down: float32 [1536], replicated, may hold values from -3 to 3
- layer_scale: float32 [1536], replicated, may hold values from 0.3 to 1.5
- cotangent: bfloat16 [8, 16, 32, 1536], P('fsdp', 'sx', 'sy'), may hold values from -6 to 6
Outputs:
- block_out: bfloat16 [8, 16, 32, 1536], P('fsdp', 'sx', 'sy')
- grad_input: bfloat16 [8, 16, 32, 1536], P('fsdp', 'sx', 'sy')
- grad_kernel: float32 [7, 7, 1536], replicated
- grad_gain: float32 [1536], replicated
- grad_scale: float32 [1536], replicated
The draws below stay inside these ranges and needn't reach their ends.
All inputs are finite; a program needn't handle non-finite values.
Results may differ from the reference program's by a relative error of at most 0.006.
Values may be sent and summed in bfloat16 or wider, within the bound.
No kernel may reach another device: no remote copies, remote signals or barrier semaphores. Data moves between devices by JAX's collectives and lax.ppermute only.
A program may use at most 192 MiB of HBM per device.

```python
import math
import jax
import jax.numpy as jnp
from jax import lax

C = 1536
FF = 3072
CG = 128
KW = 7
SLIDES = 8
H = 16
W = 32


def with_ends(entries, own_key, low, high):
    index_at = [jax.random.randint(jax.random.fold_in(own_key, axis), (), 0, length) for axis, length in enumerate(entries.shape)]
    main_axis = entries.shape.index(max(entries.shape))
    beside = index_at[:main_axis] + [(index_at[main_axis] + 1) % entries.shape[main_axis]] + index_at[main_axis + 1:]
    return entries.at[tuple(index_at)].set(low).at[tuple(beside)].set(high)


def steps_of(rng, extent, shards, low, high):
    gain, own = 1.0, jax.random.fold_in(rng, 6)
    for position, blocks in shards:
        heights = jnp.exp(jax.random.uniform(jax.random.fold_in(own, position), (blocks,), jnp.float32, low / len(shards), high / len(shards)))
        gain = gain * jnp.repeat(heights, extent[position] // blocks).reshape([-1 if axis == position else 1 for axis in range(len(extent))])
    return gain


def bell_draw(rng, dims, width, bound, pieces=(), kind=jnp.bfloat16):
    values = width * jax.random.normal(rng, dims, jnp.float32)
    if pieces:
        values = values * steps_of(rng, dims, pieces, -0.22, 0.18)
    return jnp.clip(values, -bound, bound).astype(kind)


def setup_inputs(seed: int = 0) -> dict:
    key_list = jax.random.split(jax.random.key(seed), 13)
    x_code = bell_draw(key_list[0], (SLIDES, H, W, C), 1.0, 6.0, ((0, 8), (1, 2), (2, 2)))
    x_exp = with_ends(jax.random.randint(key_list[1], (SLIDES, H, W, C // CG), -2, 3), jax.random.fold_in(key_list[1], 1), -2, 2).astype(jnp.int32)
    dw_kernel = bell_draw(key_list[2], (KW, KW, C), 0.2, 1.2, (), jnp.float32)
    dw_bias = bell_draw(key_list[3], (C,), 0.7, 4.0, (), jnp.float32)
    ln_gain = jnp.clip(1.0 + 0.18 * jax.random.normal(key_list[4], (C,), jnp.float32), 0.1, 1.9)
    ln_bias = bell_draw(key_list[5], (C,), 0.5, 3.0, (), jnp.float32)
    w_up = bell_draw(key_list[6], (C, FF), C ** -0.5, 0.15625, ((0, 8),))
    b_up = bell_draw(key_list[7], (FF,), 0.5, 3.0, (), jnp.float32)
    w_down = bell_draw(key_list[8], (FF, C), FF ** -0.5, 0.109375, ((1, 8),))
    b_down = bell_draw(key_list[9], (C,), 0.5, 3.0, (), jnp.float32)
    layer_scale = jnp.clip(jnp.exp(jax.random.uniform(key_list[10], (C,), jnp.float32, math.log(0.3), math.log(1.5))), 0.3, 1.5)
    cotangent = bell_draw(key_list[11], (SLIDES, H, W, C), 1.0, 6.0, ((0, 8), (1, 2), (2, 2)))
    return dict(x_code=x_code, x_exp=x_exp, dw_kernel=dw_kernel, dw_bias=dw_bias, ln_gain=ln_gain, ln_bias=ln_bias, w_up=w_up, b_up=b_up, w_down=w_down, b_down=b_down, layer_scale=layer_scale, cotangent=cotangent)


def gelu_tanh(v):
    return jax.nn.gelu(v, approximate=True)

def dequantize(code, expo):
    rows, cols, chans = code.shape
    factor = jnp.exp2(expo.astype(jnp.float32))
    grouped = code.astype(jnp.float32).reshape(rows, cols, chans // CG, CG) * factor[..., None]
    return grouped.reshape(rows, cols, chans).astype(jnp.bfloat16)

def one_slide(code, expo, grad_out, dw_kernel, dw_bias, ln_gain, ln_bias, w_up, b_up, w_down, b_down, layer_scale):
    rows, cols, chans = code.shape
    scaled = dequantize(code, expo)
    padded = jnp.pad(scaled.astype(jnp.float32), ((3, 3), (3, 3), (0, 0)))
    conv = jnp.zeros((rows, cols, chans), jnp.float32) + dw_bias
    for i in range(KW):
        for j in range(KW):
            conv = conv + dw_kernel[i, j] * padded[i:i + rows, j:j + cols]
    mean_val = lax.optimization_barrier(jnp.mean(conv, axis=-1, keepdims=True))
    centred = conv - mean_val
    rstd = lax.rsqrt(lax.optimization_barrier(jnp.mean(centred * centred, axis=-1, keepdims=True)) + 1e-06)
    normed = centred * rstd
    ln_out = (normed * ln_gain + ln_bias).astype(jnp.bfloat16).reshape(rows * cols, chans)
    pre = jnp.dot(ln_out, w_up, preferred_element_type=jnp.float32) + b_up
    act, gelu_back = jax.vjp(gelu_tanh, pre)
    mlp = jnp.dot(act.astype(jnp.bfloat16), w_down, preferred_element_type=jnp.float32) + b_down
    mlp = mlp.reshape(rows, cols, chans)
    block_out = (scaled.astype(jnp.float32) + layer_scale * mlp).astype(jnp.bfloat16)
    grad_f = grad_out.astype(jnp.float32)
    scale_term = lax.optimization_barrier(jnp.sum(grad_f * mlp, axis=(0, 1)))
    d_mlp = (layer_scale * grad_f).astype(jnp.bfloat16).reshape(rows * cols, chans)
    d_act = jnp.dot(d_mlp, w_down.T, preferred_element_type=jnp.float32)
    d_pre = gelu_back(d_act)[0].astype(jnp.bfloat16)
    d_ln = jnp.dot(d_pre, w_up.T, preferred_element_type=jnp.float32).reshape(rows, cols, chans)
    gain_term = lax.optimization_barrier(jnp.sum(d_ln * normed, axis=(0, 1)))
    d_norm = d_ln * ln_gain
    d_conv = rstd * (d_norm - lax.optimization_barrier(jnp.mean(d_norm, axis=-1, keepdims=True)) - normed * lax.optimization_barrier(jnp.mean(d_norm * normed, axis=-1, keepdims=True)))
    kernel_rows = []
    for i in range(KW):
        kernel_cols = []
        for j in range(KW):
            kernel_cols.append(lax.optimization_barrier(jnp.sum(d_conv * padded[i:i + rows, j:j + cols], axis=(0, 1))))
        kernel_rows.append(jnp.stack(kernel_cols))
    kernel_term = jnp.stack(kernel_rows)
    padded_grad = jnp.pad(d_conv, ((3, 3), (3, 3), (0, 0)))
    back_conv = grad_f
    for i in range(KW):
        for j in range(KW):
            back_conv = back_conv + dw_kernel[i, j] * padded_grad[6 - i:6 - i + rows, 6 - j:6 - j + cols]
    return (block_out, back_conv.astype(jnp.bfloat16), kernel_term, gain_term, scale_term)

def reference(x_code, x_exp, dw_kernel, dw_bias, ln_gain, ln_bias, w_up, b_up, w_down, b_down, layer_scale, cotangent):

    def per_slide(items):
        return one_slide(items[0], items[1], items[2], dw_kernel, dw_bias, ln_gain, ln_bias, w_up, b_up, w_down, b_down, layer_scale)
    block_out, grad_input, kernel_terms, gain_terms, scale_terms = lax.map(per_slide, (x_code, x_exp, cotangent))
    return (block_out, grad_input, lax.optimization_barrier(jnp.sum(kernel_terms, axis=0)), lax.optimization_barrier(jnp.sum(gain_terms, axis=0)), lax.optimization_barrier(jnp.sum(scale_terms, axis=0)))
```

```python
import jax
import jax.numpy as jnp
from jax import lax
from jax.sharding import PartitionSpec as P

CG = 128
KW = 7
BF = jnp.bfloat16
F32 = jnp.float32


def with_halo(shard, sides, width):
    for axis, dim in sides:
        devices, length = (lax.axis_size(axis), shard.shape[dim])
        up = [(i, (i + 1) % devices) for i in range(devices - 1)]
        down = [(j, i) for i, j in up]
        last = lax.slice_in_dim(shard, length - width, length, axis=dim)
        initial = lax.slice_in_dim(shard, 0, width, axis=dim)
        before = lax.ppermute(last, axis, up)
        after = lax.ppermute(initial, axis, down)
        shard = jnp.concatenate([before, shard, after], axis=dim)
    return shard


def ring_order(n):
    if n == 8:
        return [0, 2, 4, 6, 7, 5, 3, 1]
    return list(range(n))


def ring_gather(block):
    n, rows = lax.axis_size("fsdp"), block.shape[0]
    order = ring_order(n)
    place = [0] * n
    for k, d in enumerate(order):
        place[d] = k
    forth = [(order[k], order[(k + 1) % n]) for k in range(n)]
    back = [(d, s) for s, d in forth]
    me = jnp.asarray(place)[lax.axis_index("fsdp")]
    order = jnp.asarray(order)
    whole = jnp.zeros((n * rows,) + block.shape[1:], block.dtype)

    def put(whole, piece, k, offset=0):
        owner = order[(me + k) % n]
        return lax.dynamic_update_slice_in_dim(whole, piece, owner * rows + offset, 0)

    whole = put(whole, block, 0)
    one = two = block
    for k in range(1, (n + 1) // 2):
        one = lax.ppermute(one, "fsdp", forth)
        two = lax.ppermute(two, "fsdp", back)
        whole = put(whole, one, -k)
        whole = put(whole, two, k)
    if n % 2 == 0:
        half = rows // 2
        one = lax.ppermute(one[:half], "fsdp", forth)
        two = lax.ppermute(two[half:], "fsdp", back)
        whole = put(whole, one, -(n // 2))
        whole = put(whole, two, n // 2, half)
    return whole


def shift(a, axis, k):
    n = lax.axis_size(axis)
    return lax.ppermute(a, axis, [((i + k) % n, i) for i in range(n)])


def gather_tile(a):
    a = jnp.concatenate([a] + [shift(a, "sy", k) for k in range(1, lax.axis_size("sy"))], 0)
    return jnp.concatenate([a] + [shift(a, "sx", k) for k in range(1, lax.axis_size("sx"))], 0)


def scatter_tile(a):
    for axis in ("sx", "sy"):
        n = lax.axis_size(axis)
        a = a.reshape((n, a.shape[0] // n) + a.shape[1:])
        total = a[0].astype(F32)
        for k in range(1, n):
            total = total + shift(a[k].astype(BF), axis, -k).astype(F32)
        a = total
    return a[0]


def swap(a, axis, mask):
    return lax.ppermute(a, axis, [(i, i ^ mask) for i in range(lax.axis_size(axis))])


def sum_everywhere(a):
    half = a.shape[0] // 2
    core = lax.axis_index("sx") % 2
    mine = lax.dynamic_slice_in_dim(a, core * half, half, 0)
    other = lax.dynamic_slice_in_dim(a, (1 - core) * half, half, 0)
    total = mine + swap(other, "sx", 1)
    for axis in ("sx", "sy", "fsdp"):
        mask = 2 if axis == "sx" else 1
        while mask < lax.axis_size(axis):
            rounded = total.astype(BF)
            total = rounded.astype(F32) + swap(rounded, axis, mask).astype(F32)
            mask *= 2
    other = swap(total, "sx", 1)
    first = jnp.where(core == 0, total, other)
    second = jnp.where(core == 0, other, total)
    return jnp.concatenate([first, second], 0)


def gelu_tanh(v):
    return jax.nn.gelu(v, approximate=True)


def on_device(
    x_code,
    x_exp,
    dw_kernel,
    dw_bias,
    ln_gain,
    ln_bias,
    w_up,
    b_up,
    w_down,
    b_down,
    layer_scale,
    cotangent,
):
    code = x_code[0]
    rows, cols, chans = code.shape
    tiles = lax.axis_size("sx") * lax.axis_size("sy")
    quarter = lax.axis_index("sx") * lax.axis_size("sy") + lax.axis_index("sy")
    hidden = w_up.shape[1] // tiles
    up = ring_gather(lax.dynamic_slice_in_dim(w_up, quarter * hidden, hidden, 1))
    down = ring_gather(lax.dynamic_slice_in_dim(w_down, quarter * hidden, hidden, 0).T)
    bias_up = lax.dynamic_slice_in_dim(b_up, quarter * hidden, hidden, 0)

    factor = jnp.exp2(x_exp[0].astype(F32))
    grouped = code.astype(F32).reshape(rows, cols, chans // CG, CG) * factor[..., None]
    scaled = grouped.reshape(rows, cols, chans).astype(BF)
    grad_f = cotangent[0].astype(F32)
    d_mlp = gather_tile((layer_scale * grad_f).astype(BF).reshape(1, rows * cols, chans))
    d_mlp = d_mlp.reshape(tiles * rows * cols, chans)

    padded_x = with_halo(scaled[None], (("sx", 1), ("sy", 2)), 3)[0].astype(F32)
    conv = jnp.zeros((rows, cols, chans), F32) + dw_bias
    for i in range(KW):
        for j in range(KW):
            conv = conv + dw_kernel[i, j] * padded_x[i : i + rows, j : j + cols]
    mean_val = jnp.mean(conv, axis=-1, keepdims=True)
    centred = conv - mean_val
    rstd = lax.rsqrt(jnp.mean(centred * centred, axis=-1, keepdims=True) + 1e-06)
    normed = centred * rstd
    ln_out = (normed * ln_gain + ln_bias).astype(BF).reshape(1, rows * cols, chans)
    ln_all = gather_tile(ln_out).reshape(tiles * rows * cols, chans)

    pre = jnp.dot(ln_all, up, preferred_element_type=F32) + bias_up
    act, gelu_back = jax.vjp(gelu_tanh, pre)
    d_act = jnp.dot(d_mlp, down, preferred_element_type=F32)
    d_pre = gelu_back(d_act)[0].astype(BF)
    d_ln = lax.dot_general(d_pre, up, (((1,), (1,)), ((), ())), preferred_element_type=F32)
    d_ln = scatter_tile(d_ln.reshape(tiles, rows, cols, chans))
    mlp = lax.dot_general(
        act.astype(BF), down, (((1,), (1,)), ((), ())), preferred_element_type=F32
    )
    mlp = scatter_tile(mlp.reshape(tiles, rows, cols, chans)) + b_down
    block_out = (scaled.astype(F32) + layer_scale * mlp).astype(BF)
    scale_term = jnp.sum(grad_f * mlp, axis=(0, 1))

    gain_term = jnp.sum(d_ln * normed, axis=(0, 1))
    d_norm = d_ln * ln_gain
    d_conv = rstd * (
        d_norm
        - jnp.mean(d_norm, axis=-1, keepdims=True)
        - normed * jnp.mean(d_norm * normed, axis=-1, keepdims=True)
    )
    terms = []
    for i in range(KW):
        for j in range(KW):
            terms.append(jnp.sum(d_conv * padded_x[i : i + rows, j : j + cols], axis=(0, 1)))
    terms += [gain_term, scale_term]
    terms += [jnp.zeros_like(gain_term)] * (-len(terms) % 32)
    sums = sum_everywhere(jnp.stack(terms))
    padded_grad = with_halo(d_conv[None].astype(BF), (("sx", 1), ("sy", 2)), 3).astype(F32)[0]
    back_conv = grad_f
    for i in range(KW):
        for j in range(KW):
            back_conv = (
                back_conv
                + dw_kernel[i, j] * padded_grad[6 - i : 6 - i + rows, 6 - j : 6 - j + cols]
            )
    grad_input = back_conv.astype(BF)
    taps = KW * KW
    grad_kernel = sums[:taps].reshape(KW, KW, chans)
    return (block_out[None], grad_input[None], grad_kernel, sums[taps], sums[taps + 1])


def solution(mesh):
    placed = (
        P("fsdp", "sx", "sy", None),
        P("fsdp", "sx", "sy", None),
        P(),
        P(),
        P(),
        P(),
        P("fsdp", None),
        P(),
        P(None, "fsdp"),
        P(),
        P(),
        P("fsdp", "sx", "sy", None),
    )
    return jax.shard_map(
        on_device,
        mesh=mesh,
        in_specs=placed,
        out_specs=(P("fsdp", "sx", "sy", None), P("fsdp", "sx", "sy", None), P(), P(), P()),
        check_vma=False,
    )
```

```python
import functools

import jax
import jax.numpy as jnp
from jax import lax
from jax.experimental import pallas as pl
from jax.experimental.pallas import tpu as pltpu
from jax.sharding import PartitionSpec as P

CG = 128
KW = 7
HALO = 3
LANES = 128
SUBLANES = 8
BF = jnp.bfloat16
F32 = jnp.float32
MIB = 1024 * 1024
GELU_A = 0.7978845608028654
GELU_B = 0.044715


def vmem(count):
    return [pl.BlockSpec(memory_space=pltpu.VMEM)] * count


def anywhere(count):
    return [pl.BlockSpec(memory_space=pl.ANY)] * count


def params(mib):
    return pltpu.CompilerParams(vmem_limit_bytes=mib * MIB)


def cost(flops, moved, special=0):
    return pl.CostEstimate(flops=flops, bytes_accessed=moved, transcendentals=special)


def shaped(shape, dtype):
    return jax.ShapeDtypeStruct(tuple(shape), dtype)


def swap(a, **masks):
    axes = tuple(masks)
    mask = 0
    total = 1
    for axis in axes:
        n = lax.axis_size(axis)
        mask, total = mask * n + masks[axis], total * n
    return lax.ppermute(a, axes, [(i, i ^ mask) for i in range(total)])


def shift(a, axis, k):
    n = lax.axis_size(axis)
    return lax.ppermute(a, axis, [((i + k) % n, i) for i in range(n)])


def sides(axis):
    return (0,) if lax.axis_size(axis) == 2 else (-1, 1)


def side_pairs(n, side):
    if side == 0:
        return [(0, 1), (1, 0)]
    return [(i, i - side) for i in range(n) if 0 <= i - side < n]


def exchange_edges(pieces):
    n, m = lax.axis_size("sx"), lax.axis_size("sy")
    got = {}
    for (a, b), piece in pieces.items():
        rows = [(i, i) for i in range(n)] if a is None else side_pairs(n, a)
        cols = [(j, j) for j in range(m)] if b is None else side_pairs(m, b)
        pairs = [(i * m + j, k * m + l) for i, k in rows for j, l in cols]
        got[a, b] = lax.ppermute(piece, ("sx", "sy"), pairs)
    return got


def edge_keys():
    rows, cols = sides("sx"), sides("sy")
    return [(a, None) for a in rows] + [(None, b) for b in cols] + [(a, b) for a in rows for b in cols]


def place_of(index, n):
    if n != 8:
        return index
    return jnp.where(index % 2 == 0, index // 2, 7 - index // 2)


def at_place(place, n):
    if n != 8:
        return place
    return jnp.where(place < 4, 2 * place, 15 - 2 * place)


def ring_pairs(n):
    order = [0, 2, 4, 6, 7, 5, 3, 1] if n == 8 else list(range(n))
    forth = [(order[k], order[(k + 1) % n]) for k in range(n)]
    return forth, [(d, s) for s, d in forth]


def ring_gather(block):
    n, rows = lax.axis_size("fsdp"), block.shape[0]
    forth, back = ring_pairs(n)
    pieces, where = [block], [(0, 0, rows)]
    one = two = block
    for k in range(1, (n + 1) // 2):
        one = lax.ppermute(one, "fsdp", forth)
        two = lax.ppermute(two, "fsdp", back)
        pieces += [one, two]
        where += [(-k, 0, rows), (k, 0, rows)]
    if n % 2 == 0:
        half = rows // 2 if rows % 32 == 0 else 0
        if half:
            pieces.append(lax.ppermute(one[:half], "fsdp", forth))
            where.append((n // 2, 0, half))
        pieces.append(lax.ppermute(two[half:], "fsdp", back))
        where.append((n // 2, half, rows - half))
    return pieces, where


def gather_tile(a):
    out = []
    for t in range(lax.axis_size("sy")):
        mine = a if t == 0 else shift(a, "sy", t)
        out.append([mine] + [shift(mine, "sx", s) for s in range(1, lax.axis_size("sx"))])
    return [piece for group in out for piece in group]


def reduce_cores(pieces):
    return [pieces[0]] + [shift(pieces[s], "sx", -s) for s in range(1, len(pieces))]


def add_up(terms):
    total = terms[0].astype(F32)
    for term in terms[1:]:
        total = total + term.astype(F32)
    return total


def sum_rows(keep, send):
    total = keep + swap(send, sx=1)
    quarter = total.shape[0] // 4
    parts = total.reshape(4, quarter, total.shape[1])
    me = 2 * (lax.axis_index("sy") % 2) + lax.axis_index("fsdp") % 2

    def part(k):
        return lax.dynamic_index_in_dim(parts, me ^ k, 0, keepdims=False)

    total = (part(0) + swap(part(1), fsdp=1)) + (swap(part(2), sy=1) + swap(part(3), sy=1, fsdp=1))
    masks = []
    for axis in ("sx", "sy", "fsdp"):
        bit = 2
        while bit < lax.axis_size(axis):
            masks.append((axis, bit))
            bit *= 2
    while masks:
        group, masks = masks[:2], masks[2:]
        rounded = total.astype(BF)
        (axis, bit) = group[0]
        total = rounded.astype(F32) + swap(rounded, **{axis: bit}).astype(F32)
        if len(group) == 2:
            (other, more) = group[1]
            both = {axis: bit + more} if axis == other else {axis: bit, other: more}
            total = total + (swap(rounded, **{other: more}).astype(F32) + swap(rounded, **both).astype(F32))
    mine = [total, swap(total, fsdp=1), swap(total, sy=1), swap(total, sy=1, fsdp=1)]
    return mine, [swap(piece, sx=1) for piece in mine]


def write_edges(tile, refs):
    rows, cols = tile.shape[:2]
    for (a, b), ref in zip(edge_keys(), refs, strict=True):
        if a is None:
            value = tile[...]
        elif a == 0:
            first = jnp.where(lax.axis_index("sx") == 0, rows - HALO, 0)
            value = tile[pl.ds(first, HALO)]
        else:
            value = tile[pl.ds(0 if a > 0 else rows - HALO, HALO)]
        if b == 0:
            low, high = value[:, :HALO], value[:, cols - HALO :]
            value = jnp.where(lax.axis_index("sy") == 0, high, low)
        elif b is not None:
            value = value[:, :HALO] if b > 0 else value[:, cols - HALO :]
        ref[...] = value.astype(BF)


def edge_shapes(rows, cols, chans):
    return [shaped((rows if a is None else HALO, cols if b is None else HALO, chans), BF) for a, b in edge_keys()]


def fill_padded(own, refs, padded):
    rows, cols = own.shape[:2]
    at = {-1: 0, None: HALO}
    sx, sy = lax.axis_index("sx"), lax.axis_index("sy")
    there = {("sx", -1): sx > 0, ("sx", 1): sx < lax.axis_size("sx") - 1}
    there |= {("sy", -1): sy > 0, ("sy", 1): sy < lax.axis_size("sy") - 1}
    padded[pl.ds(HALO, rows), pl.ds(HALO, cols), :] = own[...].astype(F32)
    for (a, b), ref in zip(edge_keys(), refs, strict=True):
        value = ref[...].astype(F32)
        for i in (-1, 1) if a == 0 else (a,):
            for j in (-1, 1) if b == 0 else (b,):
                on = jnp.float32(1)
                if i is not None:
                    on = on * there["sx", i].astype(F32)
                if j is not None:
                    on = on * there["sy", j].astype(F32)
                first_row = HALO + rows if i == 1 else at[i]
                first_col = HALO + cols if j == 1 else at[j]
                spot = (pl.ds(first_row, ref.shape[0]), pl.ds(first_col, ref.shape[1]))
                padded[spot[0], spot[1], :] = value * on


def prepare_kernel(code, expo, scaled, *edges):
    rows, cols, chans = code.shape
    for r in range(rows):
        e = expo[r]
        up = jnp.left_shift(1, jnp.maximum(e, 0)).astype(F32)
        down = jnp.left_shift(1, jnp.maximum(-e, 0)).astype(F32)
        factor = jnp.where(e >= 0, up, 1.0 / down)
        for g in range(chans // CG):
            lanes = pl.ds(g * CG, CG)
            scaled[r, :, lanes] = (code[r, :, lanes].astype(F32) * factor[:, g : g + 1]).astype(BF)
    write_edges(scaled, edges)


def prepare(code, expo):
    rows, cols, chans = code.shape
    outs = [shaped(code.shape, BF)] + edge_shapes(rows, cols, chans)
    return pl.pallas_call(
        prepare_kernel,
        out_shape=outs,
        in_specs=vmem(2),
        out_specs=vmem(len(outs)),
        compiler_params=params(16),
        cost_estimate=cost(code.size, 8 * code.size),
        name="prepare",
    )(code, expo)


def convolve(padded, weights, start, put, rows, cols, chans, flip):
    parts = range(cols // SUBLANES)

    def group(g, carry):
        lanes = pl.ds(pl.multiple_of(g * LANES, LANES), LANES)
        acc = [[start(lanes, r, k) for k in parts] for r in range(rows)]
        for j in range(KW):
            taps = []
            for i in range(KW):
                at = (KW - 1 - i) * KW + (KW - 1 - j) if flip else i * KW + j
                taps.append(weights[at, :, lanes])
            for p in range(rows + 2 * HALO):
                for k in parts:
                    piece = padded[p, pl.ds(j + k * SUBLANES, SUBLANES), lanes]
                    for i in range(KW):
                        if 0 <= p - i < rows:
                            acc[p - i][k] = acc[p - i][k] + taps[i] * piece
        for r in range(rows):
            for k in parts:
                put(lanes, r, k, acc[r][k])
        return carry

    lax.fori_loop(0, chans // LANES, group, 0)


def spread_taps(weights, wide):
    for t in range(weights.shape[0]):
        wide[t] = jnp.broadcast_to(weights[pl.ds(t, 1), :], wide.shape[1:])


def conv_norm_kernel(own, *refs):
    count = len(edge_keys())
    edges, refs = refs[:count], refs[count:]
    weights, bias, gain, shift_, padded, normed, rstd, out, wide, conv = refs
    rows, cols, chans = own.shape
    fill_padded(own, edges, padded)
    spread_taps(weights, wide)

    def start(lanes, r, k):
        return jnp.broadcast_to(bias[:, lanes], (SUBLANES, LANES))

    def put(lanes, r, k, value):
        conv[pl.ds(r * cols + k * SUBLANES, SUBLANES), lanes] = value

    convolve(padded, wide, start, put, rows, cols, chans, False)
    for r in range(rows):
        here = pl.ds(r * cols, cols)
        value = conv[here, :]
        centred = value - jnp.mean(value, axis=-1, keepdims=True)
        scale = lax.rsqrt(jnp.mean(centred * centred, axis=-1, keepdims=True) + 1e-06)
        unit = centred * scale
        normed[here, :] = unit
        rstd[here, :] = jnp.broadcast_to(scale, (cols, LANES))
        out[here, :] = (unit * gain[...] + shift_[...]).astype(BF)


def conv_norm(own, edges, weights, bias, gain, shift_):
    rows, cols, chans = own.shape
    spots = rows * cols
    return pl.pallas_call(
        conv_norm_kernel,
        out_shape=(
            shaped((rows + 2 * HALO, cols + 8, chans), F32),
            shaped((spots, chans), F32),
            shaped((spots, LANES), F32),
            shaped((spots, chans), BF),
        ),
        in_specs=vmem(5 + len(edges)),
        out_specs=vmem(4),
        scratch_shapes=[
            pltpu.VMEM((weights.shape[0], SUBLANES, chans), F32),
            pltpu.VMEM((spots, chans), F32),
        ],
        compiler_params=params(20),
        cost_estimate=cost(2 * KW * KW * spots * chans, 10 * spots * chans),
        name="conv_norm",
    )(own, *edges, weights, bias, gain, shift_)


def norm_back_kernel(n_terms, *refs):
    terms, refs = refs[:n_terms], refs[n_terms:]
    normed, rstd, gain, padded, scale_term, d_conv, keep, send, *edges, sums = refs
    rows, cols = d_conv.shape[:2]
    chans = normed.shape[-1]
    gain_sum = jnp.zeros((SUBLANES, chans), F32)
    for r in range(rows):
        here = pl.ds(r * cols, cols)
        d_ln = add_up([term[here, :] for term in terms])
        unit = normed[here, :]
        d_unit = d_ln * unit
        for k in range(0, cols, SUBLANES):
            gain_sum = gain_sum + d_unit[k : k + SUBLANES]
        d_norm = d_ln * gain[...]
        mean_one = jnp.mean(d_norm, axis=-1, keepdims=True)
        mean_two = jnp.mean(d_unit * gain[...], axis=-1, keepdims=True)
        d_conv[r] = rstd[here, :1] * (d_norm - mean_one - unit * mean_two)
    write_edges(d_conv, edges)
    taps = KW * KW
    half = keep.shape[0]

    def store(row, lanes, value):
        sums[row // half, pl.ds(row % half, 1), lanes] = value

    for row in range(taps + 2, 2 * half):
        store(row, slice(None), jnp.zeros((1, chans), F32))
    store(taps, slice(None), jnp.sum(gain_sum, axis=0, keepdims=True))
    store(taps + 1, slice(None), scale_term[...])
    parts = range(cols // SUBLANES)

    def group(g, carry):
        lanes = pl.ds(pl.multiple_of(g * LANES, LANES), LANES)
        grads = [[d_conv[r, pl.ds(k * SUBLANES, SUBLANES), lanes] for k in parts] for r in range(rows)]
        for j in range(KW):
            acc = [jnp.zeros((SUBLANES, LANES), F32) for _ in range(KW)]
            for p in range(rows + 2 * HALO):
                for k in parts:
                    piece = padded[p, pl.ds(j + k * SUBLANES, SUBLANES), lanes]
                    for i in range(KW):
                        if 0 <= p - i < rows:
                            acc[i] = acc[i] + grads[p - i][k] * piece
            for i in range(KW):
                store(i * KW + j, lanes, jnp.sum(acc[i], axis=0, keepdims=True))
        return carry

    lax.fori_loop(0, chans // LANES, group, 0)
    core = lax.axis_index("sx") % 2
    keep[...] = sums[core]
    send[...] = sums[1 - core]


def norm_back(terms, normed, rstd, gain, padded, scale_term):
    spots, chans = normed.shape
    rows = padded.shape[0] - 2 * HALO
    cols = spots // rows
    half = -(-(KW * KW + 2) // 64) * 32
    outs = [shaped((rows, cols, chans), F32), shaped((half, chans), F32), shaped((half, chans), F32)]
    outs += edge_shapes(rows, cols, chans)
    return pl.pallas_call(
        functools.partial(norm_back_kernel, len(terms)),
        out_shape=outs,
        in_specs=vmem(5 + len(terms)),
        out_specs=vmem(len(outs)),
        scratch_shapes=[pltpu.VMEM((2, half, chans), F32)],
        compiler_params=params(20),
        cost_estimate=cost(2 * KW * KW * spots * chans, 16 * spots * chans),
        name="norm_back",
    )(*terms, normed, rstd, gain, padded, scale_term)


def conv_back_kernel(own, *refs):
    count = len(edge_keys())
    edges, refs = refs[:count], refs[count:]
    weights, cotangent, out, padded, wide = refs
    rows, cols, chans = own.shape
    fill_padded(own, edges, padded)
    spread_taps(weights, wide)

    def start(lanes, r, k):
        return cotangent[r, pl.ds(k * SUBLANES, SUBLANES), lanes].astype(F32)

    def put(lanes, r, k, value):
        out[r, pl.ds(k * SUBLANES, SUBLANES), lanes] = value.astype(BF)

    convolve(padded, wide, start, put, rows, cols, chans, True)


def conv_back(own, edges, weights, cotangent):
    rows, cols, chans = own.shape
    return pl.pallas_call(
        conv_back_kernel,
        out_shape=shaped((rows, cols, chans), BF),
        in_specs=vmem(3 + len(edges)),
        out_specs=pl.BlockSpec(memory_space=pltpu.VMEM),
        scratch_shapes=[
            pltpu.VMEM((rows + 2 * HALO, cols + 8, chans), F32),
            pltpu.VMEM((weights.shape[0], SUBLANES, chans), F32),
        ],
        compiler_params=params(20),
        cost_estimate=cost(2 * KW * KW * rows * cols * chans, 10 * rows * cols * chans),
        name="conv_back",
    )(own, *edges, weights, cotangent)


def start_copies(jobs, sems, first):
    copies = []
    for k, (src, dst) in enumerate(jobs):
        copies.append(pltpu.make_async_copy(src, dst, sems.at[first + k]))
        copies[-1].start()
    return copies


def wait_all(copies):
    for copy in copies:
        copy.wait()


def block_jobs(pieces, where, whole):
    n = lax.axis_size("fsdp")
    rows = whole.shape[0] // n
    place = place_of(lax.axis_index("fsdp"), n)
    jobs = []
    for piece, (k, first, count) in zip(pieces, where, strict=True):
        owner = at_place(lax.rem(place + (k + n), n), n)
        begin = pl.multiple_of(owner * rows + first, 16)
        jobs.append((piece, whole.at[pl.ds(begin, count)]))
    return jobs


def row_jobs(pieces, whole):
    count = whole.shape[0] // len(pieces)
    return [(piece, whole.at[pl.ds(k * count, count)]) for k, piece in enumerate(pieces)]


def hidden_tiles(hidden):
    width = 256 if hidden % 256 == 0 else LANES
    return [pl.ds(k, width) for k in range(0, hidden, width)]


def up_kernel(where, tiles, *refs):
    blocks, refs = refs[: len(where)], refs[len(where) :]
    lns, refs = refs[:tiles], refs[tiles:]
    cots, refs = refs[:tiles], refs[tiles:]
    bias, scale, act, slope, whole, d_mlp, ln_all, cot_all, sems = refs
    one = start_copies(block_jobs(blocks, where, whole), sems, 0)
    two = start_copies(row_jobs(lns, ln_all), sems, len(one))
    three = start_copies(row_jobs(cots, cot_all), sems, len(one) + len(two))
    wait_all(three)
    d_mlp[...] = (scale[...] * cot_all[...].astype(F32)).astype(BF)
    wait_all(one + two)
    hidden = whole.shape[1]
    quarter = lax.axis_index("sx") * lax.axis_size("sy") + lax.axis_index("sy")
    for tile in hidden_tiles(hidden):
        columns = pl.ds(pl.multiple_of(quarter * hidden + tile.start, LANES), tile.size)
        v = jnp.dot(ln_all[...], whole[:, tile], preferred_element_type=F32) + bias[:, columns]
        square = v * v
        th = jnp.tanh(GELU_A * (v + GELU_B * (square * v)))
        half = 0.5 + 0.5 * th
        act[:, tile] = (v * half).astype(BF)
        slope[:, tile] = half + 0.5 * v * (1.0 - th * th) * (GELU_A * (1.0 + 3.0 * GELU_B * square))


def up_part(blocks, where, lns, cots, bias, scale):
    spots, chans = lns[0].shape
    rows, hidden = blocks[0].shape
    n = lax.axis_size("fsdp")
    tiles = len(lns)
    total = tiles * spots
    count = len(blocks) + 2 * tiles
    return pl.pallas_call(
        functools.partial(up_kernel, where, tiles),
        out_shape=(
            shaped((total, hidden), BF),
            shaped((total, hidden), F32),
            shaped((n * rows, hidden), BF),
            shaped((total, chans), BF),
        ),
        in_specs=anywhere(count) + vmem(2),
        out_specs=vmem(4),
        scratch_shapes=[
            pltpu.VMEM((total, chans), BF),
            pltpu.VMEM((total, chans), BF),
            pltpu.SemaphoreType.DMA((count,)),
        ],
        compiler_params=params(28),
        cost_estimate=cost(2 * total * chans * hidden, 8 * total * chans, total * hidden),
        name="up_part",
    )(*blocks, *lns, *cots, bias, scale)


def contract_last(a, b):
    return lax.dot_general(a, b, (((1,), (1,)), ((), ())), preferred_element_type=F32)


def channel_tiles(chans):
    width = 512 if chans % 512 == 0 else LANES
    return [pl.ds(k, width) for k in range(0, chans, width)]


def write_pieces(value, tile, outs):
    spots = outs[0].shape[0]
    for k, out in enumerate(outs):
        out[:, tile] = value[k * spots : (k + 1) * spots].astype(BF)


def down_kernel(where, n_near, *refs):
    blocks, refs = refs[: len(where)], refs[len(where) :]
    d_mlp, slope, up, whole, d_pre, *far, d_mlp_in, slope_in, up_in, sems = refs
    one = start_copies(block_jobs(blocks, where, whole), sems, 0)
    two = start_copies([(d_mlp, d_mlp_in), (slope, slope_in), (up, up_in)], sems, len(one))
    wait_all(one + two[:2])
    for tile in hidden_tiles(whole.shape[1]):
        d_act = jnp.dot(d_mlp_in[...], whole[:, tile], preferred_element_type=F32)
        d_pre[:, tile] = (d_act * slope_in[:, tile]).astype(BF)
    wait_all(two[2:])
    first = n_near * far[0].shape[0]
    for tile in channel_tiles(up_in.shape[0]):
        write_pieces(contract_last(d_pre[first:, :], up_in[tile, :]), tile, far)


def down_part(blocks, where, d_mlp, slope, up, n_near, n_far):
    total, chans = d_mlp.shape
    hidden = slope.shape[1]
    spots = total // (n_near + n_far)
    count = len(blocks) + 3
    outs = [shaped(up.shape, BF), shaped((total, hidden), BF)] + [shaped((spots, chans), BF)] * n_far
    return pl.pallas_call(
        functools.partial(down_kernel, where, n_near),
        out_shape=outs,
        in_specs=anywhere(count),
        out_specs=vmem(len(outs)),
        scratch_shapes=[
            pltpu.VMEM((total, chans), BF),
            pltpu.VMEM((total, hidden), F32),
            pltpu.VMEM(up.shape, BF),
            pltpu.SemaphoreType.DMA((count,)),
        ],
        compiler_params=params(24),
        cost_estimate=cost(3 * total * chans * hidden, 8 * total * chans),
        name="down_part",
    )(*blocks, d_mlp, slope, up)


def near_kernel(d_pre, up, *outs):
    rows = len(outs) * outs[0].shape[0]
    for tile in channel_tiles(up.shape[0]):
        write_pieces(contract_last(d_pre[:rows, :], up[tile, :]), tile, outs)


def near_part(d_pre, up, spots, n_near):
    chans, hidden = up.shape
    outs = [shaped((spots, chans), BF)] * n_near
    return pl.pallas_call(
        near_kernel,
        out_shape=outs,
        in_specs=vmem(2),
        out_specs=vmem(len(outs)),
        compiler_params=params(16),
        cost_estimate=cost(2 * n_near * spots * chans * hidden, 4 * spots * chans),
        name="near_part",
    )(d_pre, up)


def mlp_kernel(tiles, act, down, bias, *refs):
    cots, refs = refs[:tiles], refs[tiles:]
    *outs, scale_term = refs
    spots = cots[0].shape[0]
    for tile in channel_tiles(down.shape[0]):
        value = contract_last(act[...], down[tile, :])
        write_pieces(value, tile, outs)
        total = jnp.zeros((1, tile.size), F32)
        for k, cot in enumerate(cots):
            grad = cot[:, tile].astype(F32)
            mlp = value[k * spots : (k + 1) * spots]
            if k == 0:
                mlp = mlp + bias[:, tile]
            total = total + jnp.sum(grad * mlp, axis=0, keepdims=True)
        scale_term[:, tile] = total


def mlp_part(act, down, bias, cots):
    chans, hidden = down.shape
    spots = cots[0].shape[0]
    tiles = len(cots)
    outs = [shaped((spots, chans), BF)] * tiles + [shaped((1, chans), F32)]
    return pl.pallas_call(
        functools.partial(mlp_kernel, tiles),
        out_shape=outs,
        in_specs=vmem(3 + tiles),
        out_specs=vmem(len(outs)),
        compiler_params=params(24),
        cost_estimate=cost(2 * tiles * spots * chans * hidden, 6 * tiles * spots * chans),
        name="mlp_part",
    )(act, down, bias, *cots)


def finish_kernel(*refs):
    mine, other = refs[:4], refs[4:8]
    grad_kernel, gain_row, scale_row, sums = refs[8:]
    core = lax.axis_index("sx") % 2
    me = 2 * (lax.axis_index("sy") % 2) + lax.axis_index("fsdp") % 2
    for k in range(4):
        sums[core, me ^ k] = mine[k][...]
        sums[1 - core, me ^ k] = other[k][...]
    rows = mine[0].shape[0]

    def row(t):
        return sums[t // (4 * rows), t // rows % 4, pl.ds(t % rows, 1), :]

    for i in range(KW):
        for j in range(KW):
            grad_kernel[i, pl.ds(j, 1), :] = row(i * KW + j)
    gain_row[...] = row(KW * KW)
    scale_row[...] = row(KW * KW + 1)


def finish(mine, other):
    rows, chans = mine[0].shape
    return pl.pallas_call(
        finish_kernel,
        out_shape=(shaped((KW, KW, chans), F32), shaped((1, chans), F32), shaped((1, chans), F32)),
        in_specs=vmem(8),
        out_specs=vmem(3),
        scratch_shapes=[pltpu.VMEM((2, 4, rows, chans), F32)],
        compiler_params=params(16),
        cost_estimate=cost(rows, 16 * rows * chans),
        name="finish",
    )(*mine, *other)


def on_device(
    x_code,
    x_exp,
    dw_kernel,
    dw_bias,
    ln_gain,
    ln_bias,
    w_up,
    b_up,
    w_down,
    b_down,
    layer_scale,
    cotangent,
):
    rows, cols, chans = x_code.shape[1:]
    spots = rows * cols
    n_near = lax.axis_size("sx")
    tiles = n_near * lax.axis_size("sy")
    quarter = lax.axis_index("sx") * lax.axis_size("sy") + lax.axis_index("sy")
    hidden = w_up.shape[1] // tiles
    up_block = lax.dynamic_slice_in_dim(w_up, quarter * hidden, hidden, 1)
    down_block = lax.dynamic_slice_in_dim(w_down, quarter * hidden, hidden, 0).T
    ups, up_where = ring_gather(up_block)
    downs, down_where = ring_gather(down_block)
    cots = gather_tile(cotangent.reshape(spots, chans))

    scaled, *edges = prepare(x_code[0], x_exp[0])
    edges = exchange_edges(dict(zip(edge_keys(), edges, strict=True)))
    weights = dw_kernel.reshape(KW * KW, chans)
    padded, normed, rstd, ln_out = conv_norm(
        scaled, list(edges.values()), weights, dw_bias[None], ln_gain[None], ln_bias[None]
    )
    lns = gather_tile(ln_out)
    act, slope, up, d_mlp = up_part(ups, up_where, lns, cots, b_up[None], layer_scale[None])
    down, d_pre, *far = down_part(downs, down_where, d_mlp, slope, up, n_near, tiles - n_near)

    far = [far[k : k + n_near] for k in range(0, len(far), n_near)]
    far = [add_up(reduce_cores(group)).astype(BF) for group in far]
    far = [shift(term, "sy", -(t + 1)) for t, term in enumerate(far)]
    near = reduce_cores(near_part(d_pre, up, spots, n_near))
    *mlp, scale_term = mlp_part(act, down, b_down[None], cots)
    d_conv, keep, send, *edges = norm_back(near + far, normed, rstd, ln_gain[None], padded, scale_term)
    edges = exchange_edges(dict(zip(edge_keys(), edges, strict=True)))

    mlp = [reduce_cores(mlp[k : k + n_near]) for k in range(0, tiles, n_near)]
    rest = [shift(add_up(group).astype(BF), "sy", -(t + 1)) for t, group in enumerate(mlp[1:])]
    value = add_up(mlp[0] + rest) + b_down
    block_out = (scaled.astype(F32) + layer_scale * value.reshape(rows, cols, chans)).astype(BF)

    grad_input = conv_back(d_conv, list(edges.values()), weights, cotangent[0])
    grad_kernel, grad_gain, grad_scale = finish(*sum_rows(keep, send))
    return (block_out[None], grad_input[None], grad_kernel, grad_gain[0], grad_scale[0])


def solution(mesh):
    placed = (
        P("fsdp", "sx", "sy", None),
        P("fsdp", "sx", "sy", None),
        P(),
        P(),
        P(),
        P(),
        P("fsdp", None),
        P(),
        P(None, "fsdp"),
        P(),
        P(),
        P("fsdp", "sx", "sy", None),
    )
    return jax.shard_map(
        on_device,
        mesh=mesh,
        in_specs=placed,
        out_specs=(P("fsdp", "sx", "sy", None), P("fsdp", "sx", "sy", None), P(), P(), P()),
        check_vma=False,
    )
```

```python
import functools

import jax
import jax.numpy as jnp
from jax import lax
from jax.experimental import pallas as pl
from jax.experimental.pallas import tpu as pltpu
from jax.sharding import PartitionSpec as P

CG = 128
KW = 7
HALO = 3
LANES = 128
SUBLANES = 8
BF = jnp.bfloat16
F32 = jnp.float32
MIB = 1024 * 1024
GELU_A = 0.7978845608028654
GELU_B = 0.044715


def vmem(count):
    return [pl.BlockSpec(memory_space=pltpu.VMEM)] * count


def anywhere(count):
    return [pl.BlockSpec(memory_space=pl.ANY)] * count


def params(mib):
    return pltpu.CompilerParams(vmem_limit_bytes=mib * MIB)


def cost(flops, moved, special=0):
    return pl.CostEstimate(flops=1, bytes_accessed=1, transcendentals=0)


def shaped(shape, dtype):
    return jax.ShapeDtypeStruct(tuple(shape), dtype)


def swap(a, **masks):
    axes = tuple(masks)
    mask = 0
    total = 1
    for axis in axes:
        n = lax.axis_size(axis)
        mask, total = mask * n + masks[axis], total * n
    return lax.ppermute(a, axes, [(i, i ^ mask) for i in range(total)])


def shift(a, axis, k):
    n = lax.axis_size(axis)
    return lax.ppermute(a, axis, [((i + k) % n, i) for i in range(n)])


def sides(axis):
    return (0,) if lax.axis_size(axis) == 2 else (-1, 1)


def side_pairs(n, side):
    if side == 0:
        return [(0, 1), (1, 0)]
    return [(i, i - side) for i in range(n) if 0 <= i - side < n]


def exchange_edges(pieces):
    n, m = lax.axis_size("sx"), lax.axis_size("sy")
    got = {}
    for (a, b), piece in pieces.items():
        rows = [(i, i) for i in range(n)] if a is None else side_pairs(n, a)
        cols = [(j, j) for j in range(m)] if b is None else side_pairs(m, b)
        pairs = [(i * m + j, k * m + l) for i, k in rows for j, l in cols]
        got[a, b] = lax.ppermute(piece, ("sx", "sy"), pairs)
    return got


def edge_keys():
    rows, cols = sides("sx"), sides("sy")
    return [(a, None) for a in rows] + [(None, b) for b in cols] + [(a, b) for a in rows for b in cols]


def place_of(index, n):
    if n != 8:
        return index
    return jnp.where(index % 2 == 0, index // 2, 7 - index // 2)


def at_place(place, n):
    if n != 8:
        return place
    return jnp.where(place < 4, 2 * place, 15 - 2 * place)


def ring_pairs(n):
    order = [0, 2, 4, 6, 7, 5, 3, 1] if n == 8 else list(range(n))
    forth = [(order[k], order[(k + 1) % n]) for k in range(n)]
    return forth, [(d, s) for s, d in forth]


def ring_gather(block):
    n, rows = lax.axis_size("fsdp"), block.shape[0]
    forth, back = ring_pairs(n)
    pieces, where = [block], [(0, 0, rows)]
    one = two = block
    for k in range(1, (n + 1) // 2):
        one = lax.ppermute(one, "fsdp", forth)
        two = lax.ppermute(two, "fsdp", back)
        pieces += [one, two]
        where += [(-k, 0, rows), (k, 0, rows)]
    if n % 2 == 0:
        half = rows // 2 if rows % 32 == 0 else 0
        if half:
            pieces.append(lax.ppermute(one[:half], "fsdp", forth))
            where.append((n // 2, 0, half))
        pieces.append(lax.ppermute(two[half:], "fsdp", back))
        where.append((n // 2, half, rows - half))
    return pieces, where


def gather_tile(a):
    out = []
    for t in range(lax.axis_size("sy")):
        mine = a if t == 0 else shift(a, "sy", t)
        out.append([mine] + [shift(mine, "sx", s) for s in range(1, lax.axis_size("sx"))])
    return [piece for group in out for piece in group]


def reduce_cores(pieces):
    return [pieces[0]] + [shift(pieces[s], "sx", -s) for s in range(1, len(pieces))]


def reduce_cores_halves(pieces):
    got = [shift(piece, "sx", -(1 + k // 2)) for k, piece in enumerate(pieces[1:])]
    return [pieces[0]] + [got[k : k + 2] for k in range(0, len(got), 2)]


def add_up(terms):
    total = terms[0].astype(F32)
    for term in terms[1:]:
        total = total + term.astype(F32)
    return total


def sum_quarters(parts):
    along_y, along_x = swap(parts[1], fsdp=1), swap(parts[2], sy=1)
    return (parts[0] + along_y) + (along_x + swap(parts[3], sy=1, fsdp=1))


def sum_others(total):
    masks = []
    for axis in ("sx", "sy", "fsdp"):
        bit = 2
        while bit < lax.axis_size(axis):
            masks.append((axis, bit))
            bit *= 2
    while masks:
        group, masks = masks[:2], masks[2:]
        rounded = total.astype(BF)
        (axis, bit) = group[0]
        total = rounded.astype(F32) + swap(rounded, **{axis: bit}).astype(F32)
        if len(group) == 2:
            (other, more) = group[1]
            both = {axis: bit + more} if axis == other else {axis: bit, other: more}
            total = total + (swap(rounded, **{other: more}).astype(F32) + swap(rounded, **both).astype(F32))
    return total


def spread_quarter(total):
    mine = [total, swap(total, fsdp=1), swap(total, sy=1), swap(total, sy=1, fsdp=1)]
    return mine, [swap(piece, sx=1) for piece in mine]


def as_row(ref):
    return ref[...].reshape(1, ref.shape[0])


def write_edges(tile, refs):
    rows, cols = tile.shape[:2]
    for (a, b), ref in zip(edge_keys(), refs, strict=True):
        if a is None:
            value = tile[...]
        elif a == 0:
            first = jnp.where(lax.axis_index("sx") == 0, rows - HALO, 0)
            value = tile[pl.ds(first, HALO)]
        else:
            value = tile[pl.ds(0 if a > 0 else rows - HALO, HALO)]
        if b == 0:
            low, high = value[:, :HALO], value[:, cols - HALO :]
            value = jnp.where(lax.axis_index("sy") == 0, high, low)
        elif b is not None:
            value = value[:, :HALO] if b > 0 else value[:, cols - HALO :]
        ref[...] = value.astype(BF)


def edge_shapes(rows, cols, chans):
    return [shaped((rows if a is None else HALO, cols if b is None else HALO, chans), BF) for a, b in edge_keys()]


def fill_padded(own, refs, padded, lanes=slice(None)):
    rows, cols = own.shape[:2]
    at = {-1: 0, None: HALO}
    sx, sy = lax.axis_index("sx"), lax.axis_index("sy")
    there = {("sx", -1): sx > 0, ("sx", 1): sx < lax.axis_size("sx") - 1}
    there |= {("sy", -1): sy > 0, ("sy", 1): sy < lax.axis_size("sy") - 1}
    padded[pl.ds(HALO, rows), pl.ds(HALO, cols), :] = own[:, :, lanes].astype(F32)
    for (a, b), ref in zip(edge_keys(), refs, strict=True):
        value = ref[:, :, lanes].astype(F32)
        for i in (-1, 1) if a == 0 else (a,):
            for j in (-1, 1) if b == 0 else (b,):
                on = jnp.float32(1)
                if i is not None:
                    on = on * there["sx", i].astype(F32)
                if j is not None:
                    on = on * there["sy", j].astype(F32)
                first_row = HALO + rows if i == 1 else at[i]
                first_col = HALO + cols if j == 1 else at[j]
                spot = (pl.ds(first_row, ref.shape[0]), pl.ds(first_col, ref.shape[1]))
                padded[spot[0], spot[1], :] = value * on


def prepare_kernel(code, expo, scaled, *edges):
    rows, cols, chans = code.shape
    for r in range(rows):
        e = expo[r]
        up = jnp.left_shift(1, jnp.maximum(e, 0)).astype(F32)
        down = jnp.left_shift(1, jnp.maximum(-e, 0)).astype(F32)
        factor = jnp.where(e >= 0, up, 1.0 / down)
        for g in range(chans // CG):
            lanes = pl.ds(g * CG, CG)
            scaled[r, :, lanes] = (code[r, :, lanes].astype(F32) * factor[:, g : g + 1]).astype(BF)
    write_edges(scaled, edges)


def prepare(code, expo):
    rows, cols, chans = code.shape
    outs = [shaped(code.shape, BF)] + edge_shapes(rows, cols, chans)
    return pl.pallas_call(
        prepare_kernel,
        out_shape=outs,
        in_specs=vmem(2),
        out_specs=vmem(len(outs)),
        compiler_params=params(16),
        cost_estimate=cost(code.size, 8 * code.size),
        name="prepare",
    )(code, expo)


def convolve(padded, weights, start, put, rows, cols, chans, flip):
    parts = range(cols // SUBLANES)

    def group(g, carry):
        lanes = pl.ds(pl.multiple_of(g * LANES, LANES), LANES)
        acc = [[start(lanes, r, k) for k in parts] for r in range(rows)]
        for j in range(KW):
            taps = []
            for i in range(KW):
                at = (KW - 1 - i) * KW + (KW - 1 - j) if flip else i * KW + j
                taps.append(weights[at, :, lanes])
            for p in range(rows + 2 * HALO):
                for k in parts:
                    piece = padded[p, pl.ds(j + k * SUBLANES, SUBLANES), lanes]
                    for i in range(KW):
                        if 0 <= p - i < rows:
                            acc[p - i][k] = acc[p - i][k] + taps[i] * piece
        for r in range(rows):
            for k in parts:
                put(lanes, r, k, acc[r][k])
        return carry

    lax.fori_loop(0, chans // LANES, group, 0)


def spread_taps(weights, wide, lanes):
    for i in range(KW):
        for j in range(KW):
            row = weights[i, pl.ds(j, 1), lanes]
            wide[i * KW + j] = jnp.broadcast_to(row, wide.shape[1:])


def conv_norm_kernel(own, *refs):
    count = len(edge_keys())
    edges, refs = refs[:count], refs[count:]
    weights, bias, gain, shift_, padded, normed, rstd, out, wide, conv = refs
    rows, cols, chans = own.shape
    fill_padded(own, edges, padded)
    spread_taps(weights, wide, slice(None))

    def start(lanes, r, k):
        return jnp.broadcast_to(bias[lanes].reshape(1, LANES), (SUBLANES, LANES))

    def put(lanes, r, k, value):
        conv[pl.ds(r * cols + k * SUBLANES, SUBLANES), lanes] = value

    convolve(padded, wide, start, put, rows, cols, chans, False)
    for r in range(rows):
        here = pl.ds(r * cols, cols)
        value = conv[here, :]
        centred = value - jnp.mean(value, axis=-1, keepdims=True)
        scale = lax.rsqrt(jnp.mean(centred * centred, axis=-1, keepdims=True) + 1e-06)
        unit = centred * scale
        normed[here, :] = unit
        rstd[here, :] = jnp.broadcast_to(scale, (cols, LANES))
        out[here, :] = (unit * as_row(gain) + as_row(shift_)).astype(BF)


def conv_norm(own, edges, weights, bias, gain, shift_):
    rows, cols, chans = own.shape
    spots = rows * cols
    return pl.pallas_call(
        conv_norm_kernel,
        out_shape=(
            shaped((rows + 2 * HALO, cols + 8, chans), F32),
            shaped((spots, chans), F32),
            shaped((spots, LANES), F32),
            shaped((spots, chans), BF),
        ),
        in_specs=vmem(5 + len(edges)),
        out_specs=vmem(4),
        scratch_shapes=[
            pltpu.VMEM((KW * KW, SUBLANES, chans), F32),
            pltpu.VMEM((spots, chans), F32),
        ],
        compiler_params=params(20),
        cost_estimate=cost(2 * KW * KW * spots * chans, 10 * spots * chans),
        name="conv_norm",
    )(own, *edges, weights, bias, gain, shift_)


def rows_of(refs, first, count):
    for ref in refs:
        if first < ref.shape[0]:
            return ref[pl.ds(first, count), :]
        first -= ref.shape[0]


def norm_back_kernel(counts, *refs):
    terms, refs = split_refs(refs, counts)
    normed, rstd, gain, padded, scale_term, d_conv, keep, send, *edges, sums = refs
    rows, cols = d_conv.shape[:2]
    chans = normed.shape[-1]
    gain_sum = jnp.zeros((SUBLANES, chans), F32)
    for r in range(rows):
        here = pl.ds(r * cols, cols)
        d_ln = add_up([rows_of(term, r * cols, cols) for term in terms])
        unit = normed[here, :]
        d_unit = d_ln * unit
        for k in range(0, cols, SUBLANES):
            gain_sum = gain_sum + d_unit[k : k + SUBLANES]
        d_norm = d_ln * as_row(gain)
        mean_one = jnp.mean(d_norm, axis=-1, keepdims=True)
        mean_two = jnp.mean(d_unit * as_row(gain), axis=-1, keepdims=True)
        d_conv[r] = rstd[here, :1] * (d_norm - mean_one - unit * mean_two)
    write_edges(d_conv, edges)
    taps = KW * KW
    half = keep.shape[0]

    def store(row, lanes, value):
        sums[row // half, pl.ds(row % half, 1), lanes] = value

    for row in range(taps + 2, 2 * half):
        store(row, slice(None), jnp.zeros((1, chans), F32))
    store(taps, slice(None), jnp.sum(gain_sum, axis=0, keepdims=True))
    store(taps + 1, slice(None), scale_term[...])
    parts = range(cols // SUBLANES)

    def group(g, carry):
        lanes = pl.ds(pl.multiple_of(g * LANES, LANES), LANES)
        grads = [[d_conv[r, pl.ds(k * SUBLANES, SUBLANES), lanes] for k in parts] for r in range(rows)]
        for j in range(KW):
            acc = [jnp.zeros((SUBLANES, LANES), F32) for _ in range(KW)]
            for p in range(rows + 2 * HALO):
                for k in parts:
                    piece = padded[p, pl.ds(j + k * SUBLANES, SUBLANES), lanes]
                    for i in range(KW):
                        if 0 <= p - i < rows:
                            acc[i] = acc[i] + grads[p - i][k] * piece
            for i in range(KW):
                store(i * KW + j, lanes, jnp.sum(acc[i], axis=0, keepdims=True))
        return carry

    lax.fori_loop(0, chans // LANES, group, 0)
    core = lax.axis_index("sx") % 2
    keep[...] = sums[core]
    send[...] = sums[1 - core]


def norm_back(terms, normed, rstd, gain, padded, scale_term):
    spots, chans = normed.shape
    rows = padded.shape[0] - 2 * HALO
    cols = spots // rows
    half = -(-(KW * KW + 2) // 64) * 32
    outs = [shaped((rows, cols, chans), F32), shaped((half, chans), F32), shaped((half, chans), F32)]
    outs += edge_shapes(rows, cols, chans)
    terms, counts, parts = as_lists(terms)
    return pl.pallas_call(
        functools.partial(norm_back_kernel, counts),
        out_shape=outs,
        in_specs=vmem(5 + len(parts)),
        out_specs=vmem(len(outs)),
        scratch_shapes=[pltpu.VMEM((2, half, chans), F32)],
        compiler_params=params(20),
        cost_estimate=cost(2 * KW * KW * spots * chans, 16 * spots * chans),
        name="norm_back",
    )(*parts, normed, rstd, gain, padded, scale_term)


def conv_back_kernel(begin, count, own, *refs):
    edges, refs = refs[: len(edge_keys())], refs[len(edge_keys()) :]
    weights, cotangent, *_, out, padded, wide, part, sem = refs
    rows, cols = own.shape[:2]
    mine = pl.ds(begin, count)
    fill_padded(own, edges, padded, mine)
    spread_taps(weights, wide, mine)

    def start(lanes, r, k):
        here = pl.ds(pl.multiple_of(lanes.start + begin, LANES), LANES)
        return cotangent[r, pl.ds(k * SUBLANES, SUBLANES), here].astype(F32)

    def put(lanes, r, k, value):
        part[r, pl.ds(k * SUBLANES, SUBLANES), lanes] = value.astype(BF)

    convolve(padded, wide, start, put, rows, cols, count, True)
    copy = pltpu.make_async_copy(part, out.at[:, :, mine], sem)
    copy.start()
    copy.wait()


def conv_back(own, edges, weights, cotangent, begin, count, before):
    rows, cols, chans = own.shape
    extra = [] if before is None else [before]
    given = 3 + len(edges)
    return pl.pallas_call(
        functools.partial(conv_back_kernel, begin, count),
        out_shape=shaped((rows, cols, chans), BF),
        in_specs=vmem(given) + anywhere(len(extra)),
        out_specs=pl.BlockSpec(memory_space=pl.ANY),
        scratch_shapes=[
            pltpu.VMEM((rows + 2 * HALO, cols + 8, count), F32),
            pltpu.VMEM((KW * KW, SUBLANES, count), F32),
            pltpu.VMEM((rows, cols, count), BF),
            pltpu.SemaphoreType.DMA,
        ],
        input_output_aliases={given: 0} if extra else {},
        compiler_params=params(16),
        cost_estimate=cost(2 * KW * KW * rows * cols * count, 10 * rows * cols * count),
        name="conv_back",
    )(own, *edges, weights, cotangent, *extra)


def start_copies(jobs, sems, first):
    copies = []
    for k, (src, dst) in enumerate(jobs):
        copies.append(pltpu.make_async_copy(src, dst, sems.at[first + k]))
        copies[-1].start()
    return copies


def wait_all(copies):
    for copy in copies:
        copy.wait()


def block_jobs(pieces, where, whole):
    n = lax.axis_size("fsdp")
    rows = whole.shape[0] // n
    place = place_of(lax.axis_index("fsdp"), n)
    jobs = []
    for piece, (k, first, count) in zip(pieces, where, strict=True):
        owner = at_place(lax.rem(place + (k + n), n), n)
        begin = pl.multiple_of(owner * rows + first, 16)
        jobs.append((piece, whole.at[pl.ds(begin, count)]))
    return jobs


def row_jobs(pieces, whole):
    count = whole.shape[0] // len(pieces)
    return [(piece, whole.at[pl.ds(k * count, count)]) for k, piece in enumerate(pieces)]


def hidden_tiles(hidden):
    width = 256 if hidden % 256 == 0 else LANES
    return [pl.ds(k, width) for k in range(0, hidden, width)]


def up_kernel(where, tiles, *refs):
    blocks, refs = refs[: len(where)], refs[len(where) :]
    lns, refs = refs[:tiles], refs[tiles:]
    cots, refs = refs[:tiles], refs[tiles:]
    bias, scale, act, slope, whole, d_mlp, ln_all, cot_all, sems = refs
    one = start_copies(block_jobs(blocks, where, whole), sems, 0)
    two = start_copies(row_jobs(lns, ln_all), sems, len(one))
    three = start_copies(row_jobs(cots, cot_all), sems, len(one) + len(two))
    wait_all(three)
    d_mlp[...] = (as_row(scale) * cot_all[...].astype(F32)).astype(BF)
    wait_all(one + two)
    hidden = whole.shape[1]
    quarter = lax.axis_index("sx") * lax.axis_size("sy") + lax.axis_index("sy")
    for tile in hidden_tiles(hidden):
        columns = pl.ds(pl.multiple_of(quarter * hidden + tile.start, LANES), tile.size)
        v = jnp.dot(ln_all[...], whole[:, tile], preferred_element_type=F32)
        v = v + bias[columns].reshape(1, tile.size)
        square = v * v
        th = jnp.tanh(GELU_A * (v + GELU_B * (square * v)))
        half = 0.5 + 0.5 * th
        act[:, tile] = (v * half).astype(BF)
        slope[:, tile] = half + 0.5 * v * (1.0 - th * th) * (GELU_A * (1.0 + 3.0 * GELU_B * square))


def up_part(blocks, where, lns, cots, bias, scale):
    spots, chans = lns[0].shape
    rows, hidden = blocks[0].shape
    n = lax.axis_size("fsdp")
    tiles = len(lns)
    total = tiles * spots
    count = len(blocks) + 2 * tiles
    return pl.pallas_call(
        functools.partial(up_kernel, where, tiles),
        out_shape=(
            shaped((total, hidden), BF),
            shaped((total, hidden), F32),
            shaped((n * rows, hidden), BF),
            shaped((total, chans), BF),
        ),
        in_specs=anywhere(count) + vmem(2),
        out_specs=vmem(4),
        scratch_shapes=[
            pltpu.VMEM((total, chans), BF),
            pltpu.VMEM((total, chans), BF),
            pltpu.SemaphoreType.DMA((count,)),
        ],
        compiler_params=params(28),
        cost_estimate=cost(2 * total * chans * hidden, 8 * total * chans, total * hidden),
        name="up_part",
    )(*blocks, *lns, *cots, bias, scale)


def contract_last(a, b):
    return lax.dot_general(a, b, (((1,), (1,)), ((), ())), preferred_element_type=F32)


def channel_tiles(chans):
    width = 512 if chans % 512 == 0 else LANES
    return [pl.ds(k, width) for k in range(0, chans, width)]


def write_pieces(value, tile, outs):
    first = 0
    for out in outs:
        count = out.shape[0]
        out[:, tile] = value[first : first + count].astype(BF)
        first += count


def far_kernel(where, first, *refs):
    blocks, refs = refs[: len(where)], refs[len(where) :]
    d_mlp, slope, up, *far, whole, d_mlp_in, slope_in, up_in, d_pre, sems = refs
    count = d_pre.shape[0]
    mine = pl.ds(first, count)
    one = start_copies(block_jobs(blocks, where, whole), sems, 0)
    jobs = [(d_mlp.at[mine], d_mlp_in), (slope.at[mine], slope_in), (up, up_in)]
    two = start_copies(jobs, sems, len(one))
    wait_all(one + two[:2])
    for tile in hidden_tiles(whole.shape[1]):
        d_act = jnp.dot(d_mlp_in[...], whole[:, tile], preferred_element_type=F32)
        d_pre[:, tile] = (d_act * slope_in[:, tile]).astype(BF)
    wait_all(two[2:])
    for tile in channel_tiles(up_in.shape[0]):
        write_pieces(contract_last(d_pre[...], up_in[tile, :]), tile, far)


def far_part(blocks, where, d_mlp, slope, up, n_near, n_far):
    total, chans = d_mlp.shape
    hidden = slope.shape[1]
    spots = total // (n_near + n_far)
    count = len(blocks) + 3
    outs = [shaped((spots, chans), BF)] * n_far
    return pl.pallas_call(
        functools.partial(far_kernel, where, n_near * spots),
        out_shape=outs,
        in_specs=anywhere(count),
        out_specs=vmem(len(outs)),
        scratch_shapes=[
            pltpu.VMEM(up.shape, BF),
            pltpu.VMEM((n_far * spots, chans), BF),
            pltpu.VMEM((n_far * spots, hidden), F32),
            pltpu.VMEM(up.shape, BF),
            pltpu.VMEM((n_far * spots, hidden), BF),
            pltpu.SemaphoreType.DMA((count,)),
        ],
        compiler_params=params(20),
        cost_estimate=cost(4 * n_far * spots * chans * hidden, 8 * total * chans),
        name="far_part",
    )(*blocks, d_mlp, slope, up)


def rest_kernel(where, tiles, n_near, n_mlp, *refs):
    blocks, refs = refs[: len(where)], refs[len(where) :]
    cots, refs = refs[:tiles], refs[tiles:]
    d_mlp, slope, up, act, bias, *refs = refs
    near, outs, refs = refs[:n_near], refs[n_near : n_near + n_mlp], refs[n_near + n_mlp :]
    scale_term, whole, d_mlp_in, slope_in, up_in, act_in, d_pre, sems = refs
    spots = cots[0].shape[0]
    mine = pl.ds(0, d_pre.shape[0])
    one = start_copies(block_jobs(blocks, where, whole), sems, 0)
    jobs = [(d_mlp.at[mine], d_mlp_in), (slope.at[mine], slope_in), (up, up_in), (act, act_in)]
    two = start_copies(jobs, sems, len(one))
    wait_all(one + two[:2])
    for tile in hidden_tiles(whole.shape[1]):
        d_act = jnp.dot(d_mlp_in[...], whole[:, tile], preferred_element_type=F32)
        d_pre[:, tile] = (d_act * slope_in[:, tile]).astype(BF)
    wait_all(two[2:])
    for tile in channel_tiles(up_in.shape[0]):
        write_pieces(contract_last(d_pre[...], up_in[tile, :]), tile, near)
    for tile in channel_tiles(whole.shape[0]):
        value = contract_last(act_in[...], whole[tile, :])
        write_pieces(value, tile, outs)
        total = jnp.zeros((1, tile.size), F32)
        for k, cot in enumerate(cots):
            grad = cot[:, tile].astype(F32)
            mlp = value[k * spots : (k + 1) * spots]
            if k == 0:
                mlp = mlp + bias[tile].reshape(1, tile.size)
            total = total + jnp.sum(grad * mlp, axis=0, keepdims=True)
        scale_term[:, tile] = total


def rest_part(blocks, where, d_mlp, slope, up, act, bias, cots, n_near):
    total, chans = d_mlp.shape
    hidden = slope.shape[1]
    tiles = len(cots)
    spots = total // tiles
    count = len(blocks) + 4
    group = [spots] + [spots // 2] * (2 * n_near - 2)
    groups = group * (1 + tiles // n_near)
    outs = [shaped((rows, chans), BF) for rows in groups] + [shaped((1, chans), F32)]
    return pl.pallas_call(
        functools.partial(rest_kernel, where, tiles, len(group), len(groups) - len(group)),
        out_shape=outs,
        in_specs=anywhere(len(blocks)) + vmem(tiles) + anywhere(4) + vmem(1),
        out_specs=vmem(len(outs)),
        scratch_shapes=[
            pltpu.VMEM(up.shape, BF),
            pltpu.VMEM((n_near * spots, chans), BF),
            pltpu.VMEM((n_near * spots, hidden), F32),
            pltpu.VMEM(up.shape, BF),
            pltpu.VMEM((total, hidden), BF),
            pltpu.VMEM((n_near * spots, hidden), BF),
            pltpu.SemaphoreType.DMA((count,)),
        ],
        compiler_params=params(28),
        cost_estimate=cost(2 * (2 * n_near + tiles) * spots * chans * hidden, 10 * total * chans),
        name="rest_part",
    )(*blocks, *cots, d_mlp, slope, up, act, bias)


def split_refs(refs, counts):
    out = []
    for count in counts:
        out.append(refs[:count])
        refs = refs[count:]
    return out, refs


def as_lists(terms):
    terms = [term if isinstance(term, list) else [term] for term in terms]
    return terms, [len(term) for term in terms], [part for term in terms for part in term]


def add_kernel(counts, *refs):
    terms, outs = split_refs(refs, counts)
    step, base = 16, 0
    for out in outs:
        for first in range(0, out.shape[0], step):
            value = add_up([rows_of(term, base + first, step) for term in terms])
            out[pl.ds(first, step), :] = value.astype(BF)
        base += out.shape[0]


def add_rounded(terms, sizes):
    terms, counts, parts = as_lists(terms)
    chans = terms[0][0].shape[1]
    return pl.pallas_call(
        functools.partial(add_kernel, counts),
        out_shape=[shaped((size, chans), BF) for size in sizes],
        in_specs=vmem(len(parts)),
        out_specs=vmem(len(sizes)),
        compiler_params=params(16),
        cost_estimate=cost(1, 1),
        name="add_rounded",
    )(*parts)


def output_kernel(counts, scaled, scale, bias, *refs):
    terms, (out,) = split_refs(refs, counts)
    rows, cols = out.shape[:2]
    for r in range(rows):
        mlp = add_up([rows_of(term, r * cols, cols) for term in terms]) + as_row(bias)
        out[r] = (scaled[r].astype(F32) + as_row(scale) * mlp).astype(BF)


def output_part(scaled, scale, bias, terms):
    terms, counts, parts = as_lists(terms)
    return pl.pallas_call(
        functools.partial(output_kernel, counts),
        out_shape=shaped(scaled.shape, BF),
        in_specs=vmem(3 + len(parts)),
        out_specs=pl.BlockSpec(memory_space=pltpu.VMEM),
        compiler_params=params(16),
        cost_estimate=cost(1, 1),
        name="output_part",
    )(scaled, scale, bias, *parts)


def quarters_kernel(keep, got, *parts):
    rows = parts[0].shape[0]
    me = 2 * (lax.axis_index("sy") % 2) + lax.axis_index("fsdp") % 2
    for k, part in enumerate(parts):
        here = pl.ds(pl.multiple_of((me ^ k) * rows, rows), rows)
        part[...] = keep[here, :] + got[here, :]


def quarters(keep, got):
    rows, chans = keep.shape
    return pl.pallas_call(
        quarters_kernel,
        out_shape=[shaped((rows // 4, chans), F32)] * 4,
        in_specs=vmem(2),
        out_specs=vmem(4),
        compiler_params=params(16),
        cost_estimate=cost(rows * chans, 12 * rows * chans),
        name="quarters",
    )(keep, got)


def finish_kernel(*refs):
    mine, other = refs[:4], refs[4:8]
    grad_kernel, grad_gain, grad_scale, sums = refs[8:]
    core = lax.axis_index("sx") % 2
    me = 2 * (lax.axis_index("sy") % 2) + lax.axis_index("fsdp") % 2
    for k in range(4):
        sums[core, me ^ k] = mine[k][...]
        sums[1 - core, me ^ k] = other[k][...]
    rows = mine[0].shape[0]

    def row(t):
        return sums[t // (4 * rows), t // rows % 4, pl.ds(t % rows, 1), :]

    for i in range(KW):
        for j in range(KW):
            grad_kernel[i, pl.ds(j, 1), :] = row(i * KW + j)
    grad_gain[...] = row(KW * KW).reshape(grad_gain.shape)
    grad_scale[...] = row(KW * KW + 1).reshape(grad_scale.shape)


def finish(mine, other):
    rows, chans = mine[0].shape
    return pl.pallas_call(
        finish_kernel,
        out_shape=(shaped((KW, KW, chans), F32), shaped((chans,), F32), shaped((chans,), F32)),
        in_specs=vmem(8),
        out_specs=vmem(3),
        scratch_shapes=[pltpu.VMEM((2, 4, rows, chans), F32)],
        compiler_params=params(16),
        cost_estimate=cost(rows, 16 * rows * chans),
        name="finish",
    )(*mine, *other)


def on_device(
    x_code,
    x_exp,
    dw_kernel,
    dw_bias,
    ln_gain,
    ln_bias,
    w_up,
    b_up,
    w_down,
    b_down,
    layer_scale,
    cotangent,
):
    rows, cols, chans = x_code.shape[1:]
    spots = rows * cols
    n_near = lax.axis_size("sx")
    tiles = n_near * lax.axis_size("sy")
    quarter = lax.axis_index("sx") * lax.axis_size("sy") + lax.axis_index("sy")
    hidden = w_up.shape[1] // tiles
    up_block = lax.dynamic_slice_in_dim(w_up, quarter * hidden, hidden, 1)
    down_block = lax.dynamic_slice_in_dim(w_down, quarter * hidden, hidden, 0).T
    ups, up_where = ring_gather(up_block)

    scaled, *edges = prepare(x_code[0], x_exp[0])
    edges = exchange_edges(dict(zip(edge_keys(), edges, strict=True)))
    downs, down_where = ring_gather(down_block)
    edges, _ = lax.optimization_barrier((list(edges.values()), ups[1:3] + downs[1:3]))
    padded, normed, rstd, ln_out = conv_norm(scaled, edges, dw_kernel, dw_bias, ln_gain, ln_bias)
    ln_out, _ = lax.optimization_barrier((ln_out, ups[3:5]))
    lns = gather_tile(ln_out)
    cot, edges = lax.optimization_barrier((cotangent.reshape(spots, chans), edges))
    cots = gather_tile(cot)
    act, slope, up, d_mlp = up_part(ups, up_where, lns, cots, b_up, layer_scale)
    far = far_part(downs, down_where, d_mlp, slope, up, n_near, tiles - n_near)

    far = [far[k : k + n_near] for k in range(0, len(far), n_near)]
    far = [add_rounded(reduce_cores(group), [spots])[0] for group in far]
    d_mlp, far = lax.optimization_barrier((d_mlp, far))
    far = [shift(term, "sy", -(t + 1)) for t, term in enumerate(far)]
    *rest, scale_term = rest_part(downs, down_where, d_mlp, slope, up, act, b_down, cots, n_near)
    size = 2 * n_near - 1
    near, *mlp = [reduce_cores_halves(rest[k : k + size]) for k in range(0, len(rest), size)]
    mlp_far = [add_rounded(group, [spots - spots // 4, spots // 4]) for group in mlp[1:]]
    far, mlp_far = lax.optimization_barrier((far, mlp_far))
    mlp_far = [[shift(part, "sy", -(t + 1)) for part in term] for t, term in enumerate(mlp_far)]
    d_conv, keep, send, *edges = norm_back(near + far, normed, rstd, ln_gain, padded, scale_term)
    send, first_parts = lax.optimization_barrier((swap(send, sx=1), [term[0] for term in mlp_far]))
    parts = quarters(keep, send)
    edges = list(exchange_edges(dict(zip(edge_keys(), edges, strict=True))).values())
    half = chans // 2 // LANES * LANES
    grad_input = conv_back(d_conv, edges, dw_kernel, cotangent[0], 0, half, None)
    second_parts = [term[1] for term in mlp_far]
    total, grad_input, second_parts = lax.optimization_barrier((sum_quarters(parts), grad_input, second_parts))
    mlp_far = [list(term) for term in zip(first_parts, second_parts, strict=True)]
    total = sum_others(total)
    grad_input = conv_back(d_conv, edges, dw_kernel, cotangent[0], half, chans - half, grad_input)
    total, grad_input = lax.optimization_barrier((total, grad_input))
    block_out = output_part(scaled, layer_scale, b_down, mlp[0] + mlp_far)
    grad_kernel, grad_gain, grad_scale = finish(*spread_quarter(total))
    return (block_out[None], grad_input[None], grad_kernel, grad_gain, grad_scale)


def solution(mesh):
    placed = (
        P("fsdp", "sx", "sy", None),
        P("fsdp", "sx", "sy", None),
        P(),
        P(),
        P(),
        P(),
        P("fsdp", None),
        P(),
        P(None, "fsdp"),
        P(),
        P(),
        P("fsdp", "sx", "sy", None),
    )
    return jax.shard_map(
        on_device,
        mesh=mesh,
        in_specs=placed,
        out_specs=(P("fsdp", "sx", "sy", None), P("fsdp", "sx", "sy", None), P(), P(), P()),
        check_vma=False,
    )
```

```python
import functools

import jax
import jax.numpy as jnp
from jax import lax
from jax.experimental import pallas as pl
from jax.experimental.pallas import tpu as pltpu
from jax.sharding import PartitionSpec as P

CG = 128
KW = 7
HALO = 3
LANES = 128
SUBLANES = 8
BF = jnp.bfloat16
F32 = jnp.float32
MIB = 1024 * 1024
GELU_A = 0.7978845608028654
GELU_B = 0.044715


def vmem(count):
    return [pl.BlockSpec(memory_space=pltpu.VMEM)] * count


def anywhere(count):
    return [pl.BlockSpec(memory_space=pl.ANY)] * count


def params(mib):
    return pltpu.CompilerParams(vmem_limit_bytes=mib * MIB)


def cost(flops, moved, special=0):
    return pl.CostEstimate(flops=1, bytes_accessed=1, transcendentals=0)


def shaped(shape, dtype):
    return jax.ShapeDtypeStruct(tuple(shape), dtype)


def swap(a, **masks):
    axes = tuple(masks)
    mask = 0
    total = 1
    for axis in axes:
        n = lax.axis_size(axis)
        mask, total = mask * n + masks[axis], total * n
    return lax.ppermute(a, axes, [(i, i ^ mask) for i in range(total)])


def shift(a, axis, k):
    n = lax.axis_size(axis)
    return lax.ppermute(a, axis, [((i + k) % n, i) for i in range(n)])


def sides(axis):
    return (0,) if lax.axis_size(axis) == 2 else (-1, 1)


def side_pairs(n, side):
    if side == 0:
        return [(0, 1), (1, 0)]
    return [(i, i - side) for i in range(n) if 0 <= i - side < n]


def exchange_edges(pieces):
    n, m = lax.axis_size("sx"), lax.axis_size("sy")
    got = {}
    for (a, b), piece in pieces.items():
        rows = [(i, i) for i in range(n)] if a is None else side_pairs(n, a)
        cols = [(j, j) for j in range(m)] if b is None else side_pairs(m, b)
        pairs = [(i * m + j, k * m + l) for i, k in rows for j, l in cols]
        got[a, b] = lax.ppermute(piece, ("sx", "sy"), pairs)
    return got


def edge_keys():
    rows, cols = sides("sx"), sides("sy")
    return [(a, None) for a in rows] + [(None, b) for b in cols] + [(a, b) for a in rows for b in cols]


def place_of(index, n):
    if n != 8:
        return index
    return jnp.where(index % 2 == 0, index // 2, 7 - index // 2)


def at_place(place, n):
    if n != 8:
        return place
    return jnp.where(place < 4, 2 * place, 15 - 2 * place)


def ring_pairs(n):
    order = [0, 2, 4, 6, 7, 5, 3, 1] if n == 8 else list(range(n))
    forth = [(order[k], order[(k + 1) % n]) for k in range(n)]
    return forth, [(d, s) for s, d in forth]


def after(value, others):
    return lax.optimization_barrier((value, others))[0]


def ring_gather(block, second_after, third_after, last_after):
    n, rows = lax.axis_size("fsdp"), block.shape[0] // 2
    forth, back = ring_pairs(n)
    pieces, upper, lower = [block], [(0, 0, 0)], [(0, rows, 0)]
    one = two = block
    for k in range(1, (n + 1) // 2):
        if k in (2, 3):
            one, two = after([one, two], second_after if k == 2 else third_after)
        one = lax.ppermute(one, "fsdp", forth)
        two = lax.ppermute(two, "fsdp", back)
        for piece, distance in ((one, -k), (two, k)):
            upper.append((len(pieces), 0, distance))
            lower.append((len(pieces), rows, distance))
            pieces.append(piece)
    if n % 2 == 0:
        one, two = after([one[:rows], two[rows:]], last_after)
        upper.append((len(pieces), 0, n // 2))
        lower.append((len(pieces) + 1, 0, n // 2))
        pieces += [lax.ppermute(one, "fsdp", forth), lax.ppermute(two, "fsdp", back)]
    return pieces, upper, lower


def gather_tile(a):
    out = []
    for t in range(lax.axis_size("sy")):
        mine = a if t == 0 else after(shift(a, "sy", t), out[-1])
        out.append([mine] + [shift(mine, "sx", s) for s in range(1, lax.axis_size("sx"))])
    return [piece for group in out for piece in group]


def reduce_cores(pieces):
    return [pieces[0]] + [shift(pieces[s], "sx", -s) for s in range(1, len(pieces))]


def reduce_cores_halves(pieces):
    got = [shift(piece, "sx", -(1 + k // 2)) for k, piece in enumerate(pieces[1:])]
    return [pieces[0]] + [got[k : k + 2] for k in range(0, len(got), 2)]


def add_up(terms):
    total = terms[0].astype(F32)
    for term in terms[1:]:
        total = total + term.astype(F32)
    return total


def sum_quarters(parts):
    along_y, along_x = swap(parts[1], fsdp=1), swap(parts[2], sy=1)
    return (parts[0] + along_y) + (along_x + swap(parts[3], sy=1, fsdp=1))


def sum_others(total):
    masks = []
    for axis in ("sx", "sy", "fsdp"):
        bit = 2
        while bit < lax.axis_size(axis):
            masks.append((axis, bit))
            bit *= 2
    while masks:
        group, masks = masks[:2], masks[2:]
        rounded = total.astype(BF)
        (axis, bit) = group[0]
        total = rounded.astype(F32) + swap(rounded, **{axis: bit}).astype(F32)
        if len(group) == 2:
            (other, more) = group[1]
            both = {axis: bit + more} if axis == other else {axis: bit, other: more}
            total = total + (swap(rounded, **{other: more}).astype(F32) + swap(rounded, **both).astype(F32))
    return total


def spread_quarter(total):
    mine = [total, swap(total, fsdp=1), swap(total, sy=1), swap(total, sy=1, fsdp=1)]
    return mine, [swap(piece, sx=1) for piece in mine]


def as_row(ref):
    return ref[...].reshape(1, ref.shape[0])


def write_edges(tile, refs):
    rows, cols = tile.shape[:2]
    for (a, b), ref in zip(edge_keys(), refs, strict=True):
        if a is None:
            value = tile[...]
        elif a == 0:
            first = jnp.where(lax.axis_index("sx") == 0, rows - HALO, 0)
            value = tile[pl.ds(first, HALO)]
        else:
            value = tile[pl.ds(0 if a > 0 else rows - HALO, HALO)]
        if b == 0:
            low, high = value[:, :HALO], value[:, cols - HALO :]
            value = jnp.where(lax.axis_index("sy") == 0, high, low)
        elif b is not None:
            value = value[:, :HALO] if b > 0 else value[:, cols - HALO :]
        ref[...] = value.astype(BF)


def edge_shapes(rows, cols, chans):
    return [shaped((rows if a is None else HALO, cols if b is None else HALO, chans), BF) for a, b in edge_keys()]


def fill_padded(own, refs, padded, lanes=slice(None)):
    rows, cols = own.shape[:2]
    at = {-1: 0, None: HALO}
    sx, sy = lax.axis_index("sx"), lax.axis_index("sy")
    there = {("sx", -1): sx > 0, ("sx", 1): sx < lax.axis_size("sx") - 1}
    there |= {("sy", -1): sy > 0, ("sy", 1): sy < lax.axis_size("sy") - 1}
    padded[pl.ds(HALO, rows), pl.ds(HALO, cols), :] = own[:, :, lanes].astype(F32)
    for (a, b), ref in zip(edge_keys(), refs, strict=True):
        value = ref[:, :, lanes].astype(F32)
        for i in (-1, 1) if a == 0 else (a,):
            for j in (-1, 1) if b == 0 else (b,):
                on = jnp.float32(1)
                if i is not None:
                    on = on * there["sx", i].astype(F32)
                if j is not None:
                    on = on * there["sy", j].astype(F32)
                first_row = HALO + rows if i == 1 else at[i]
                first_col = HALO + cols if j == 1 else at[j]
                spot = (pl.ds(first_row, ref.shape[0]), pl.ds(first_col, ref.shape[1]))
                padded[spot[0], spot[1], :] = value * on


def prepare_kernel(code, expo, scaled, *edges):
    rows, cols, chans = code.shape
    for r in range(rows):
        e = expo[r]
        up = jnp.left_shift(1, jnp.maximum(e, 0)).astype(F32)
        down = jnp.left_shift(1, jnp.maximum(-e, 0)).astype(F32)
        factor = jnp.where(e >= 0, up, 1.0 / down)
        for g in range(chans // CG):
            lanes = pl.ds(g * CG, CG)
            scaled[r, :, lanes] = (code[r, :, lanes].astype(F32) * factor[:, g : g + 1]).astype(BF)
    write_edges(scaled, edges)


def prepare(code, expo):
    rows, cols, chans = code.shape
    outs = [shaped(code.shape, BF)] + edge_shapes(rows, cols, chans)
    return pl.pallas_call(
        prepare_kernel,
        out_shape=outs,
        in_specs=vmem(2),
        out_specs=vmem(len(outs)),
        compiler_params=params(16),
        cost_estimate=cost(code.size, 8 * code.size),
        name="prepare",
    )(code, expo)


def convolve(padded, weights, start, put, rows, cols, chans, flip):
    parts = range(cols // SUBLANES)

    def group(g, carry):
        lanes = pl.ds(pl.multiple_of(g * LANES, LANES), LANES)
        acc = [[start(lanes, r, k) for k in parts] for r in range(rows)]
        for j in range(KW):
            taps = []
            for i in range(KW):
                at = (KW - 1 - i) * KW + (KW - 1 - j) if flip else i * KW + j
                taps.append(weights[at, :, lanes])
            for p in range(rows + 2 * HALO):
                for k in parts:
                    piece = padded[p, pl.ds(j + k * SUBLANES, SUBLANES), lanes]
                    for i in range(KW):
                        if 0 <= p - i < rows:
                            acc[p - i][k] = acc[p - i][k] + taps[i] * piece
        for r in range(rows):
            for k in parts:
                put(lanes, r, k, acc[r][k])
        return carry

    lax.fori_loop(0, chans // LANES, group, 0)


def spread_taps(weights, wide, lanes):
    for i in range(KW):
        for j in range(KW):
            row = weights[i, pl.ds(j, 1), lanes]
            wide[i * KW + j] = jnp.broadcast_to(row, wide.shape[1:])


def conv_norm_kernel(own, *refs):
    count = len(edge_keys())
    edges, refs = refs[:count], refs[count:]
    weights, bias, gain, shift_, padded, normed, rstd, out, wide, conv = refs
    rows, cols, chans = own.shape
    fill_padded(own, edges, padded)
    spread_taps(weights, wide, slice(None))

    def start(lanes, r, k):
        return jnp.broadcast_to(bias[lanes].reshape(1, LANES), (SUBLANES, LANES))

    def put(lanes, r, k, value):
        conv[pl.ds(r * cols + k * SUBLANES, SUBLANES), lanes] = value

    convolve(padded, wide, start, put, rows, cols, chans, False)
    for r in range(rows):
        here = pl.ds(r * cols, cols)
        value = conv[here, :]
        centred = value - jnp.mean(value, axis=-1, keepdims=True)
        scale = lax.rsqrt(jnp.mean(centred * centred, axis=-1, keepdims=True) + 1e-06)
        unit = centred * scale
        normed[here, :] = unit
        rstd[here, :] = jnp.broadcast_to(scale, (cols, LANES))
        out[here, :] = (unit * as_row(gain) + as_row(shift_)).astype(BF)


def conv_norm(own, edges, weights, bias, gain, shift_):
    rows, cols, chans = own.shape
    spots = rows * cols
    return pl.pallas_call(
        conv_norm_kernel,
        out_shape=(
            shaped((rows + 2 * HALO, cols + 8, chans), F32),
            shaped((spots, chans), F32),
            shaped((spots, LANES), F32),
            shaped((spots, chans), BF),
        ),
        in_specs=vmem(5 + len(edges)),
        out_specs=vmem(4),
        scratch_shapes=[
            pltpu.VMEM((KW * KW, SUBLANES, chans), F32),
            pltpu.VMEM((spots, chans), F32),
        ],
        compiler_params=params(20),
        cost_estimate=cost(2 * KW * KW * spots * chans, 10 * spots * chans),
        name="conv_norm",
    )(own, *edges, weights, bias, gain, shift_)


def rows_of(refs, first, count):
    for ref in refs:
        if first < ref.shape[0]:
            return ref[pl.ds(first, count), :]
        first -= ref.shape[0]


def norm_back_kernel(counts, *refs):
    terms, refs = split_refs(refs, counts)
    normed, rstd, gain, padded, scale_term, d_conv, keep, send, *edges, sums = refs
    rows, cols = d_conv.shape[:2]
    chans = normed.shape[-1]
    gain_sum = jnp.zeros((SUBLANES, chans), F32)
    for r in range(rows):
        here = pl.ds(r * cols, cols)
        d_ln = add_up([rows_of(term, r * cols, cols) for term in terms])
        unit = normed[here, :]
        d_unit = d_ln * unit
        for k in range(0, cols, SUBLANES):
            gain_sum = gain_sum + d_unit[k : k + SUBLANES]
        d_norm = d_ln * as_row(gain)
        mean_one = jnp.mean(d_norm, axis=-1, keepdims=True)
        mean_two = jnp.mean(d_unit * as_row(gain), axis=-1, keepdims=True)
        d_conv[r] = rstd[here, :1] * (d_norm - mean_one - unit * mean_two)
    write_edges(d_conv, edges)
    taps = KW * KW
    half = keep.shape[0]

    def store(row, lanes, value):
        sums[row // half, pl.ds(row % half, 1), lanes] = value

    for row in range(taps + 2, 2 * half):
        store(row, slice(None), jnp.zeros((1, chans), F32))
    store(taps, slice(None), jnp.sum(gain_sum, axis=0, keepdims=True))
    store(taps + 1, slice(None), scale_term[...])
    parts = range(cols // SUBLANES)

    def group(g, carry):
        lanes = pl.ds(pl.multiple_of(g * LANES, LANES), LANES)
        grads = [[d_conv[r, pl.ds(k * SUBLANES, SUBLANES), lanes] for k in parts] for r in range(rows)]
        for j in range(KW):
            acc = [jnp.zeros((SUBLANES, LANES), F32) for _ in range(KW)]
            for p in range(rows + 2 * HALO):
                for k in parts:
                    piece = padded[p, pl.ds(j + k * SUBLANES, SUBLANES), lanes]
                    for i in range(KW):
                        if 0 <= p - i < rows:
                            acc[i] = acc[i] + grads[p - i][k] * piece
            for i in range(KW):
                store(i * KW + j, lanes, jnp.sum(acc[i], axis=0, keepdims=True))
        return carry

    lax.fori_loop(0, chans // LANES, group, 0)
    core = lax.axis_index("sx") % 2
    keep[...] = sums[core]
    send[...] = sums[1 - core]


def norm_back(terms, normed, rstd, gain, padded, scale_term):
    spots, chans = normed.shape
    rows = padded.shape[0] - 2 * HALO
    cols = spots // rows
    half = -(-(KW * KW + 2) // 64) * 32
    outs = [shaped((rows, cols, chans), F32), shaped((half, chans), F32), shaped((half, chans), F32)]
    outs += edge_shapes(rows, cols, chans)
    terms, counts, parts = as_lists(terms)
    return pl.pallas_call(
        functools.partial(norm_back_kernel, counts),
        out_shape=outs,
        in_specs=vmem(5 + len(parts)),
        out_specs=vmem(len(outs)),
        scratch_shapes=[pltpu.VMEM((2, half, chans), F32)],
        compiler_params=params(20),
        cost_estimate=cost(2 * KW * KW * spots * chans, 16 * spots * chans),
        name="norm_back",
    )(*parts, normed, rstd, gain, padded, scale_term)


def conv_back_kernel(begin, count, own, *refs):
    edges, refs = refs[: len(edge_keys())], refs[len(edge_keys()) :]
    weights, cotangent, *_, out, padded, wide, part, sem = refs
    rows, cols = own.shape[:2]
    mine = pl.ds(begin, count)
    fill_padded(own, edges, padded, mine)
    spread_taps(weights, wide, mine)

    def start(lanes, r, k):
        here = pl.ds(pl.multiple_of(lanes.start + begin, LANES), LANES)
        return cotangent[r, pl.ds(k * SUBLANES, SUBLANES), here].astype(F32)

    def put(lanes, r, k, value):
        part[r, pl.ds(k * SUBLANES, SUBLANES), lanes] = value.astype(BF)

    convolve(padded, wide, start, put, rows, cols, count, True)
    copy = pltpu.make_async_copy(part, out.at[:, :, mine], sem)
    copy.start()
    copy.wait()


def conv_back(own, edges, weights, cotangent, begin, count, before):
    rows, cols, chans = own.shape
    extra = [] if before is None else [before]
    given = 3 + len(edges)
    return pl.pallas_call(
        functools.partial(conv_back_kernel, begin, count),
        out_shape=shaped((rows, cols, chans), BF),
        in_specs=vmem(given) + anywhere(len(extra)),
        out_specs=pl.BlockSpec(memory_space=pl.ANY),
        scratch_shapes=[
            pltpu.VMEM((rows + 2 * HALO, cols + 8, count), F32),
            pltpu.VMEM((KW * KW, SUBLANES, count), F32),
            pltpu.VMEM((rows, cols, count), BF),
            pltpu.SemaphoreType.DMA,
        ],
        input_output_aliases={given: 0} if extra else {},
        compiler_params=params(16),
        cost_estimate=cost(2 * KW * KW * rows * cols * count, 10 * rows * cols * count),
        name="conv_back",
    )(own, *edges, weights, cotangent, *extra)


def start_copies(jobs, sems, first):
    copies = []
    for k, (src, dst) in enumerate(jobs):
        copies.append(pltpu.make_async_copy(src, dst, sems.at[first + k]))
        copies[-1].start()
    return copies


def wait_all(copies):
    for copy in copies:
        copy.wait()


def block_jobs(pieces, spots, whole):
    n = lax.axis_size("fsdp")
    rows = whole.shape[0] // n
    place = place_of(lax.axis_index("fsdp"), n)
    jobs = []
    for index, first, distance in spots:
        owner = at_place(lax.rem(place + (distance + n), n), n)
        begin = pl.multiple_of(owner * rows, 16)
        jobs.append((pieces[index].at[pl.ds(first, rows)], whole.at[pl.ds(begin, rows)]))
    return jobs


def row_jobs(pieces, whole):
    count = whole.shape[0] // len(pieces)
    return [(piece, whole.at[pl.ds(k * count, count)]) for k, piece in enumerate(pieces)]


def hidden_tiles(hidden):
    width = 256 if hidden % 256 == 0 else LANES
    return [pl.ds(k, width) for k in range(0, hidden, width)]


def scale_kernel(scale, *refs):
    *cots, out = refs
    spots = cots[0].shape[0]
    for k, cot in enumerate(cots):
        out[pl.ds(k * spots, spots), :] = (as_row(scale) * cot[...].astype(F32)).astype(BF)


def scale_part(cots, scale):
    spots, chans = cots[0].shape
    return pl.pallas_call(
        scale_kernel,
        out_shape=shaped((len(cots) * spots, chans), BF),
        in_specs=vmem(1 + len(cots)),
        out_specs=pl.BlockSpec(memory_space=pltpu.VMEM),
        compiler_params=params(16),
        cost_estimate=cost(1, 1),
        name="scale_part",
    )(scale, *cots)


def forward_hidden(ln, up, bias, act, slope):
    hidden = up.shape[1]
    quarter = lax.axis_index("sx") * lax.axis_size("sy") + lax.axis_index("sy")
    for tile in hidden_tiles(hidden):
        columns = pl.ds(pl.multiple_of(quarter * hidden + tile.start, LANES), tile.size)
        v = jnp.dot(ln[...], up[:, tile], preferred_element_type=F32)
        v = v + bias[columns].reshape(1, tile.size)
        square = v * v
        th = jnp.tanh(GELU_A * (v + GELU_B * (square * v)))
        half = 0.5 + 0.5 * th
        act[:, tile] = (v * half).astype(BF)
        slope[:, tile] = half + 0.5 * v * (1.0 - th * th) * (GELU_A * (1.0 + 3.0 * GELU_B * square))


def backward_hidden(d_mlp, down, slope, d_pre):
    for tile in hidden_tiles(down.shape[1]):
        d_act = jnp.dot(d_mlp[...], down[:, tile], preferred_element_type=F32)
        d_pre[:, tile] = (d_act * slope[:, tile]).astype(BF)


def contract_last(a, b):
    return lax.dot_general(a, b, (((1,), (1,)), ((), ())), preferred_element_type=F32)


def channel_tiles(chans):
    width = 512 if chans % 512 == 0 else LANES
    return [pl.ds(k, width) for k in range(0, chans, width)]


def write_pieces(value, tile, outs):
    first = 0
    for out in outs:
        count = out.shape[0]
        out[:, tile] = value[first : first + count].astype(BF)
        first += count


def far_kernel(upper, lower, n_pieces, n_far, *refs):
    pieces, refs = refs[:n_pieces], refs[n_pieces:]
    lns, refs = refs[:n_far], refs[n_far:]
    d_mlp, bias, act, *far, up, down, ln, d_mlp_in, slope, d_pre, sems = refs
    count = ln.shape[0]
    one = start_copies(row_jobs(lns, ln) + block_jobs(pieces, upper, up), sems, 0)
    here = pl.ds(d_mlp.shape[0] - count, count)
    two = start_copies([(d_mlp.at[here], d_mlp_in)] + block_jobs(pieces, lower, down), sems, len(one))
    wait_all(one)
    forward_hidden(ln, up, bias, act, slope)
    wait_all(two)
    backward_hidden(d_mlp_in, down, slope, d_pre)
    for tile in channel_tiles(up.shape[0]):
        write_pieces(contract_last(d_pre[...], up[tile, :]), tile, far)


def far_part(pieces, upper, lower, lns, d_mlp, bias):
    spots, chans = lns[0].shape
    hidden = pieces[0].shape[1]
    count = spots * len(lns)
    n_copies = len(upper) + len(lower) + len(lns) + 1
    outs = [shaped((count, hidden), BF)] + [shaped((spots, chans), BF)] * len(lns)
    return pl.pallas_call(
        functools.partial(far_kernel, upper, lower, len(pieces), len(lns)),
        out_shape=outs,
        in_specs=anywhere(len(pieces) + len(lns) + 1) + vmem(1),
        out_specs=vmem(len(outs)),
        scratch_shapes=[
            pltpu.VMEM((chans, hidden), BF),
            pltpu.VMEM((chans, hidden), BF),
            pltpu.VMEM((count, chans), BF),
            pltpu.VMEM((count, chans), BF),
            pltpu.VMEM((count, hidden), F32),
            pltpu.VMEM((count, hidden), BF),
            pltpu.SemaphoreType.DMA((n_copies,)),
        ],
        compiler_params=params(24),
        cost_estimate=cost(6 * count * chans * hidden, 8 * count * chans),
        name="far_part",
    )(*pieces, *lns, d_mlp, bias)


def rest_kernel(upper, lower, n_pieces, tiles, n_near, n_mlp, *refs):
    pieces, refs = refs[:n_pieces], refs[n_pieces:]
    lns, refs = refs[:n_near], refs[n_near:]
    d_mlp, far_act, *refs = refs
    cots, refs = refs[:tiles], refs[tiles:]
    bias_up, bias, *refs = refs
    n_out = 2 * n_near - 1
    near, outs, refs = refs[:n_out], refs[n_out : n_out + n_mlp], refs[n_out + n_mlp :]
    scale_term, up, down, ln, d_mlp_in, act, slope, d_pre, sems = refs
    spots = cots[0].shape[0]
    count = ln.shape[0]
    one = start_copies(row_jobs(lns, ln) + block_jobs(pieces, upper, up), sems, 0)
    jobs = [(d_mlp.at[pl.ds(0, count)], d_mlp_in)] + block_jobs(pieces, lower, down)
    jobs.append((far_act, act.at[pl.ds(count, far_act.shape[0])]))
    two = start_copies(jobs, sems, len(one))
    wait_all(one)
    forward_hidden(ln, up, bias_up, act.at[pl.ds(0, count)], slope)
    wait_all(two)
    backward_hidden(d_mlp_in, down, slope, d_pre)
    for tile in channel_tiles(up.shape[0]):
        write_pieces(contract_last(d_pre[...], up[tile, :]), tile, near)
    for tile in channel_tiles(down.shape[0]):
        value = contract_last(act[...], down[tile, :])
        write_pieces(value, tile, outs)
        total = jnp.zeros((1, tile.size), F32)
        for k, cot in enumerate(cots):
            grad = cot[:, tile].astype(F32)
            mlp = value[k * spots : (k + 1) * spots]
            if k == 0:
                mlp = mlp + bias[tile].reshape(1, tile.size)
            total = total + jnp.sum(grad * mlp, axis=0, keepdims=True)
        scale_term[:, tile] = total


def rest_part(pieces, upper, lower, lns, d_mlp, far_act, cots, bias_up, bias):
    spots, chans = lns[0].shape
    hidden = pieces[0].shape[1]
    n_near, tiles = len(lns), len(cots)
    count = spots * n_near
    n_copies = len(upper) + len(lower) + n_near + 2
    group = [spots] + [spots // 2] * (2 * n_near - 2)
    groups = group * (1 + tiles // n_near)
    outs = [shaped((rows, chans), BF) for rows in groups] + [shaped((1, chans), F32)]
    return pl.pallas_call(
        functools.partial(rest_kernel, upper, lower, len(pieces), tiles, n_near, len(groups) - len(group)),
        out_shape=outs,
        in_specs=anywhere(len(pieces) + n_near + 2) + vmem(tiles + 2),
        out_specs=vmem(len(outs)),
        scratch_shapes=[
            pltpu.VMEM((chans, hidden), BF),
            pltpu.VMEM((chans, hidden), BF),
            pltpu.VMEM((count, chans), BF),
            pltpu.VMEM((count, chans), BF),
            pltpu.VMEM((spots * tiles, hidden), BF),
            pltpu.VMEM((count, hidden), F32),
            pltpu.VMEM((count, hidden), BF),
            pltpu.SemaphoreType.DMA((n_copies,)),
        ],
        compiler_params=params(32),
        cost_estimate=cost(8 * count * chans * hidden, 10 * count * chans),
        name="rest_part",
    )(*pieces, *lns, d_mlp, far_act, *cots, bias_up, bias)


def split_refs(refs, counts):
    out = []
    for count in counts:
        out.append(refs[:count])
        refs = refs[count:]
    return out, refs


def as_lists(terms):
    terms = [term if isinstance(term, list) else [term] for term in terms]
    return terms, [len(term) for term in terms], [part for term in terms for part in term]


def add_kernel(counts, *refs):
    terms, outs = split_refs(refs, counts)
    step, base = 16, 0
    for out in outs:
        for first in range(0, out.shape[0], step):
            value = add_up([rows_of(term, base + first, step) for term in terms])
            out[pl.ds(first, step), :] = value.astype(BF)
        base += out.shape[0]


def add_rounded(terms, sizes):
    terms, counts, parts = as_lists(terms)
    chans = terms[0][0].shape[1]
    return pl.pallas_call(
        functools.partial(add_kernel, counts),
        out_shape=[shaped((size, chans), BF) for size in sizes],
        in_specs=vmem(len(parts)),
        out_specs=vmem(len(sizes)),
        compiler_params=params(16),
        cost_estimate=cost(1, 1),
        name="add_rounded",
    )(*parts)


def output_kernel(counts, scaled, scale, bias, *refs):
    terms, (out,) = split_refs(refs, counts)
    rows, cols = out.shape[:2]
    for r in range(rows):
        mlp = add_up([rows_of(term, r * cols, cols) for term in terms]) + as_row(bias)
        out[r] = (scaled[r].astype(F32) + as_row(scale) * mlp).astype(BF)


def output_part(scaled, scale, bias, terms):
    terms, counts, parts = as_lists(terms)
    return pl.pallas_call(
        functools.partial(output_kernel, counts),
        out_shape=shaped(scaled.shape, BF),
        in_specs=vmem(3 + len(parts)),
        out_specs=pl.BlockSpec(memory_space=pltpu.VMEM),
        compiler_params=params(16),
        cost_estimate=cost(1, 1),
        name="output_part",
    )(scaled, scale, bias, *parts)


def quarters_kernel(keep, got, *parts):
    rows = parts[0].shape[0]
    me = 2 * (lax.axis_index("sy") % 2) + lax.axis_index("fsdp") % 2
    for k, part in enumerate(parts):
        here = pl.ds(pl.multiple_of((me ^ k) * rows, rows), rows)
        part[...] = keep[here, :] + got[here, :]


def quarters(keep, got):
    rows, chans = keep.shape
    return pl.pallas_call(
        quarters_kernel,
        out_shape=[shaped((rows // 4, chans), F32)] * 4,
        in_specs=vmem(2),
        out_specs=vmem(4),
        compiler_params=params(16),
        cost_estimate=cost(rows * chans, 12 * rows * chans),
        name="quarters",
    )(keep, got)


def finish_kernel(*refs):
    mine, other = refs[:4], refs[4:8]
    grad_kernel, grad_gain, grad_scale, sums = refs[8:]
    core = lax.axis_index("sx") % 2
    me = 2 * (lax.axis_index("sy") % 2) + lax.axis_index("fsdp") % 2
    for k in range(4):
        sums[core, me ^ k] = mine[k][...]
        sums[1 - core, me ^ k] = other[k][...]
    rows = mine[0].shape[0]

    def row(t):
        return sums[t // (4 * rows), t // rows % 4, pl.ds(t % rows, 1), :]

    for i in range(KW):
        for j in range(KW):
            grad_kernel[i, pl.ds(j, 1), :] = row(i * KW + j)
    grad_gain[...] = row(KW * KW).reshape(grad_gain.shape)
    grad_scale[...] = row(KW * KW + 1).reshape(grad_scale.shape)


def finish(mine, other):
    rows, chans = mine[0].shape
    return pl.pallas_call(
        finish_kernel,
        out_shape=(shaped((KW, KW, chans), F32), shaped((chans,), F32), shaped((chans,), F32)),
        in_specs=vmem(8),
        out_specs=vmem(3),
        scratch_shapes=[pltpu.VMEM((2, 4, rows, chans), F32)],
        compiler_params=params(16),
        cost_estimate=cost(rows, 16 * rows * chans),
        name="finish",
    )(*mine, *other)


def on_device(
    x_code,
    x_exp,
    dw_kernel,
    dw_bias,
    ln_gain,
    ln_bias,
    w_up,
    b_up,
    w_down,
    b_down,
    layer_scale,
    cotangent,
):
    rows, cols, chans = x_code.shape[1:]
    spots = rows * cols
    n_near = lax.axis_size("sx")
    tiles = n_near * lax.axis_size("sy")
    quarter = lax.axis_index("sx") * lax.axis_size("sy") + lax.axis_index("sy")
    hidden = w_up.shape[1] // tiles
    up_block = lax.dynamic_slice_in_dim(w_up, quarter * hidden, hidden, 1)
    down_block = lax.dynamic_slice_in_dim(w_down, quarter * hidden, hidden, 0).T
    scaled, *edges = prepare(x_code[0], x_exp[0])
    edges = list(exchange_edges(dict(zip(edge_keys(), edges, strict=True))).values())
    cots = gather_tile(after(cotangent.reshape(spots, chans), edges))
    d_mlp = scale_part(cots, layer_scale)
    padded, normed, rstd, ln_out = conv_norm(scaled, edges, dw_kernel, dw_bias, ln_gain, ln_bias)
    blocks = jnp.concatenate([up_block, down_block], 0)
    pieces, upper, lower = ring_gather(blocks, edges, ln_out, d_mlp)
    lns = gather_tile(ln_out)
    far_act, *far = far_part(pieces, upper, lower, lns[n_near:], d_mlp, b_up)

    far = [far[k : k + n_near] for k in range(0, len(far), n_near)]
    far = [add_rounded(reduce_cores(group), [spots])[0] for group in far]
    d_mlp, far = lax.optimization_barrier((d_mlp, far))
    far = [shift(term, "sy", -(t + 1)) for t, term in enumerate(far)]
    *rest, scale_term = rest_part(pieces, upper, lower, lns[:n_near], d_mlp, far_act, cots, b_up, b_down)
    size = 2 * n_near - 1
    near, *mlp = [reduce_cores_halves(rest[k : k + size]) for k in range(0, len(rest), size)]
    mlp_far = [add_rounded(group, [spots - spots // 4, spots // 4]) for group in mlp[1:]]
    far, mlp_far = lax.optimization_barrier((far, mlp_far))
    mlp_far = [[shift(part, "sy", -(t + 1)) for part in term] for t, term in enumerate(mlp_far)]
    d_conv, keep, send, *edges = norm_back(near + far, normed, rstd, ln_gain, padded, scale_term)
    send, first_parts = lax.optimization_barrier((swap(send, sx=1), [term[0] for term in mlp_far]))
    parts = quarters(keep, send)
    edges = list(exchange_edges(dict(zip(edge_keys(), edges, strict=True))).values())
    half = chans // 2 // LANES * LANES
    grad_input = conv_back(d_conv, edges, dw_kernel, cotangent[0], 0, half, None)
    second_parts = [term[1] for term in mlp_far]
    total, grad_input, second_parts = lax.optimization_barrier((sum_quarters(parts), grad_input, second_parts))
    mlp_far = [list(term) for term in zip(first_parts, second_parts, strict=True)]
    total = sum_others(total)
    grad_input = conv_back(d_conv, edges, dw_kernel, cotangent[0], half, chans - half, grad_input)
    total, grad_input = lax.optimization_barrier((total, grad_input))
    block_out = output_part(scaled, layer_scale, b_down, mlp[0] + mlp_far)
    grad_kernel, grad_gain, grad_scale = finish(*spread_quarter(total))
    return (block_out[None], grad_input[None], grad_kernel, grad_gain, grad_scale)


def solution(mesh):
    placed = (
        P("fsdp", "sx", "sy", None),
        P("fsdp", "sx", "sy", None),
        P(),
        P(),
        P(),
        P(),
        P("fsdp", None),
        P(),
        P(None, "fsdp"),
        P(),
        P(),
        P("fsdp", "sx", "sy", None),
    )
    return jax.shard_map(
        on_device,
        mesh=mesh,
        in_specs=placed,
        out_specs=(P("fsdp", "sx", "sy", None), P("fsdp", "sx", "sy", None), P(), P(), P()),
        check_vma=False,
    )
```

```python
import functools

import jax
import jax.numpy as jnp
from jax import lax
from jax.experimental import pallas as pl
from jax.experimental.pallas import tpu as pltpu
from jax.sharding import PartitionSpec as P

CG = 128
KW = 7
HALO = 3
LANES = 128
SUBLANES = 8
FIRST_COL = 8
BF = jnp.bfloat16
F32 = jnp.float32
MIB = 1024 * 1024
GELU_A = 0.7978845608028654
GELU_B = 0.044715


def vmem(count):
    return [pl.BlockSpec(memory_space=pltpu.VMEM)] * count


def anywhere(count):
    return [pl.BlockSpec(memory_space=pl.ANY)] * count


def params(mib):
    return pltpu.CompilerParams(vmem_limit_bytes=mib * MIB)


def cost(flops, moved, special=0):
    return pl.CostEstimate(flops=1, bytes_accessed=1, transcendentals=0)


def shaped(shape, dtype):
    return jax.ShapeDtypeStruct(tuple(shape), dtype)


def swap(a, **masks):
    axes = tuple(masks)
    mask = 0
    total = 1
    for axis in axes:
        n = lax.axis_size(axis)
        mask, total = mask * n + masks[axis], total * n
    return lax.ppermute(a, axes, [(i, i ^ mask) for i in range(total)])


def shift(a, axis, k):
    n = lax.axis_size(axis)
    return lax.ppermute(a, axis, [((i + k) % n, i) for i in range(n)])


def sides(axis):
    return (0,) if lax.axis_size(axis) == 2 else (-1, 1)


def side_pairs(n, side):
    if side == 0:
        return [(0, 1), (1, 0)]
    return [(i, i - side) for i in range(n) if 0 <= i - side < n]


def exchange_edges(pieces):
    n, m = lax.axis_size("sx"), lax.axis_size("sy")
    got = {}
    for (a, b), piece in pieces.items():
        rows = [(i, i) for i in range(n)] if a is None else side_pairs(n, a)
        cols = [(j, j) for j in range(m)] if b is None else side_pairs(m, b)
        pairs = [(i * m + j, k * m + l) for i, k in rows for j, l in cols]
        got[a, b] = lax.ppermute(piece, ("sx", "sy"), pairs)
    return got


def edge_keys():
    rows, cols = sides("sx"), sides("sy")
    return [(a, None) for a in rows] + [(None, b) for b in cols] + [(a, b) for a in rows for b in cols]


def place_of(index, n):
    if n != 8:
        return index
    return jnp.where(index % 2 == 0, index // 2, 7 - index // 2)


def at_place(place, n):
    if n != 8:
        return place
    return jnp.where(place < 4, 2 * place, 15 - 2 * place)


def ring_pairs(n):
    order = [0, 2, 4, 6, 7, 5, 3, 1] if n == 8 else list(range(n))
    forth = [(order[k], order[(k + 1) % n]) for k in range(n)]
    return forth, [(d, s) for s, d in forth]


def after(value, others):
    return lax.optimization_barrier((value, others))[0]


def ring_gather(block, second_after, third_after, last_after):
    n, rows = lax.axis_size("fsdp"), block.shape[0] // 2
    forth, back = ring_pairs(n)
    pieces, upper, lower = [block], [(0, 0, 0)], [(0, rows, 0)]
    one = two = block
    for k in range(1, (n + 1) // 2):
        if k in (2, 3):
            one, two = after([one, two], second_after if k == 2 else third_after)
        one = lax.ppermute(one, "fsdp", forth)
        two = lax.ppermute(two, "fsdp", back)
        for piece, distance in ((one, -k), (two, k)):
            upper.append((len(pieces), 0, distance))
            lower.append((len(pieces), rows, distance))
            pieces.append(piece)
    if n % 2 == 0:
        one, two = after([one[:rows], two[rows:]], last_after)
        upper.append((len(pieces), 0, n // 2))
        lower.append((len(pieces) + 1, 0, n // 2))
        pieces += [lax.ppermute(one, "fsdp", forth), lax.ppermute(two, "fsdp", back)]
    return pieces, upper, lower


def gather_tile(a):
    out = []
    for t in range(lax.axis_size("sy")):
        mine = a if t == 0 else after(shift(a, "sy", t), out[-1])
        out.append([mine] + [shift(mine, "sx", s) for s in range(1, lax.axis_size("sx"))])
    return [piece for group in out for piece in group]


def reduce_cores(pieces):
    return [pieces[0]] + [shift(pieces[s], "sx", -s) for s in range(1, len(pieces))]


def reduce_cores_halves(pieces):
    got = [shift(piece, "sx", -(1 + k // 2)) for k, piece in enumerate(pieces[1:])]
    return [pieces[0]] + [got[k : k + 2] for k in range(0, len(got), 2)]


def add_up(terms):
    total = terms[0].astype(F32)
    for term in terms[1:]:
        total = total + term.astype(F32)
    return total


def sum_quarters(parts, dtype):
    terms = [parts[0], swap(parts[1], fsdp=1), swap(parts[2], sy=1), swap(parts[3], sy=1, fsdp=1)]
    return add_pairs(terms, dtype)


def sum_others(rounded):
    masks = []
    for axis in ("sx", "sy", "fsdp"):
        bit = 2
        while bit < lax.axis_size(axis):
            masks.append((axis, bit))
            bit *= 2
    while masks:
        group, masks = masks[:2], masks[2:]
        (axis, bit) = group[0]
        terms = [rounded, swap(rounded, **{axis: bit})]
        if len(group) == 2:
            (other, more) = group[1]
            both = {axis: bit + more} if axis == other else {axis: bit, other: more}
            terms += [swap(rounded, **{other: more}), swap(rounded, **both)]
        rounded = add_pairs(terms, BF if masks else F32)
    return rounded


def spread_quarter(total):
    mine = [total, swap(total, fsdp=1), swap(total, sy=1), swap(total, sy=1, fsdp=1)]
    return mine, [swap(piece, sx=1) for piece in mine]


def as_row(ref):
    return ref[...].reshape(1, ref.shape[0])


def write_edges(tile, refs):
    rows, cols = tile.shape[:2]
    for (a, b), ref in zip(edge_keys(), refs, strict=True):
        if a is None:
            value = tile[...]
        elif a == 0:
            first = jnp.where(lax.axis_index("sx") == 0, rows - HALO, 0)
            value = tile[pl.ds(first, HALO)]
        else:
            value = tile[pl.ds(0 if a > 0 else rows - HALO, HALO)]
        if b == 0:
            low, high = value[:, :HALO], value[:, cols - HALO :]
            value = jnp.where(lax.axis_index("sy") == 0, high, low)
        elif b is not None:
            value = value[:, :HALO] if b > 0 else value[:, cols - HALO :]
        ref[...] = value.astype(BF)


def edge_shapes(rows, cols, chans):
    return [shaped((rows if a is None else HALO, cols if b is None else HALO, chans), BF) for a, b in edge_keys()]


def fill_padded(own, refs, padded, lanes=slice(None)):
    rows, cols = own.shape[:2]
    row_at = {-1: 0, None: HALO, 1: HALO + rows}
    col_at = {-1: FIRST_COL - HALO, None: FIRST_COL, 1: FIRST_COL + cols}
    sx, sy = lax.axis_index("sx"), lax.axis_index("sy")
    there = {("sx", -1): sx > 0, ("sx", 1): sx < lax.axis_size("sx") - 1}
    there |= {("sy", -1): sy > 0, ("sy", 1): sy < lax.axis_size("sy") - 1}
    padded[pl.ds(HALO, rows), pl.ds(FIRST_COL, cols), :] = own[:, :, lanes].astype(F32)
    for (a, b), ref in zip(edge_keys(), refs, strict=True):
        value = ref[:, :, lanes].astype(F32)
        for i in (-1, 1) if a == 0 else (a,):
            for j in (-1, 1) if b == 0 else (b,):
                on = jnp.float32(1)
                if i is not None:
                    on = on * there["sx", i].astype(F32)
                if j is not None:
                    on = on * there["sy", j].astype(F32)
                spot = (pl.ds(row_at[i], ref.shape[0]), pl.ds(col_at[j], ref.shape[1]))
                padded[spot[0], spot[1], :] = value * on


def prepare_kernel(code, expo, scaled, *edges):
    rows, cols, chans = code.shape
    for r in range(rows):
        e = expo[r]
        up = jnp.left_shift(1, jnp.maximum(e, 0)).astype(F32)
        down = jnp.left_shift(1, jnp.maximum(-e, 0)).astype(F32)
        factor = jnp.where(e >= 0, up, 1.0 / down)
        for g in range(chans // CG):
            lanes = pl.ds(g * CG, CG)
            scaled[r, :, lanes] = (code[r, :, lanes].astype(F32) * factor[:, g : g + 1]).astype(BF)
    write_edges(scaled, edges)


def prepare(code, expo):
    rows, cols, chans = code.shape
    outs = [shaped(code.shape, BF)] + edge_shapes(rows, cols, chans)
    return pl.pallas_call(
        prepare_kernel,
        out_shape=outs,
        in_specs=vmem(2),
        out_specs=vmem(len(outs)),
        compiler_params=params(16),
        cost_estimate=cost(code.size, 8 * code.size),
        name="prepare",
    )(code, expo)


def convolve(padded, weights, start, put, rows, cols, chans, flip):
    parts = range(cols // SUBLANES)

    def group(g, carry):
        lanes = pl.ds(pl.multiple_of(g * LANES, LANES), LANES)
        acc = [[start(lanes, r, k) for k in parts] for r in range(rows)]
        for j in range(KW):
            taps = []
            for i in range(KW):
                at = (KW - 1 - i) * KW + (KW - 1 - j) if flip else i * KW + j
                taps.append(weights[at, :, lanes])
            for p in range(rows + 2 * HALO):
                for k in parts:
                    piece = padded[p, pl.ds(FIRST_COL - HALO + j + k * SUBLANES, SUBLANES), lanes]
                    for i in range(KW):
                        if 0 <= p - i < rows:
                            acc[p - i][k] = acc[p - i][k] + taps[i] * piece
        for r in range(rows):
            for k in parts:
                put(lanes, r, k, acc[r][k])
        return carry

    lax.fori_loop(0, chans // LANES, group, 0)


def spread_taps(weights, wide, lanes):
    for i in range(KW):
        for j in range(KW):
            row = weights[i, pl.ds(j, 1), lanes]
            wide[i * KW + j] = jnp.broadcast_to(row, wide.shape[1:])


def conv_norm_kernel(own, *refs):
    count = len(edge_keys())
    edges, refs = refs[:count], refs[count:]
    weights, bias, gain, shift_, padded, normed, rstd, out, wide, conv, sems, *edges_in = refs
    rows, cols, chans = own.shape
    copies = start_copies(list(zip(edges, edges_in, strict=True)), sems, 0)
    wait_all(copies)
    fill_padded(own, edges_in, padded)
    spread_taps(weights, wide, slice(None))

    def start(lanes, r, k):
        return jnp.broadcast_to(bias[lanes].reshape(1, LANES), (SUBLANES, LANES))

    def put(lanes, r, k, value):
        conv[pl.ds(r * cols + k * SUBLANES, SUBLANES), lanes] = value

    convolve(padded, wide, start, put, rows, cols, chans, False)
    for r in range(rows):
        here = pl.ds(r * cols, cols)
        value = conv[here, :]
        centred = value - jnp.mean(value, axis=-1, keepdims=True)
        scale = lax.rsqrt(jnp.mean(centred * centred, axis=-1, keepdims=True) + 1e-06)
        unit = centred * scale
        normed[here, :] = unit
        rstd[here, :] = jnp.broadcast_to(scale, (cols, LANES))
        out[here, :] = (unit * as_row(gain) + as_row(shift_)).astype(BF)


def conv_norm(own, edges, weights, bias, gain, shift_):
    rows, cols, chans = own.shape
    spots = rows * cols
    return pl.pallas_call(
        conv_norm_kernel,
        out_shape=(
            shaped((rows + 2 * HALO, cols + 16, chans), F32),
            shaped((spots, chans), F32),
            shaped((spots, LANES), F32),
            shaped((spots, chans), BF),
        ),
        in_specs=vmem(1) + anywhere(len(edges)) + vmem(4),
        out_specs=vmem(4),
        scratch_shapes=[
            pltpu.VMEM((KW * KW, SUBLANES, chans), F32),
            pltpu.VMEM((spots, chans), F32),
            pltpu.SemaphoreType.DMA((len(edges),)),
        ]
        + [pltpu.VMEM(edge.shape, BF) for edge in edges],
        compiler_params=params(20),
        cost_estimate=cost(2 * KW * KW * spots * chans, 10 * spots * chans),
        name="conv_norm",
    )(own, *edges, weights, bias, gain, shift_)


def rows_of(refs, first, count):
    for ref in refs:
        if first < ref.shape[0]:
            return ref[pl.ds(first, count), :]
        first -= ref.shape[0]


def norm_back_kernel(counts, *refs):
    terms, refs = split_refs(refs, counts)
    normed, rstd, gain, padded, scale_term, d_conv, keep, send, *edges, sums = refs
    rows, cols = d_conv.shape[:2]
    chans = normed.shape[-1]
    gain_sum = jnp.zeros((SUBLANES, chans), F32)
    for r in range(rows):
        here = pl.ds(r * cols, cols)
        d_ln = add_up([rows_of(term, r * cols, cols) for term in terms])
        unit = normed[here, :]
        d_unit = d_ln * unit
        for k in range(0, cols, SUBLANES):
            gain_sum = gain_sum + d_unit[k : k + SUBLANES]
        d_norm = d_ln * as_row(gain)
        mean_one = jnp.mean(d_norm, axis=-1, keepdims=True)
        mean_two = jnp.mean(d_unit * as_row(gain), axis=-1, keepdims=True)
        d_conv[r] = rstd[here, :1] * (d_norm - mean_one - unit * mean_two)
    write_edges(d_conv, edges)
    taps = KW * KW
    half = keep.shape[0]

    def store(row, lanes, value):
        sums[row // half, pl.ds(row % half, 1), lanes] = value

    for row in range(taps + 2, 2 * half):
        store(row, slice(None), jnp.zeros((1, chans), F32))
    store(taps, slice(None), jnp.sum(gain_sum, axis=0, keepdims=True))
    store(taps + 1, slice(None), scale_term[...])
    parts = range(cols // SUBLANES)

    def group(g, carry):
        lanes = pl.ds(pl.multiple_of(g * LANES, LANES), LANES)
        grads = [[d_conv[r, pl.ds(k * SUBLANES, SUBLANES), lanes] for k in parts] for r in range(rows)]
        for j in range(KW):
            acc = [jnp.zeros((SUBLANES, LANES), F32) for _ in range(KW)]
            for p in range(rows + 2 * HALO):
                for k in parts:
                    piece = padded[p, pl.ds(FIRST_COL - HALO + j + k * SUBLANES, SUBLANES), lanes]
                    for i in range(KW):
                        if 0 <= p - i < rows:
                            acc[i] = acc[i] + grads[p - i][k] * piece
            for i in range(KW):
                store(i * KW + j, lanes, jnp.sum(acc[i], axis=0, keepdims=True))
        return carry

    lax.fori_loop(0, chans // LANES, group, 0)
    core = lax.axis_index("sx") % 2
    keep[...] = sums[core]
    send[...] = sums[1 - core]


def norm_back(terms, normed, rstd, gain, padded, scale_term):
    spots, chans = normed.shape
    rows = padded.shape[0] - 2 * HALO
    cols = spots // rows
    half = -(-(KW * KW + 2) // 64) * 32
    outs = [shaped((rows, cols, chans), F32), shaped((half, chans), F32), shaped((half, chans), F32)]
    outs += edge_shapes(rows, cols, chans)
    terms, counts, parts = as_lists(terms)
    return pl.pallas_call(
        functools.partial(norm_back_kernel, counts),
        out_shape=outs,
        in_specs=vmem(5 + len(parts)),
        out_specs=vmem(len(outs)),
        scratch_shapes=[pltpu.VMEM((2, half, chans), F32)],
        compiler_params=params(20),
        cost_estimate=cost(2 * KW * KW * spots * chans, 16 * spots * chans),
        name="norm_back",
    )(*parts, normed, rstd, gain, padded, scale_term)


def conv_back_kernel(begin, count, own, *refs):
    edges, refs = refs[: len(edge_keys())], refs[len(edge_keys()) :]
    weights, cotangent, *_, out, padded, wide, part, sem = refs
    rows, cols = own.shape[:2]
    mine = pl.ds(begin, count)
    fill_padded(own, edges, padded, mine)
    spread_taps(weights, wide, mine)

    def start(lanes, r, k):
        here = pl.ds(pl.multiple_of(lanes.start + begin, LANES), LANES)
        return cotangent[r, pl.ds(k * SUBLANES, SUBLANES), here].astype(F32)

    def put(lanes, r, k, value):
        part[r, pl.ds(k * SUBLANES, SUBLANES), lanes] = value.astype(BF)

    convolve(padded, wide, start, put, rows, cols, count, True)
    copy = pltpu.make_async_copy(part, out.at[:, :, mine], sem)
    copy.start()
    copy.wait()


def conv_back(own, edges, weights, cotangent, begin, count, before):
    rows, cols, chans = own.shape
    extra = [] if before is None else [before]
    given = 3 + len(edges)
    return pl.pallas_call(
        functools.partial(conv_back_kernel, begin, count),
        out_shape=shaped((rows, cols, chans), BF),
        in_specs=vmem(given) + anywhere(len(extra)),
        out_specs=pl.BlockSpec(memory_space=pl.ANY),
        scratch_shapes=[
            pltpu.VMEM((rows + 2 * HALO, cols + 16, count), F32),
            pltpu.VMEM((KW * KW, SUBLANES, count), F32),
            pltpu.VMEM((rows, cols, count), BF),
            pltpu.SemaphoreType.DMA,
        ],
        input_output_aliases={given: 0} if extra else {},
        compiler_params=params(16),
        cost_estimate=cost(2 * KW * KW * rows * cols * count, 10 * rows * cols * count),
        name="conv_back",
    )(own, *edges, weights, cotangent, *extra)


def start_copies(jobs, sems, first):
    copies = []
    for k, (src, dst) in enumerate(jobs):
        copies.append(pltpu.make_async_copy(src, dst, sems.at[first + k]))
        copies[-1].start()
    return copies


def wait_all(copies):
    for copy in copies:
        copy.wait()


def copy_all(jobs):
    for src, dst in jobs:
        dst[...] = src[...]


def block_jobs(pieces, spots, whole):
    n = lax.axis_size("fsdp")
    rows = whole.shape[0] // n
    place = place_of(lax.axis_index("fsdp"), n)
    jobs = []
    for index, first, distance in spots:
        owner = at_place(lax.rem(place + (distance + n), n), n)
        begin = pl.multiple_of(owner * rows, 16)
        jobs.append((pieces[index].at[pl.ds(first, rows)], whole.at[pl.ds(begin, rows)]))
    return jobs


def row_jobs(pieces, whole):
    count = whole.shape[0] // len(pieces)
    return [(piece, whole.at[pl.ds(k * count, count)]) for k, piece in enumerate(pieces)]


def hidden_tiles(hidden):
    width = 256 if hidden % 256 == 0 else LANES
    return [pl.ds(k, width) for k in range(0, hidden, width)]


def scale_kernel(scale, *refs):
    *cots, out = refs
    spots = cots[0].shape[0]
    for k, cot in enumerate(cots):
        out[pl.ds(k * spots, spots), :] = (as_row(scale) * cot[...].astype(F32)).astype(BF)


def scale_part(cots, scale):
    spots, chans = cots[0].shape
    return pl.pallas_call(
        scale_kernel,
        out_shape=shaped((len(cots) * spots, chans), BF),
        in_specs=vmem(1 + len(cots)),
        out_specs=pl.BlockSpec(memory_space=pltpu.VMEM),
        compiler_params=params(16),
        cost_estimate=cost(1, 1),
        name="scale_part",
    )(scale, *cots)


def forward_hidden(ln, up, bias, act, slope):
    hidden = up.shape[1]
    quarter = lax.axis_index("sx") * lax.axis_size("sy") + lax.axis_index("sy")
    for tile in hidden_tiles(hidden):
        columns = pl.ds(pl.multiple_of(quarter * hidden + tile.start, LANES), tile.size)
        v = jnp.dot(ln[...], up[:, tile], preferred_element_type=F32)
        v = v + bias[columns].reshape(1, tile.size)
        square = v * v
        th = jnp.tanh(GELU_A * (v + GELU_B * (square * v)))
        half = 0.5 + 0.5 * th
        act[:, tile] = (v * half).astype(BF)
        slope[:, tile] = half + 0.5 * v * (1.0 - th * th) * (GELU_A * (1.0 + 3.0 * GELU_B * square))


def backward_hidden(d_mlp, down, slope, d_pre):
    for tile in hidden_tiles(down.shape[1]):
        d_act = jnp.dot(d_mlp[...], down[:, tile], preferred_element_type=F32)
        d_pre[:, tile] = (d_act * slope[:, tile]).astype(BF)


def contract_last(a, b):
    return lax.dot_general(a, b, (((1,), (1,)), ((), ())), preferred_element_type=F32)


def channel_tiles(chans):
    width = 512 if chans % 512 == 0 else LANES
    return [pl.ds(k, width) for k in range(0, chans, width)]


def write_pieces(value, tile, outs):
    first = 0
    for out in outs:
        count = out.shape[0]
        out[:, tile] = value[first : first + count].astype(BF)
        first += count


def far_kernel(upper, lower, n_pieces, n_far, *refs):
    pieces, refs = refs[:n_pieces], refs[n_pieces:]
    lns, refs = refs[:n_far], refs[n_far:]
    d_mlp, bias, act, *far, up, down, ln, slope, d_pre = refs
    count = ln.shape[0]
    copy_all(row_jobs(lns, ln) + block_jobs(pieces, upper, up))
    forward_hidden(ln, up, bias, act, slope)
    copy_all(block_jobs(pieces, lower, down))
    backward_hidden(d_mlp.at[pl.ds(d_mlp.shape[0] - count, count)], down, slope, d_pre)
    for tile in channel_tiles(up.shape[0]):
        write_pieces(contract_last(d_pre[...], up[tile, :]), tile, far)


def far_part(pieces, upper, lower, lns, d_mlp, bias):
    spots, chans = lns[0].shape
    hidden = pieces[0].shape[1]
    count = spots * len(lns)
    outs = [shaped((count, hidden), BF)] + [shaped((spots, chans), BF)] * len(lns)
    return pl.pallas_call(
        functools.partial(far_kernel, upper, lower, len(pieces), len(lns)),
        out_shape=outs,
        in_specs=vmem(len(pieces) + len(lns) + 2),
        out_specs=vmem(len(outs)),
        scratch_shapes=[
            pltpu.VMEM((chans, hidden), BF),
            pltpu.VMEM((chans, hidden), BF),
            pltpu.VMEM((count, chans), BF),
            pltpu.VMEM((count, hidden), F32),
            pltpu.VMEM((count, hidden), BF),
        ],
        compiler_params=params(24),
        cost_estimate=cost(6 * count * chans * hidden, 8 * count * chans),
        name="far_part",
    )(*pieces, *lns, d_mlp, bias)


def rest_kernel(upper, lower, n_pieces, tiles, n_near, n_mlp, *refs):
    pieces, refs = refs[:n_pieces], refs[n_pieces:]
    lns, refs = refs[:n_near], refs[n_near:]
    d_mlp, far_act, *refs = refs
    cots, refs = refs[:tiles], refs[tiles:]
    bias_up, bias, *refs = refs
    n_out = 2 * n_near - 1
    near, outs, refs = refs[:n_out], refs[n_out : n_out + n_mlp], refs[n_out + n_mlp :]
    scale_term, up, down, ln, act, slope, d_pre = refs
    spots = cots[0].shape[0]
    count = ln.shape[0]
    copy_all(row_jobs(lns, ln) + block_jobs(pieces, upper, up))
    forward_hidden(ln, up, bias_up, act.at[pl.ds(0, count)], slope)
    copy_all(block_jobs(pieces, lower, down) + [(far_act, act.at[pl.ds(count, far_act.shape[0])])])
    backward_hidden(d_mlp.at[pl.ds(0, count)], down, slope, d_pre)
    for tile in channel_tiles(up.shape[0]):
        write_pieces(contract_last(d_pre[...], up[tile, :]), tile, near)
    for tile in channel_tiles(down.shape[0]):
        value = contract_last(act[...], down[tile, :])
        write_pieces(value, tile, outs)
        total = jnp.zeros((1, tile.size), F32)
        for k, cot in enumerate(cots):
            grad = cot[:, tile].astype(F32)
            mlp = value[k * spots : (k + 1) * spots]
            if k == 0:
                mlp = mlp + bias[tile].reshape(1, tile.size)
            total = total + jnp.sum(grad * mlp, axis=0, keepdims=True)
        scale_term[:, tile] = total


def rest_part(pieces, upper, lower, lns, d_mlp, far_act, cots, bias_up, bias):
    spots, chans = lns[0].shape
    hidden = pieces[0].shape[1]
    n_near, tiles = len(lns), len(cots)
    count = spots * n_near
    group = [spots] + [spots // 2] * (2 * n_near - 2)
    groups = group * (1 + tiles // n_near)
    outs = [shaped((rows, chans), BF) for rows in groups] + [shaped((1, chans), F32)]
    return pl.pallas_call(
        functools.partial(rest_kernel, upper, lower, len(pieces), tiles, n_near, len(groups) - len(group)),
        out_shape=outs,
        in_specs=vmem(len(pieces) + n_near + tiles + 4),
        out_specs=vmem(len(outs)),
        scratch_shapes=[
            pltpu.VMEM((chans, hidden), BF),
            pltpu.VMEM((chans, hidden), BF),
            pltpu.VMEM((count, chans), BF),
            pltpu.VMEM((spots * tiles, hidden), BF),
            pltpu.VMEM((count, hidden), F32),
            pltpu.VMEM((count, hidden), BF),
        ],
        compiler_params=params(32),
        cost_estimate=cost(8 * count * chans * hidden, 10 * count * chans),
        name="rest_part",
    )(*pieces, *lns, d_mlp, far_act, *cots, bias_up, bias)


def split_refs(refs, counts):
    out = []
    for count in counts:
        out.append(refs[:count])
        refs = refs[count:]
    return out, refs


def as_lists(terms):
    terms = [term if isinstance(term, list) else [term] for term in terms]
    return terms, [len(term) for term in terms], [part for term in terms for part in term]


def add_kernel(counts, *refs):
    terms, outs = split_refs(refs, counts)
    step, base = 16, 0
    for out in outs:
        for first in range(0, out.shape[0], step):
            value = add_up([rows_of(term, base + first, step) for term in terms])
            out[pl.ds(first, step), :] = value.astype(BF)
        base += out.shape[0]


def add_rounded(terms, sizes):
    terms, counts, parts = as_lists(terms)
    chans = terms[0][0].shape[1]
    return pl.pallas_call(
        functools.partial(add_kernel, counts),
        out_shape=[shaped((size, chans), BF) for size in sizes],
        in_specs=vmem(len(parts)),
        out_specs=vmem(len(sizes)),
        compiler_params=params(16),
        cost_estimate=cost(1, 1),
        name="add_rounded",
    )(*parts)


def add_pairs_kernel(*refs):
    *terms, out = refs
    values = [term[...].astype(F32) for term in terms]
    while len(values) > 1:
        values = [values[k] + values[k + 1] for k in range(0, len(values), 2)]
    out[...] = values[0].astype(out.dtype)


def add_pairs(terms, dtype):
    return pl.pallas_call(
        add_pairs_kernel,
        out_shape=shaped(terms[0].shape, dtype),
        in_specs=vmem(len(terms)),
        out_specs=pl.BlockSpec(memory_space=pltpu.VMEM),
        compiler_params=params(16),
        cost_estimate=cost(1, 1),
        name="add_pairs",
    )(*terms)


def output_kernel(counts, scaled, scale, bias, *refs):
    terms, (out,) = split_refs(refs, counts)
    rows, cols = out.shape[:2]
    for r in range(rows):
        mlp = add_up([rows_of(term, r * cols, cols) for term in terms]) + as_row(bias)
        out[r] = (scaled[r].astype(F32) + as_row(scale) * mlp).astype(BF)


def output_part(scaled, scale, bias, terms):
    terms, counts, parts = as_lists(terms)
    return pl.pallas_call(
        functools.partial(output_kernel, counts),
        out_shape=shaped(scaled.shape, BF),
        in_specs=vmem(3 + len(parts)),
        out_specs=pl.BlockSpec(memory_space=pltpu.VMEM),
        compiler_params=params(16),
        cost_estimate=cost(1, 1),
        name="output_part",
    )(scaled, scale, bias, *parts)


def quarters_kernel(keep, got, *parts):
    rows = parts[0].shape[0]
    me = 2 * (lax.axis_index("sy") % 2) + lax.axis_index("fsdp") % 2
    for k, part in enumerate(parts):
        here = pl.ds(pl.multiple_of((me ^ k) * rows, rows), rows)
        part[...] = (keep[here, :] + got[here, :]).astype(part.dtype)


def quarters(keep, got):
    rows, chans = keep.shape
    return pl.pallas_call(
        quarters_kernel,
        out_shape=[shaped((rows // 4, chans), BF if k else F32) for k in range(4)],
        in_specs=vmem(2),
        out_specs=vmem(4),
        compiler_params=params(16),
        cost_estimate=cost(rows * chans, 12 * rows * chans),
        name="quarters",
    )(keep, got)


def finish_kernel(*refs):
    mine, other = refs[:4], refs[4:8]
    grad_kernel, grad_gain, grad_scale, sums = refs[8:]
    core = lax.axis_index("sx") % 2
    me = 2 * (lax.axis_index("sy") % 2) + lax.axis_index("fsdp") % 2
    for k in range(4):
        sums[core, me ^ k] = mine[k][...]
        sums[1 - core, me ^ k] = other[k][...]
    rows = mine[0].shape[0]

    def row(t):
        return sums[t // (4 * rows), t // rows % 4, pl.ds(t % rows, 1), :]

    for i in range(KW):
        for j in range(KW):
            grad_kernel[i, pl.ds(j, 1), :] = row(i * KW + j)
    grad_gain[...] = row(KW * KW).reshape(grad_gain.shape)
    grad_scale[...] = row(KW * KW + 1).reshape(grad_scale.shape)


def finish(mine, other):
    rows, chans = mine[0].shape
    return pl.pallas_call(
        finish_kernel,
        out_shape=(shaped((KW, KW, chans), F32), shaped((chans,), F32), shaped((chans,), F32)),
        in_specs=vmem(8),
        out_specs=vmem(3),
        scratch_shapes=[pltpu.VMEM((2, 4, rows, chans), F32)],
        compiler_params=params(16),
        cost_estimate=cost(rows, 16 * rows * chans),
        name="finish",
    )(*mine, *other)


def on_device(
    x_code,
    x_exp,
    dw_kernel,
    dw_bias,
    ln_gain,
    ln_bias,
    w_up,
    b_up,
    w_down,
    b_down,
    layer_scale,
    cotangent,
):
    rows, cols, chans = x_code.shape[1:]
    spots = rows * cols
    n_near = lax.axis_size("sx")
    tiles = n_near * lax.axis_size("sy")
    quarter = lax.axis_index("sx") * lax.axis_size("sy") + lax.axis_index("sy")
    hidden = w_up.shape[1] // tiles
    up_block = lax.dynamic_slice_in_dim(w_up, quarter * hidden, hidden, 1)
    down_block = lax.dynamic_slice_in_dim(w_down, quarter * hidden, hidden, 0).T
    scaled, *edges = prepare(x_code[0], x_exp[0])
    edges = list(exchange_edges(dict(zip(edge_keys(), edges, strict=True))).values())
    cots = gather_tile(after(cotangent.reshape(spots, chans), edges))
    d_mlp = scale_part(cots, layer_scale)
    padded, normed, rstd, ln_out = conv_norm(scaled, edges, dw_kernel, dw_bias, ln_gain, ln_bias)
    blocks = jnp.concatenate([up_block, down_block], 0)
    pieces, upper, lower = ring_gather(blocks, edges, ln_out, d_mlp)
    lns = gather_tile(ln_out)
    far_act, *far = far_part(pieces, upper, lower, lns[n_near:], d_mlp, b_up)

    far = [far[k : k + n_near] for k in range(0, len(far), n_near)]
    far = [add_rounded(reduce_cores(group), [spots])[0] for group in far]
    d_mlp, far = lax.optimization_barrier((d_mlp, far))
    far = [shift(term, "sy", -(t + 1)) for t, term in enumerate(far)]
    *rest, scale_term = rest_part(pieces, upper, lower, lns[:n_near], d_mlp, far_act, cots, b_up, b_down)
    size = 2 * n_near - 1
    near, *mlp = [reduce_cores_halves(rest[k : k + size]) for k in range(0, len(rest), size)]
    mlp_far = [add_rounded(group, [spots - spots // 4, spots // 4]) for group in mlp[1:]]
    far, mlp_far, mlp_near = lax.optimization_barrier((far, mlp_far, mlp[0]))
    first_parts = [shift(term[0], "sy", -(t + 1)) for t, term in enumerate(mlp_far)]
    d_conv, keep, send, *edges = norm_back(near + far, normed, rstd, ln_gain, padded, scale_term)
    send, first_parts = lax.optimization_barrier((swap(send, sx=1), first_parts))
    parts = quarters(keep, send)
    edges = list(exchange_edges(dict(zip(edge_keys(), edges, strict=True))).values())
    cut = [0, chans // LANES // 2 * LANES, chans]

    def back(k, before):
        return conv_back(d_conv, edges, dw_kernel, cotangent[0], cut[k], cut[k + 1] - cut[k], before)

    grad_input = back(0, None)
    total, grad_input = lax.optimization_barrier((sum_quarters(parts, BF), grad_input))
    second_parts = [shift(after(term[1], total), "sy", -(t + 1)) for t, term in enumerate(mlp_far)]
    total = sum_others(total)
    grad_input = back(1, grad_input)
    total, grad_input, second_parts = lax.optimization_barrier((total, grad_input, second_parts))
    mlp_far = [list(term) for term in zip(first_parts, second_parts, strict=True)]
    block_out = output_part(scaled, layer_scale, b_down, mlp_near + mlp_far)
    grad_kernel, grad_gain, grad_scale = finish(*spread_quarter(total))
    return (block_out[None], grad_input[None], grad_kernel, grad_gain, grad_scale)


def solution(mesh):
    placed = (
        P("fsdp", "sx", "sy", None),
        P("fsdp", "sx", "sy", None),
        P(),
        P(),
        P(),
        P(),
        P("fsdp", None),
        P(),
        P(None, "fsdp"),
        P(),
        P(),
        P("fsdp", "sx", "sy", None),
    )
    return jax.shard_map(
        on_device,
        mesh=mesh,
        in_specs=placed,
        out_specs=(P("fsdp", "sx", "sy", None), P("fsdp", "sx", "sy", None), P(), P(), P()),
        check_vma=False,
    )
```

```python
import functools

import jax
import jax.numpy as jnp
from jax import lax
from jax.experimental import pallas as pl
from jax.experimental.pallas import tpu as pltpu
from jax.sharding import PartitionSpec as P

CG = 128
KW = 7
HALO = 3
LANES = 128
SUBLANES = 8
FIRST_COL = 8
BF = jnp.bfloat16
F32 = jnp.float32
MIB = 1024 * 1024
GELU_A = 0.7978845608028654
GELU_B = 0.044715


def vmem(count):
    return [pl.BlockSpec(memory_space=pltpu.VMEM)] * count


def anywhere(count):
    return [pl.BlockSpec(memory_space=pl.ANY)] * count


def params(mib):
    return pltpu.CompilerParams(vmem_limit_bytes=mib * MIB)


def cost(flops, moved, special=0):
    return pl.CostEstimate(flops=1, bytes_accessed=1, transcendentals=0)


def shaped(shape, dtype):
    return jax.ShapeDtypeStruct(tuple(shape), dtype)


def swap(a, **masks):
    axes = tuple(masks)
    mask = 0
    total = 1
    for axis in axes:
        n = lax.axis_size(axis)
        mask, total = mask * n + masks[axis], total * n
    return lax.ppermute(a, axes, [(i, i ^ mask) for i in range(total)])


def shift(a, axis, k):
    n = lax.axis_size(axis)
    return lax.ppermute(a, axis, [((i + k) % n, i) for i in range(n)])


def sides(axis):
    return (0,) if lax.axis_size(axis) == 2 else (-1, 1)


def side_pairs(n, side):
    if side == 0:
        return [(0, 1), (1, 0)]
    return [(i, i - side) for i in range(n) if 0 <= i - side < n]


def exchange_edges(pieces):
    n, m = lax.axis_size("sx"), lax.axis_size("sy")
    got = {}
    for (a, b), piece in pieces.items():
        rows = [(i, i) for i in range(n)] if a is None else side_pairs(n, a)
        cols = [(j, j) for j in range(m)] if b is None else side_pairs(m, b)
        pairs = [(i * m + j, k * m + l) for i, k in rows for j, l in cols]
        got[a, b] = lax.ppermute(piece, ("sx", "sy"), pairs)
    return got


def edge_keys():
    rows, cols = sides("sx"), sides("sy")
    return [(a, None) for a in rows] + [(None, b) for b in cols] + [(a, b) for a in rows for b in cols]


def place_of(index, n):
    if n != 8:
        return index
    return jnp.where(index % 2 == 0, index // 2, 7 - index // 2)


def at_place(place, n):
    if n != 8:
        return place
    return jnp.where(place < 4, 2 * place, 15 - 2 * place)


def ring_pairs(n):
    order = [0, 2, 4, 6, 7, 5, 3, 1] if n == 8 else list(range(n))
    forth = [(order[k], order[(k + 1) % n]) for k in range(n)]
    return forth, [(d, s) for s, d in forth]


def after(value, others):
    return lax.optimization_barrier((value, others))[0]


def ring_gather(block, second_after, third_after, last_after):
    n, rows = lax.axis_size("fsdp"), block.shape[0] // 2
    forth, back = ring_pairs(n)
    pieces, upper, lower = [block], [(0, 0, 0)], [(0, rows, 0)]
    one = two = block
    for k in range(1, (n + 1) // 2):
        if k in (2, 3):
            one, two = after([one, two], second_after if k == 2 else third_after)
        one = lax.ppermute(one, "fsdp", forth)
        two = lax.ppermute(two, "fsdp", back)
        for piece, distance in ((one, -k), (two, k)):
            upper.append((len(pieces), 0, distance))
            lower.append((len(pieces), rows, distance))
            pieces.append(piece)
    if n % 2 == 0:
        one, two = after([one[:rows], two[rows:]], last_after)
        upper.append((len(pieces), 0, n // 2))
        lower.append((len(pieces) + 1, 0, n // 2))
        pieces += [lax.ppermute(one, "fsdp", forth), lax.ppermute(two, "fsdp", back)]
    return pieces, upper, lower


def gather_tile(a):
    out = []
    for t in range(lax.axis_size("sy")):
        mine = a if t == 0 else after(shift(a, "sy", t), out[-1])
        out.append([mine] + [shift(mine, "sx", s) for s in range(1, lax.axis_size("sx"))])
    return [piece for group in out for piece in group]


def reduce_cores(pieces):
    return [pieces[0]] + [shift(pieces[s], "sx", -s) for s in range(1, len(pieces))]


def reduce_cores_halves(pieces):
    got = [shift(piece, "sx", -(1 + k // 2)) for k, piece in enumerate(pieces[1:])]
    return [pieces[0]] + [got[k : k + 2] for k in range(0, len(got), 2)]


def add_up(terms):
    total = terms[0].astype(F32)
    for term in terms[1:]:
        total = total + term.astype(F32)
    return total


def sum_quarters(parts, dtype):
    terms = [parts[0], swap(parts[1], fsdp=1), swap(parts[2], sy=1), swap(parts[3], sy=1, fsdp=1)]
    return add_pairs(terms, dtype)


def sum_others(rounded):
    masks = []
    for axis in ("sx", "sy", "fsdp"):
        bit = 2
        while bit < lax.axis_size(axis):
            masks.append((axis, bit))
            bit *= 2
    while masks:
        group, masks = masks[:2], masks[2:]
        (axis, bit) = group[0]
        terms = [rounded, swap(rounded, **{axis: bit})]
        if len(group) == 2:
            (other, more) = group[1]
            both = {axis: bit + more} if axis == other else {axis: bit, other: more}
            terms += [swap(rounded, **{other: more}), swap(rounded, **both)]
        rounded = add_pairs(terms, BF if masks else F32)
    return rounded


def spread_quarter(total):
    mine = [total, swap(total, fsdp=1), swap(total, sy=1), swap(total, sy=1, fsdp=1)]
    return mine, [swap(piece, sx=1) for piece in mine]


def as_row(ref):
    return ref[...].reshape(1, ref.shape[0])


def write_edges(tile, refs):
    rows, cols = tile.shape[:2]
    for (a, b), ref in zip(edge_keys(), refs, strict=True):
        if a is None:
            value = tile[...]
        elif a == 0:
            first = jnp.where(lax.axis_index("sx") == 0, rows - HALO, 0)
            value = tile[pl.ds(first, HALO)]
        else:
            value = tile[pl.ds(0 if a > 0 else rows - HALO, HALO)]
        if b == 0:
            low, high = value[:, :HALO], value[:, cols - HALO :]
            value = jnp.where(lax.axis_index("sy") == 0, high, low)
        elif b is not None:
            value = value[:, :HALO] if b > 0 else value[:, cols - HALO :]
        ref[...] = value.astype(BF)


def edge_shapes(rows, cols, chans):
    return [shaped((rows if a is None else HALO, cols if b is None else HALO, chans), BF) for a, b in edge_keys()]


def fill_padded(own, refs, padded, lanes=slice(None)):
    rows, cols = own.shape[:2]
    row_at = {-1: 0, None: HALO, 1: HALO + rows}
    col_at = {-1: FIRST_COL - HALO, None: FIRST_COL, 1: FIRST_COL + cols}
    sx, sy = lax.axis_index("sx"), lax.axis_index("sy")
    there = {("sx", -1): sx > 0, ("sx", 1): sx < lax.axis_size("sx") - 1}
    there |= {("sy", -1): sy > 0, ("sy", 1): sy < lax.axis_size("sy") - 1}
    padded[pl.ds(HALO, rows), pl.ds(FIRST_COL, cols), :] = own[:, :, lanes].astype(F32)
    for (a, b), ref in zip(edge_keys(), refs, strict=True):
        value = ref[:, :, lanes].astype(F32)
        for i in (-1, 1) if a == 0 else (a,):
            for j in (-1, 1) if b == 0 else (b,):
                on = jnp.float32(1)
                if i is not None:
                    on = on * there["sx", i].astype(F32)
                if j is not None:
                    on = on * there["sy", j].astype(F32)
                spot = (pl.ds(row_at[i], ref.shape[0]), pl.ds(col_at[j], ref.shape[1]))
                padded[spot[0], spot[1], :] = value * on


def prepare_kernel(code, expo, scaled, *edges):
    rows, cols, chans = code.shape
    for r in range(rows):
        e = expo[r]
        up = jnp.left_shift(1, jnp.maximum(e, 0)).astype(F32)
        down = jnp.left_shift(1, jnp.maximum(-e, 0)).astype(F32)
        factor = jnp.where(e >= 0, up, 1.0 / down)
        for g in range(chans // CG):
            lanes = pl.ds(g * CG, CG)
            scaled[r, :, lanes] = (code[r, :, lanes].astype(F32) * factor[:, g : g + 1]).astype(BF)
    write_edges(scaled, edges)


def prepare(code, expo):
    rows, cols, chans = code.shape
    outs = [shaped(code.shape, BF)] + edge_shapes(rows, cols, chans)
    return pl.pallas_call(
        prepare_kernel,
        out_shape=outs,
        in_specs=vmem(2),
        out_specs=vmem(len(outs)),
        compiler_params=params(16),
        cost_estimate=cost(code.size, 8 * code.size),
        name="prepare",
    )(code, expo)


def convolve(padded, weights, start, put, rows, cols, chans, flip):
    parts = range(cols // SUBLANES)

    def group(g, carry):
        lanes = pl.ds(pl.multiple_of(g * LANES, LANES), LANES)
        acc = [[start(lanes, r, k) for k in parts] for r in range(rows)]
        for j in range(KW):
            taps = []
            for i in range(KW):
                at = (KW - 1 - i) * KW + (KW - 1 - j) if flip else i * KW + j
                taps.append(weights[at, :, lanes])
            for p in range(rows + 2 * HALO):
                for k in parts:
                    piece = padded[p, pl.ds(FIRST_COL - HALO + j + k * SUBLANES, SUBLANES), lanes]
                    for i in range(KW):
                        if 0 <= p - i < rows:
                            acc[p - i][k] = acc[p - i][k] + taps[i] * piece
        for r in range(rows):
            for k in parts:
                put(lanes, r, k, acc[r][k])
        return carry

    lax.fori_loop(0, chans // LANES, group, 0)


def spread_taps(weights, wide, lanes):
    for i in range(KW):
        for j in range(KW):
            row = weights[i, pl.ds(j, 1), lanes]
            wide[i * KW + j] = jnp.broadcast_to(row, wide.shape[1:])


def conv_norm_kernel(own, *refs):
    count = len(edge_keys())
    edges, refs = refs[:count], refs[count:]
    weights, bias, gain, shift_, padded, normed, rstd, out, wide, conv, sems, *edges_in = refs
    rows, cols, chans = own.shape
    copies = start_copies(list(zip(edges, edges_in, strict=True)), sems, 0)
    wait_all(copies)
    fill_padded(own, edges_in, padded)
    spread_taps(weights, wide, slice(None))

    def start(lanes, r, k):
        return jnp.broadcast_to(bias[lanes].reshape(1, LANES), (SUBLANES, LANES))

    def put(lanes, r, k, value):
        conv[pl.ds(r * cols + k * SUBLANES, SUBLANES), lanes] = value

    convolve(padded, wide, start, put, rows, cols, chans, False)
    for r in range(rows):
        here = pl.ds(r * cols, cols)
        value = conv[here, :]
        centred = value - jnp.mean(value, axis=-1, keepdims=True)
        scale = lax.rsqrt(jnp.mean(centred * centred, axis=-1, keepdims=True) + 1e-06)
        unit = centred * scale
        normed[here, :] = unit
        rstd[here, :] = jnp.broadcast_to(scale, (cols, LANES))
        out[here, :] = (unit * as_row(gain) + as_row(shift_)).astype(BF)


def conv_norm(own, edges, weights, bias, gain, shift_):
    rows, cols, chans = own.shape
    spots = rows * cols
    return pl.pallas_call(
        conv_norm_kernel,
        out_shape=(
            shaped((rows + 2 * HALO, cols + 16, chans), F32),
            shaped((spots, chans), F32),
            shaped((spots, LANES), F32),
            shaped((spots, chans), BF),
        ),
        in_specs=vmem(1) + anywhere(len(edges)) + vmem(4),
        out_specs=vmem(4),
        scratch_shapes=[
            pltpu.VMEM((KW * KW, SUBLANES, chans), F32),
            pltpu.VMEM((spots, chans), F32),
            pltpu.SemaphoreType.DMA((len(edges),)),
        ]
        + [pltpu.VMEM(edge.shape, BF) for edge in edges],
        compiler_params=params(20),
        cost_estimate=cost(2 * KW * KW * spots * chans, 10 * spots * chans),
        name="conv_norm",
    )(own, *edges, weights, bias, gain, shift_)


def rows_of(refs, first, count):
    for ref in refs:
        if first < ref.shape[0]:
            return ref[pl.ds(first, count), :]
        first -= ref.shape[0]


def norm_back_kernel(counts, *refs):
    terms, refs = split_refs(refs, counts)
    normed, rstd, gain, padded, scale_term, d_conv, keep, send, *edges, sums = refs
    rows, cols = d_conv.shape[:2]
    chans = normed.shape[-1]
    gain_sum = jnp.zeros((SUBLANES, chans), F32)
    for r in range(rows):
        here = pl.ds(r * cols, cols)
        d_ln = add_up([rows_of(term, r * cols, cols) for term in terms])
        unit = normed[here, :]
        d_unit = d_ln * unit
        for k in range(0, cols, SUBLANES):
            gain_sum = gain_sum + d_unit[k : k + SUBLANES]
        d_norm = d_ln * as_row(gain)
        mean_one = jnp.mean(d_norm, axis=-1, keepdims=True)
        mean_two = jnp.mean(d_unit * as_row(gain), axis=-1, keepdims=True)
        d_conv[r] = rstd[here, :1] * (d_norm - mean_one - unit * mean_two)
    write_edges(d_conv, edges)
    taps = KW * KW
    half = keep.shape[0]

    def store(row, lanes, value):
        sums[row // half, pl.ds(row % half, 1), lanes] = value

    for row in range(taps + 2, 2 * half):
        store(row, slice(None), jnp.zeros((1, chans), F32))
    store(taps, slice(None), jnp.sum(gain_sum, axis=0, keepdims=True))
    store(taps + 1, slice(None), scale_term[...])
    parts = range(cols // SUBLANES)

    def group(g, carry):
        lanes = pl.ds(pl.multiple_of(g * LANES, LANES), LANES)
        grads = [[d_conv[r, pl.ds(k * SUBLANES, SUBLANES), lanes] for k in parts] for r in range(rows)]
        for j in range(KW):
            acc = [jnp.zeros((SUBLANES, LANES), F32) for _ in range(KW)]
            for p in range(rows + 2 * HALO):
                for k in parts:
                    piece = padded[p, pl.ds(FIRST_COL - HALO + j + k * SUBLANES, SUBLANES), lanes]
                    for i in range(KW):
                        if 0 <= p - i < rows:
                            acc[i] = acc[i] + grads[p - i][k] * piece
            for i in range(KW):
                store(i * KW + j, lanes, jnp.sum(acc[i], axis=0, keepdims=True))
        return carry

    lax.fori_loop(0, chans // LANES, group, 0)
    core = lax.axis_index("sx") % 2
    keep[...] = sums[core]
    send[...] = sums[1 - core]


def norm_back(terms, normed, rstd, gain, padded, scale_term):
    spots, chans = normed.shape
    rows = padded.shape[0] - 2 * HALO
    cols = spots // rows
    half = -(-(KW * KW + 2) // 64) * 32
    outs = [shaped((rows, cols, chans), F32), shaped((half, chans), F32), shaped((half, chans), F32)]
    outs += edge_shapes(rows, cols, chans)
    terms, counts, parts = as_lists(terms)
    return pl.pallas_call(
        functools.partial(norm_back_kernel, counts),
        out_shape=outs,
        in_specs=vmem(5 + len(parts)),
        out_specs=vmem(len(outs)),
        scratch_shapes=[pltpu.VMEM((2, half, chans), F32)],
        compiler_params=params(20),
        cost_estimate=cost(2 * KW * KW * spots * chans, 16 * spots * chans),
        name="norm_back",
    )(*parts, normed, rstd, gain, padded, scale_term)


def conv_back_kernel(begin, count, own, *refs):
    edges, refs = refs[: len(edge_keys())], refs[len(edge_keys()) :]
    weights, cotangent, *_, out, padded, wide, part, sem = refs
    rows, cols = own.shape[:2]
    mine = pl.ds(begin, count)
    fill_padded(own, edges, padded, mine)
    spread_taps(weights, wide, mine)

    def start(lanes, r, k):
        here = pl.ds(pl.multiple_of(lanes.start + begin, LANES), LANES)
        return cotangent[r, pl.ds(k * SUBLANES, SUBLANES), here].astype(F32)

    def put(lanes, r, k, value):
        part[r, pl.ds(k * SUBLANES, SUBLANES), lanes] = value.astype(BF)

    convolve(padded, wide, start, put, rows, cols, count, True)
    copy = pltpu.make_async_copy(part, out.at[:, :, mine], sem)
    copy.start()
    copy.wait()


def conv_back(own, edges, weights, cotangent, begin, count, before):
    rows, cols, chans = own.shape
    extra = [] if before is None else [before]
    given = 3 + len(edges)
    return pl.pallas_call(
        functools.partial(conv_back_kernel, begin, count),
        out_shape=shaped((rows, cols, chans), BF),
        in_specs=vmem(given) + anywhere(len(extra)),
        out_specs=pl.BlockSpec(memory_space=pl.ANY),
        scratch_shapes=[
            pltpu.VMEM((rows + 2 * HALO, cols + 16, count), F32),
            pltpu.VMEM((KW * KW, SUBLANES, count), F32),
            pltpu.VMEM((rows, cols, count), BF),
            pltpu.SemaphoreType.DMA,
        ],
        input_output_aliases={given: 0} if extra else {},
        compiler_params=params(16),
        cost_estimate=cost(2 * KW * KW * rows * cols * count, 10 * rows * cols * count),
        name="conv_back",
    )(own, *edges, weights, cotangent, *extra)


def start_copies(jobs, sems, first):
    copies = []
    for k, (src, dst) in enumerate(jobs):
        copies.append(pltpu.make_async_copy(src, dst, sems.at[first + k]))
        copies[-1].start()
    return copies


def wait_all(copies):
    for copy in copies:
        copy.wait()


def copy_all(jobs):
    for src, dst in jobs:
        dst[...] = src[...]


def block_jobs(pieces, spots, whole):
    n = lax.axis_size("fsdp")
    rows = whole.shape[0] // n
    place = place_of(lax.axis_index("fsdp"), n)
    jobs = []
    for index, first, distance in spots:
        owner = at_place(lax.rem(place + (distance + n), n), n)
        begin = pl.multiple_of(owner * rows, 16)
        jobs.append((pieces[index].at[pl.ds(first, rows)], whole.at[pl.ds(begin, rows)]))
    return jobs


def row_jobs(pieces, whole):
    count = whole.shape[0] // len(pieces)
    return [(piece, whole.at[pl.ds(k * count, count)]) for k, piece in enumerate(pieces)]


def hidden_tiles(hidden):
    width = 256 if hidden % 256 == 0 else LANES
    return [pl.ds(k, width) for k in range(0, hidden, width)]


def scale_kernel(scale, *refs):
    *cots, out = refs
    spots = cots[0].shape[0]
    for k, cot in enumerate(cots):
        out[pl.ds(k * spots, spots), :] = (as_row(scale) * cot[...].astype(F32)).astype(BF)


def scale_part(cots, scale):
    spots, chans = cots[0].shape
    return pl.pallas_call(
        scale_kernel,
        out_shape=shaped((len(cots) * spots, chans), BF),
        in_specs=vmem(1 + len(cots)),
        out_specs=pl.BlockSpec(memory_space=pltpu.VMEM),
        compiler_params=params(16),
        cost_estimate=cost(1, 1),
        name="scale_part",
    )(scale, *cots)


def forward_hidden(ln, up, bias, act, slope):
    hidden = up.shape[1]
    quarter = lax.axis_index("sx") * lax.axis_size("sy") + lax.axis_index("sy")
    for tile in hidden_tiles(hidden):
        columns = pl.ds(pl.multiple_of(quarter * hidden + tile.start, LANES), tile.size)
        v = jnp.dot(ln[...], up[:, tile], preferred_element_type=F32)
        v = v + bias[columns].reshape(1, tile.size)
        value, slope[:, tile] = gelu_parts(v)
        act[:, tile] = value.astype(BF)


def backward_hidden(d_mlp, down, slope, d_pre):
    for tile in hidden_tiles(down.shape[1]):
        d_act = jnp.dot(d_mlp[...], down[:, tile], preferred_element_type=F32)
        d_pre[:, tile] = (d_act * slope[:, tile]).astype(BF)


def contract_last(a, b):
    return lax.dot_general(a, b, (((1,), (1,)), ((), ())), preferred_element_type=F32)


def channel_tiles(chans):
    width = 512 if chans % 512 == 0 else LANES
    return [pl.ds(k, width) for k in range(0, chans, width)]


def write_pieces(value, tile, outs):
    first = 0
    for out in outs:
        count = out.shape[0]
        out[:, tile] = value[first : first + count].astype(BF)
        first += count


def gelu_parts(v):
    square = v * v
    th = jnp.tanh(GELU_A * (v + GELU_B * (square * v)))
    half = 0.5 + 0.5 * th
    return v * half, half + 0.5 * v * (1.0 - th * th) * (GELU_A * (1.0 + 3.0 * GELU_B * square))


def early_kernel(upper, lower, n_pieces, n_far, *refs):
    pieces, refs = refs[:n_pieces], refs[n_pieces:]
    lns, refs = refs[:n_far], refs[n_far:]
    d_mlp, pre, d_act, up, chosen, ln_last, d_mlp_last, down, ln = refs
    count = ln.shape[0]
    chans, width = chosen.shape
    n = lax.axis_size("fsdp")
    size = chans // n
    place = place_of(lax.axis_index("fsdp"), n)
    begin = pl.multiple_of(at_place(lax.rem(place + n // 2, n), n) * size, 16)
    for whole in (up, down):
        whole[pl.ds(begin, size), :] = jnp.zeros((size, whole.shape[1]), BF)
    row = lax.broadcasted_iota(jnp.int32, chosen.shape, 0)
    col = lax.broadcasted_iota(jnp.int32, chosen.shape, 1)
    chosen[...] = jnp.where((row == begin + col) & (col < size), 1.0, 0.0).astype(BF)
    copy_all(row_jobs(lns, ln) + block_jobs(pieces, upper, up) + block_jobs(pieces, lower, down))
    here = pl.ds(d_mlp.shape[0] - count, count)
    for tile in hidden_tiles(up.shape[1]):
        pre[:, tile] = jnp.dot(ln[...], up[:, tile], preferred_element_type=F32)
        d_act[:, tile] = jnp.dot(d_mlp[here, :], down[:, tile], preferred_element_type=F32)
    ln_last[...] = jnp.dot(ln[...], chosen[...], preferred_element_type=F32).astype(BF)
    d_mlp_last[...] = jnp.dot(d_mlp[here, :], chosen[...], preferred_element_type=F32).astype(BF)


def early_part(pieces, upper, lower, lns, d_mlp):
    spots, chans = lns[0].shape
    hidden = pieces[0].shape[1]
    count = spots * len(lns)
    width = -(-(chans // lax.axis_size("fsdp")) // LANES) * LANES
    outs = [shaped((count, hidden), F32)] * 2 + [shaped((chans, hidden), BF), shaped((chans, width), BF)]
    outs += [shaped((count, width), BF)] * 2
    return pl.pallas_call(
        functools.partial(early_kernel, upper, lower, len(pieces), len(lns)),
        out_shape=outs,
        in_specs=vmem(len(pieces) + len(lns) + 1),
        out_specs=vmem(len(outs)),
        scratch_shapes=[pltpu.VMEM((chans, hidden), BF), pltpu.VMEM((count, chans), BF)],
        compiler_params=params(28),
        cost_estimate=cost(4 * count * chans * hidden, 8 * count * chans),
        name="early_part",
    )(*pieces, *lns, d_mlp)


def far_kernel(up_last, down_last, pre, d_act, up, chosen, ln_last, d_mlp_last, bias, act, *refs):
    *far, up_block, down_block, d_pre = refs
    size, hidden = up_last.shape
    for block, last in ((up_block, up_last), (down_block, down_last)):
        block[pl.ds(0, size), :] = last[...]
        if block.shape[0] > size:
            block[pl.ds(size, block.shape[0] - size), :] = jnp.zeros((block.shape[0] - size, hidden), BF)
    quarter = lax.axis_index("sx") * lax.axis_size("sy") + lax.axis_index("sy")
    for tile in hidden_tiles(hidden):
        columns = pl.ds(pl.multiple_of(quarter * hidden + tile.start, LANES), tile.size)
        v = pre[:, tile] + jnp.dot(ln_last[...], up_block[:, tile], preferred_element_type=F32)
        value, slope = gelu_parts(v + bias[columns].reshape(1, tile.size))
        act[:, tile] = value.astype(BF)
        grad = d_act[:, tile] + jnp.dot(d_mlp_last[...], down_block[:, tile], preferred_element_type=F32)
        d_pre[:, tile] = (grad * slope).astype(BF)
    corner = contract_last(d_pre[...], up_block[...]).astype(BF)
    for tile in channel_tiles(up.shape[0]):
        value = contract_last(d_pre[...], up[tile, :]) + contract_last(corner, chosen[tile, :])
        write_pieces(value, tile, far)


def far_part(up_last, down_last, early, bias, n_far):
    count, hidden = early[0].shape
    chans, width = early[3].shape
    outs = [shaped((count, hidden), BF)] + [shaped((count // n_far, chans), BF)] * n_far
    return pl.pallas_call(
        far_kernel,
        out_shape=outs,
        in_specs=vmem(3 + len(early)),
        out_specs=vmem(len(outs)),
        scratch_shapes=[
            pltpu.VMEM((width, hidden), BF),
            pltpu.VMEM((width, hidden), BF),
            pltpu.VMEM((count, hidden), BF),
        ],
        compiler_params=params(20),
        cost_estimate=cost(2 * count * chans * hidden, 8 * count * chans),
        name="far_part",
    )(up_last, down_last, *early, bias)


def rest_kernel(upper, lower, n_pieces, tiles, n_near, n_mlp, *refs):
    pieces, refs = refs[:n_pieces], refs[n_pieces:]
    lns, refs = refs[:n_near], refs[n_near:]
    d_mlp, far_act, *refs = refs
    cots, refs = refs[:tiles], refs[tiles:]
    bias_up, bias, *refs = refs
    n_out = 2 * n_near - 1
    near, outs, refs = refs[:n_out], refs[n_out : n_out + n_mlp], refs[n_out + n_mlp :]
    scale_term, up, down, ln, act, slope, d_pre = refs
    spots = cots[0].shape[0]
    count = ln.shape[0]
    copy_all(row_jobs(lns, ln) + block_jobs(pieces, upper, up))
    forward_hidden(ln, up, bias_up, act.at[pl.ds(0, count)], slope)
    copy_all(block_jobs(pieces, lower, down) + [(far_act, act.at[pl.ds(count, far_act.shape[0])])])
    backward_hidden(d_mlp.at[pl.ds(0, count)], down, slope, d_pre)
    for tile in channel_tiles(up.shape[0]):
        write_pieces(contract_last(d_pre[...], up[tile, :]), tile, near)
    for tile in channel_tiles(down.shape[0]):
        value = contract_last(act[...], down[tile, :])
        write_pieces(value, tile, outs)
        total = jnp.zeros((1, tile.size), F32)
        for k, cot in enumerate(cots):
            grad = cot[:, tile].astype(F32)
            mlp = value[k * spots : (k + 1) * spots]
            if k == 0:
                mlp = mlp + bias[tile].reshape(1, tile.size)
            total = total + jnp.sum(grad * mlp, axis=0, keepdims=True)
        scale_term[:, tile] = total


def rest_part(pieces, upper, lower, lns, d_mlp, far_act, cots, bias_up, bias):
    spots, chans = lns[0].shape
    hidden = pieces[0].shape[1]
    n_near, tiles = len(lns), len(cots)
    count = spots * n_near
    group = [spots] + [spots // 2] * (2 * n_near - 2)
    groups = group * (1 + tiles // n_near)
    outs = [shaped((rows, chans), BF) for rows in groups] + [shaped((1, chans), F32)]
    return pl.pallas_call(
        functools.partial(rest_kernel, upper, lower, len(pieces), tiles, n_near, len(groups) - len(group)),
        out_shape=outs,
        in_specs=vmem(len(pieces) + n_near + tiles + 4),
        out_specs=vmem(len(outs)),
        scratch_shapes=[
            pltpu.VMEM((chans, hidden), BF),
            pltpu.VMEM((chans, hidden), BF),
            pltpu.VMEM((count, chans), BF),
            pltpu.VMEM((spots * tiles, hidden), BF),
            pltpu.VMEM((count, hidden), F32),
            pltpu.VMEM((count, hidden), BF),
        ],
        compiler_params=params(32),
        cost_estimate=cost(8 * count * chans * hidden, 10 * count * chans),
        name="rest_part",
    )(*pieces, *lns, d_mlp, far_act, *cots, bias_up, bias)


def split_refs(refs, counts):
    out = []
    for count in counts:
        out.append(refs[:count])
        refs = refs[count:]
    return out, refs


def as_lists(terms):
    terms = [term if isinstance(term, list) else [term] for term in terms]
    return terms, [len(term) for term in terms], [part for term in terms for part in term]


def add_kernel(counts, *refs):
    terms, outs = split_refs(refs, counts)
    step, base = 16, 0
    for out in outs:
        for first in range(0, out.shape[0], step):
            value = add_up([rows_of(term, base + first, step) for term in terms])
            out[pl.ds(first, step), :] = value.astype(BF)
        base += out.shape[0]


def add_rounded(terms, sizes):
    terms, counts, parts = as_lists(terms)
    chans = terms[0][0].shape[1]
    return pl.pallas_call(
        functools.partial(add_kernel, counts),
        out_shape=[shaped((size, chans), BF) for size in sizes],
        in_specs=vmem(len(parts)),
        out_specs=vmem(len(sizes)),
        compiler_params=params(16),
        cost_estimate=cost(1, 1),
        name="add_rounded",
    )(*parts)


def add_pairs_kernel(*refs):
    *terms, out = refs
    values = [term[...].astype(F32) for term in terms]
    while len(values) > 1:
        values = [values[k] + values[k + 1] for k in range(0, len(values), 2)]
    out[...] = values[0].astype(out.dtype)


def add_pairs(terms, dtype):
    return pl.pallas_call(
        add_pairs_kernel,
        out_shape=shaped(terms[0].shape, dtype),
        in_specs=vmem(len(terms)),
        out_specs=pl.BlockSpec(memory_space=pltpu.VMEM),
        compiler_params=params(16),
        cost_estimate=cost(1, 1),
        name="add_pairs",
    )(*terms)


def output_kernel(counts, scaled, scale, bias, *refs):
    terms, (out,) = split_refs(refs, counts)
    rows, cols = out.shape[:2]
    for r in range(rows):
        mlp = add_up([rows_of(term, r * cols, cols) for term in terms]) + as_row(bias)
        out[r] = (scaled[r].astype(F32) + as_row(scale) * mlp).astype(BF)


def output_part(scaled, scale, bias, terms):
    terms, counts, parts = as_lists(terms)
    return pl.pallas_call(
        functools.partial(output_kernel, counts),
        out_shape=shaped(scaled.shape, BF),
        in_specs=vmem(3 + len(parts)),
        out_specs=pl.BlockSpec(memory_space=pltpu.VMEM),
        compiler_params=params(16),
        cost_estimate=cost(1, 1),
        name="output_part",
    )(scaled, scale, bias, *parts)


def quarters_kernel(keep, got, *parts):
    rows = parts[0].shape[0]
    me = 2 * (lax.axis_index("sy") % 2) + lax.axis_index("fsdp") % 2
    for k, part in enumerate(parts):
        here = pl.ds(pl.multiple_of((me ^ k) * rows, rows), rows)
        part[...] = (keep[here, :] + got[here, :]).astype(part.dtype)


def quarters(keep, got):
    rows, chans = keep.shape
    return pl.pallas_call(
        quarters_kernel,
        out_shape=[shaped((rows // 4, chans), BF if k else F32) for k in range(4)],
        in_specs=vmem(2),
        out_specs=vmem(4),
        compiler_params=params(16),
        cost_estimate=cost(rows * chans, 12 * rows * chans),
        name="quarters",
    )(keep, got)


def finish_kernel(*refs):
    mine, other = refs[:4], refs[4:8]
    grad_kernel, grad_gain, grad_scale, sums = refs[8:]
    core = lax.axis_index("sx") % 2
    me = 2 * (lax.axis_index("sy") % 2) + lax.axis_index("fsdp") % 2
    for k in range(4):
        sums[core, me ^ k] = mine[k][...]
        sums[1 - core, me ^ k] = other[k][...]
    rows = mine[0].shape[0]

    def row(t):
        return sums[t // (4 * rows), t // rows % 4, pl.ds(t % rows, 1), :]

    for i in range(KW):
        for j in range(KW):
            grad_kernel[i, pl.ds(j, 1), :] = row(i * KW + j)
    grad_gain[...] = row(KW * KW).reshape(grad_gain.shape)
    grad_scale[...] = row(KW * KW + 1).reshape(grad_scale.shape)


def finish(mine, other):
    rows, chans = mine[0].shape
    return pl.pallas_call(
        finish_kernel,
        out_shape=(shaped((KW, KW, chans), F32), shaped((chans,), F32), shaped((chans,), F32)),
        in_specs=vmem(8),
        out_specs=vmem(3),
        scratch_shapes=[pltpu.VMEM((2, 4, rows, chans), F32)],
        compiler_params=params(16),
        cost_estimate=cost(rows, 16 * rows * chans),
        name="finish",
    )(*mine, *other)


def on_device(
    x_code,
    x_exp,
    dw_kernel,
    dw_bias,
    ln_gain,
    ln_bias,
    w_up,
    b_up,
    w_down,
    b_down,
    layer_scale,
    cotangent,
):
    rows, cols, chans = x_code.shape[1:]
    spots = rows * cols
    n_near = lax.axis_size("sx")
    tiles = n_near * lax.axis_size("sy")
    quarter = lax.axis_index("sx") * lax.axis_size("sy") + lax.axis_index("sy")
    hidden = w_up.shape[1] // tiles
    up_block = lax.dynamic_slice_in_dim(w_up, quarter * hidden, hidden, 1)
    down_block = lax.dynamic_slice_in_dim(w_down, quarter * hidden, hidden, 0).T
    scaled, *edges = prepare(x_code[0], x_exp[0])
    edges = list(exchange_edges(dict(zip(edge_keys(), edges, strict=True))).values())
    cots = gather_tile(after(cotangent.reshape(spots, chans), edges))
    d_mlp = scale_part(cots, layer_scale)
    padded, normed, rstd, ln_out = conv_norm(scaled, edges, dw_kernel, dw_bias, ln_gain, ln_bias)
    blocks = jnp.concatenate([up_block, down_block], 0)
    pieces, upper, lower = ring_gather(blocks, edges, ln_out, d_mlp)
    lns = gather_tile(ln_out)
    early = early_part(pieces[:-2], upper[:-1], lower[:-1], lns[n_near:], d_mlp)
    far_act, *far = far_part(*pieces[-2:], early, b_up, tiles - n_near)

    far = [far[k : k + n_near] for k in range(0, len(far), n_near)]
    far = [add_rounded(reduce_cores(group), [spots])[0] for group in far]
    d_mlp, far = lax.optimization_barrier((d_mlp, far))
    far = [shift(term, "sy", -(t + 1)) for t, term in enumerate(far)]
    *rest, scale_term = rest_part(pieces, upper, lower, lns[:n_near], d_mlp, far_act, cots, b_up, b_down)
    size = 2 * n_near - 1
    near, *mlp = [reduce_cores_halves(rest[k : k + size]) for k in range(0, len(rest), size)]
    mlp_far = [add_rounded(group, [spots - spots // 4, spots // 4]) for group in mlp[1:]]
    far, mlp_far, mlp_near = lax.optimization_barrier((far, mlp_far, mlp[0]))
    first_parts = [shift(term[0], "sy", -(t + 1)) for t, term in enumerate(mlp_far)]
    d_conv, keep, send, *edges = norm_back(near + far, normed, rstd, ln_gain, padded, scale_term)
    send, first_parts = lax.optimization_barrier((swap(send, sx=1), first_parts))
    parts = quarters(keep, send)
    edges = list(exchange_edges(dict(zip(edge_keys(), edges, strict=True))).values())
    cut = [0, chans // LANES // 2 * LANES, chans]

    def back(k, before):
        return conv_back(d_conv, edges, dw_kernel, cotangent[0], cut[k], cut[k + 1] - cut[k], before)

    grad_input = back(0, None)
    total, grad_input = lax.optimization_barrier((sum_quarters(parts, BF), grad_input))
    second_parts = [shift(after(term[1], total), "sy", -(t + 1)) for t, term in enumerate(mlp_far)]
    total = sum_others(total)
    grad_input = back(1, grad_input)
    total, grad_input, second_parts = lax.optimization_barrier((total, grad_input, second_parts))
    mlp_far = [list(term) for term in zip(first_parts, second_parts, strict=True)]
    block_out = output_part(scaled, layer_scale, b_down, mlp_near + mlp_far)
    grad_kernel, grad_gain, grad_scale = finish(*spread_quarter(total))
    return (block_out[None], grad_input[None], grad_kernel, grad_gain, grad_scale)


def solution(mesh):
    placed = (
        P("fsdp", "sx", "sy", None),
        P("fsdp", "sx", "sy", None),
        P(),
        P(),
        P(),
        P(),
        P("fsdp", None),
        P(),
        P(None, "fsdp"),
        P(),
        P(),
        P("fsdp", "sx", "sy", None),
    )
    return jax.shard_map(
        on_device,
        mesh=mesh,
        in_specs=placed,
        out_specs=(P("fsdp", "sx", "sy", None), P("fsdp", "sx", "sy", None), P(), P(), P()),
        check_vma=False,
    )
```

```python
import functools

import jax
import jax.numpy as jnp
from jax import lax
from jax.experimental import pallas as pl
from jax.experimental.pallas import tpu as pltpu
from jax.sharding import PartitionSpec as P

CG = 128
KW = 7
HALO = 3
LANES = 128
SUBLANES = 8
FIRST_COL = 8
BF = jnp.bfloat16
F32 = jnp.float32
MIB = 1024 * 1024
GELU_A = 0.7978845608028654
GELU_B = 0.044715


def vmem(count):
    return [pl.BlockSpec(memory_space=pltpu.VMEM)] * count


def anywhere(count):
    return [pl.BlockSpec(memory_space=pl.ANY)] * count


def params(mib):
    return pltpu.CompilerParams(vmem_limit_bytes=mib * MIB)


def cost(flops, moved, special=0):
    return pl.CostEstimate(flops=1, bytes_accessed=1, transcendentals=0)


def shaped(shape, dtype):
    return jax.ShapeDtypeStruct(tuple(shape), dtype)


def swap(a, **masks):
    axes = tuple(masks)
    mask = 0
    total = 1
    for axis in axes:
        n = lax.axis_size(axis)
        mask, total = mask * n + masks[axis], total * n
    return lax.ppermute(a, axes, [(i, i ^ mask) for i in range(total)])


def shift(a, axis, k):
    n = lax.axis_size(axis)
    return lax.ppermute(a, axis, [((i + k) % n, i) for i in range(n)])


def sides(axis):
    return (0,) if lax.axis_size(axis) == 2 else (-1, 1)


def side_pairs(n, side):
    if side == 0:
        return [(0, 1), (1, 0)]
    return [(i, i - side) for i in range(n) if 0 <= i - side < n]


def exchange_edges(pieces):
    n, m = lax.axis_size("sx"), lax.axis_size("sy")
    got = {}
    for (a, b), piece in pieces.items():
        rows = [(i, i) for i in range(n)] if a is None else side_pairs(n, a)
        cols = [(j, j) for j in range(m)] if b is None else side_pairs(m, b)
        pairs = [(i * m + j, k * m + l) for i, k in rows for j, l in cols]
        got[a, b] = lax.ppermute(piece, ("sx", "sy"), pairs)
    return got


def edge_keys():
    rows, cols = sides("sx"), sides("sy")
    return [(a, None) for a in rows] + [(None, b) for b in cols] + [(a, b) for a in rows for b in cols]


def place_of(index, n):
    if n != 8:
        return index
    return jnp.where(index % 2 == 0, index // 2, 7 - index // 2)


def at_place(place, n):
    if n != 8:
        return place
    return jnp.where(place < 4, 2 * place, 15 - 2 * place)


def ring_pairs(n):
    order = [0, 2, 4, 6, 7, 5, 3, 1] if n == 8 else list(range(n))
    forth = [(order[k], order[(k + 1) % n]) for k in range(n)]
    return forth, [(d, s) for s, d in forth]


def after(value, others):
    return lax.optimization_barrier((value, others))[0]


def ring_gather(block, second_after, third_after, last_after):
    n, rows = lax.axis_size("fsdp"), block.shape[0] // 2
    forth, back = ring_pairs(n)
    pieces, upper, lower = [block], [(0, 0, 0)], [(0, rows, 0)]
    one = two = block
    for k in range(1, (n + 1) // 2):
        if k in (2, 3):
            one, two = after([one, two], second_after if k == 2 else third_after)
        one = lax.ppermute(one, "fsdp", forth)
        two = lax.ppermute(two, "fsdp", back)
        for piece, distance in ((one, -k), (two, k)):
            upper.append((len(pieces), 0, distance))
            lower.append((len(pieces), rows, distance))
            pieces.append(piece)
    if n % 2 == 0:
        one, two = after([one[:rows], two[rows:]], last_after)
        upper.append((len(pieces), 0, n // 2))
        lower.append((len(pieces) + 1, 0, n // 2))
        pieces += [lax.ppermute(one, "fsdp", forth), lax.ppermute(two, "fsdp", back)]
    return pieces, upper, lower


def gather_tile(a, own_after):
    out = []
    for t in range(lax.axis_size("sy")):
        mine = a if t == 0 else after(shift(a, "sy", t), out[-1])
        sent = after(a, own_after) if t == 0 else mine
        out.append([mine] + [shift(sent, "sx", s) for s in range(1, lax.axis_size("sx"))])
    return [piece for group in out for piece in group]


def reduce_cores(pieces):
    return [pieces[0]] + [shift(pieces[s], "sx", -s) for s in range(1, len(pieces))]


def reduce_cores_halves(pieces):
    got = [shift(piece, "sx", -(1 + k // 2)) for k, piece in enumerate(pieces[1:])]
    return [pieces[0]] + [got[k : k + 2] for k in range(0, len(got), 2)]


def add_up(terms):
    total = terms[0].astype(F32)
    for term in terms[1:]:
        total = total + term.astype(F32)
    return total


def sum_quarters(parts, dtype):
    terms = [parts[0], swap(parts[1], fsdp=1), swap(parts[2], sy=1), swap(parts[3], sy=1, fsdp=1)]
    return add_pairs(terms, dtype)


def sum_others(rounded):
    masks = []
    for axis in ("sx", "sy", "fsdp"):
        bit = 2
        while bit < lax.axis_size(axis):
            masks.append((axis, bit))
            bit *= 2
    while masks:
        group, masks = masks[:2], masks[2:]
        (axis, bit) = group[0]
        terms = [rounded, swap(rounded, **{axis: bit})]
        if len(group) == 2:
            (other, more) = group[1]
            both = {axis: bit + more} if axis == other else {axis: bit, other: more}
            terms += [swap(rounded, **{other: more}), swap(rounded, **both)]
        rounded = add_pairs(terms, BF if masks else F32)
    return rounded


def spread_quarter(total):
    mine = [total, swap(total, fsdp=1), swap(total, sy=1), swap(total, sy=1, fsdp=1)]
    return mine, [swap(piece, sx=1) for piece in mine]


def as_row(ref):
    return ref[...].reshape(1, ref.shape[0])


def write_edges(tile, refs):
    rows, cols = tile.shape[:2]
    for (a, b), ref in zip(edge_keys(), refs, strict=True):
        if a is None:
            value = tile[...]
        elif a == 0:
            first = jnp.where(lax.axis_index("sx") == 0, rows - HALO, 0)
            value = tile[pl.ds(first, HALO)]
        else:
            value = tile[pl.ds(0 if a > 0 else rows - HALO, HALO)]
        if b == 0:
            low, high = value[:, :HALO], value[:, cols - HALO :]
            value = jnp.where(lax.axis_index("sy") == 0, high, low)
        elif b is not None:
            value = value[:, :HALO] if b > 0 else value[:, cols - HALO :]
        ref[...] = value.astype(BF)


def edge_shapes(rows, cols, chans):
    return [shaped((rows if a is None else HALO, cols if b is None else HALO, chans), BF) for a, b in edge_keys()]


def fill_padded(own, refs, padded, lanes=slice(None)):
    rows, cols = own.shape[:2]
    row_at = {-1: 0, None: HALO, 1: HALO + rows}
    col_at = {-1: FIRST_COL - HALO, None: FIRST_COL, 1: FIRST_COL + cols}
    sx, sy = lax.axis_index("sx"), lax.axis_index("sy")
    there = {("sx", -1): sx > 0, ("sx", 1): sx < lax.axis_size("sx") - 1}
    there |= {("sy", -1): sy > 0, ("sy", 1): sy < lax.axis_size("sy") - 1}
    padded[pl.ds(HALO, rows), pl.ds(FIRST_COL, cols), :] = own[:, :, lanes].astype(F32)
    for (a, b), ref in zip(edge_keys(), refs, strict=True):
        value = ref[:, :, lanes].astype(F32)
        for i in (-1, 1) if a == 0 else (a,):
            for j in (-1, 1) if b == 0 else (b,):
                on = jnp.float32(1)
                if i is not None:
                    on = on * there["sx", i].astype(F32)
                if j is not None:
                    on = on * there["sy", j].astype(F32)
                spot = (pl.ds(row_at[i], ref.shape[0]), pl.ds(col_at[j], ref.shape[1]))
                padded[spot[0], spot[1], :] = value * on


def prepare_kernel(code, expo, scaled, *edges):
    rows, cols, chans = code.shape
    for r in range(rows):
        e = expo[r]
        up = jnp.left_shift(1, jnp.maximum(e, 0)).astype(F32)
        down = jnp.left_shift(1, jnp.maximum(-e, 0)).astype(F32)
        factor = jnp.where(e >= 0, up, 1.0 / down)
        for g in range(chans // CG):
            lanes = pl.ds(g * CG, CG)
            scaled[r, :, lanes] = (code[r, :, lanes].astype(F32) * factor[:, g : g + 1]).astype(BF)
    write_edges(scaled, edges)


def prepare(code, expo):
    rows, cols, chans = code.shape
    outs = [shaped(code.shape, BF)] + edge_shapes(rows, cols, chans)
    return pl.pallas_call(
        prepare_kernel,
        out_shape=outs,
        in_specs=vmem(2),
        out_specs=vmem(len(outs)),
        compiler_params=params(16),
        cost_estimate=cost(code.size, 8 * code.size),
        name="prepare",
    )(code, expo)


def convolve(padded, weights, start, put, rows, cols, chans, flip):
    parts = range(cols // SUBLANES)

    def group(g, carry):
        lanes = pl.ds(pl.multiple_of(g * LANES, LANES), LANES)
        acc = [[start(lanes, r, k) for k in parts] for r in range(rows)]
        for j in range(KW):
            taps = []
            for i in range(KW):
                at = (KW - 1 - i) * KW + (KW - 1 - j) if flip else i * KW + j
                taps.append(weights[at, :, lanes])
            for p in range(rows + 2 * HALO):
                for k in parts:
                    piece = padded[p, pl.ds(FIRST_COL - HALO + j + k * SUBLANES, SUBLANES), lanes]
                    for i in range(KW):
                        if 0 <= p - i < rows:
                            acc[p - i][k] = acc[p - i][k] + taps[i] * piece
        for r in range(rows):
            for k in parts:
                put(lanes, r, k, acc[r][k])
        return carry

    lax.fori_loop(0, chans // LANES, group, 0)


def spread_taps(weights, wide, lanes):
    for i in range(KW):
        for j in range(KW):
            row = weights[i, pl.ds(j, 1), lanes]
            wide[i * KW + j] = jnp.broadcast_to(row, wide.shape[1:])


def conv_norm_kernel(own, *refs):
    count = len(edge_keys())
    edges, refs = refs[:count], refs[count:]
    weights, bias, gain, shift_, padded, normed, rstd, out, wide, conv, sems, *edges_in = refs
    rows, cols, chans = own.shape
    copies = start_copies(list(zip(edges, edges_in, strict=True)), sems, 0)
    wait_all(copies)
    fill_padded(own, edges_in, padded)
    spread_taps(weights, wide, slice(None))

    def start(lanes, r, k):
        return jnp.broadcast_to(bias[lanes].reshape(1, LANES), (SUBLANES, LANES))

    def put(lanes, r, k, value):
        conv[pl.ds(r * cols + k * SUBLANES, SUBLANES), lanes] = value

    convolve(padded, wide, start, put, rows, cols, chans, False)
    for r in range(rows):
        here = pl.ds(r * cols, cols)
        value = conv[here, :]
        centred = value - jnp.mean(value, axis=-1, keepdims=True)
        scale = lax.rsqrt(jnp.mean(centred * centred, axis=-1, keepdims=True) + 1e-06)
        unit = centred * scale
        normed[here, :] = unit
        rstd[here, :] = jnp.broadcast_to(scale, (cols, LANES))
        out[here, :] = (unit * as_row(gain) + as_row(shift_)).astype(BF)


def conv_norm(own, edges, weights, bias, gain, shift_):
    rows, cols, chans = own.shape
    spots = rows * cols
    return pl.pallas_call(
        conv_norm_kernel,
        out_shape=(
            shaped((rows + 2 * HALO, cols + 16, chans), F32),
            shaped((spots, chans), F32),
            shaped((spots, LANES), F32),
            shaped((spots, chans), BF),
        ),
        in_specs=vmem(1) + anywhere(len(edges)) + vmem(4),
        out_specs=vmem(4),
        scratch_shapes=[
            pltpu.VMEM((KW * KW, SUBLANES, chans), F32),
            pltpu.VMEM((spots, chans), F32),
            pltpu.SemaphoreType.DMA((len(edges),)),
        ]
        + [pltpu.VMEM(edge.shape, BF) for edge in edges],
        compiler_params=params(20),
        cost_estimate=cost(2 * KW * KW * spots * chans, 10 * spots * chans),
        name="conv_norm",
    )(own, *edges, weights, bias, gain, shift_)


def rows_of(refs, first, count):
    for ref in refs:
        if first < ref.shape[0]:
            return ref[pl.ds(first, count), :]
        first -= ref.shape[0]


def norm_back_kernel(counts, *refs):
    terms, refs = split_refs(refs, counts)
    normed, rstd, gain, padded, scale_term, d_conv, keep, send, *edges, sums = refs
    rows, cols = d_conv.shape[:2]
    chans = normed.shape[-1]
    gain_sum = jnp.zeros((SUBLANES, chans), F32)
    for r in range(rows):
        here = pl.ds(r * cols, cols)
        d_ln = add_up([rows_of(term, r * cols, cols) for term in terms])
        unit = normed[here, :]
        d_unit = d_ln * unit
        for k in range(0, cols, SUBLANES):
            gain_sum = gain_sum + d_unit[k : k + SUBLANES]
        d_norm = d_ln * as_row(gain)
        mean_one = jnp.mean(d_norm, axis=-1, keepdims=True)
        mean_two = jnp.mean(d_unit * as_row(gain), axis=-1, keepdims=True)
        d_conv[r] = rstd[here, :1] * (d_norm - mean_one - unit * mean_two)
    write_edges(d_conv, edges)
    taps = KW * KW
    half = keep.shape[0]

    def store(row, lanes, value):
        sums[row // half, pl.ds(row % half, 1), lanes] = value

    for row in range(taps + 2, 2 * half):
        store(row, slice(None), jnp.zeros((1, chans), F32))
    store(taps, slice(None), jnp.sum(gain_sum, axis=0, keepdims=True))
    store(taps + 1, slice(None), scale_term[...])
    parts = range(cols // SUBLANES)

    def group(g, carry):
        lanes = pl.ds(pl.multiple_of(g * LANES, LANES), LANES)
        grads = [[d_conv[r, pl.ds(k * SUBLANES, SUBLANES), lanes] for k in parts] for r in range(rows)]
        for j in range(KW):
            acc = [jnp.zeros((SUBLANES, LANES), F32) for _ in range(KW)]
            for p in range(rows + 2 * HALO):
                for k in parts:
                    piece = padded[p, pl.ds(FIRST_COL - HALO + j + k * SUBLANES, SUBLANES), lanes]
                    for i in range(KW):
                        if 0 <= p - i < rows:
                            acc[i] = acc[i] + grads[p - i][k] * piece
            for i in range(KW):
                store(i * KW + j, lanes, jnp.sum(acc[i], axis=0, keepdims=True))
        return carry

    lax.fori_loop(0, chans // LANES, group, 0)
    core = lax.axis_index("sx") % 2
    keep[...] = sums[core]
    send[...] = sums[1 - core]


def norm_back(terms, normed, rstd, gain, padded, scale_term):
    spots, chans = normed.shape
    rows = padded.shape[0] - 2 * HALO
    cols = spots // rows
    half = -(-(KW * KW + 2) // 64) * 32
    outs = [shaped((rows, cols, chans), F32), shaped((half, chans), F32), shaped((half, chans), F32)]
    outs += edge_shapes(rows, cols, chans)
    terms, counts, parts = as_lists(terms)
    return pl.pallas_call(
        functools.partial(norm_back_kernel, counts),
        out_shape=outs,
        in_specs=vmem(5 + len(parts)),
        out_specs=vmem(len(outs)),
        scratch_shapes=[pltpu.VMEM((2, half, chans), F32)],
        compiler_params=params(20),
        cost_estimate=cost(2 * KW * KW * spots * chans, 16 * spots * chans),
        name="norm_back",
    )(*parts, normed, rstd, gain, padded, scale_term)


def conv_back_kernel(begin, count, own, *refs):
    edges, refs = refs[: len(edge_keys())], refs[len(edge_keys()) :]
    weights, cotangent, *_, out, padded, wide, part, sem = refs
    rows, cols = own.shape[:2]
    mine = pl.ds(begin, count)
    fill_padded(own, edges, padded, mine)
    spread_taps(weights, wide, mine)

    def start(lanes, r, k):
        here = pl.ds(pl.multiple_of(lanes.start + begin, LANES), LANES)
        return cotangent[r, pl.ds(k * SUBLANES, SUBLANES), here].astype(F32)

    def put(lanes, r, k, value):
        part[r, pl.ds(k * SUBLANES, SUBLANES), lanes] = value.astype(BF)

    convolve(padded, wide, start, put, rows, cols, count, True)
    copy = pltpu.make_async_copy(part, out.at[:, :, mine], sem)
    copy.start()
    copy.wait()


def conv_back(own, edges, weights, cotangent, begin, count, before):
    rows, cols, chans = own.shape
    extra = [] if before is None else [before]
    given = 3 + len(edges)
    return pl.pallas_call(
        functools.partial(conv_back_kernel, begin, count),
        out_shape=shaped((rows, cols, chans), BF),
        in_specs=vmem(given) + anywhere(len(extra)),
        out_specs=pl.BlockSpec(memory_space=pl.ANY),
        scratch_shapes=[
            pltpu.VMEM((rows + 2 * HALO, cols + 16, count), F32),
            pltpu.VMEM((KW * KW, SUBLANES, count), F32),
            pltpu.VMEM((rows, cols, count), BF),
            pltpu.SemaphoreType.DMA,
        ],
        input_output_aliases={given: 0} if extra else {},
        compiler_params=params(16),
        cost_estimate=cost(2 * KW * KW * rows * cols * count, 10 * rows * cols * count),
        name="conv_back",
    )(own, *edges, weights, cotangent, *extra)


def start_copies(jobs, sems, first):
    copies = []
    for k, (src, dst) in enumerate(jobs):
        copies.append(pltpu.make_async_copy(src, dst, sems.at[first + k]))
        copies[-1].start()
    return copies


def wait_all(copies):
    for copy in copies:
        copy.wait()


def copy_all(jobs):
    for src, dst in jobs:
        dst[...] = src[...]


def block_jobs(pieces, spots, whole):
    n = lax.axis_size("fsdp")
    rows = whole.shape[0] // n
    place = place_of(lax.axis_index("fsdp"), n)
    jobs = []
    for index, first, distance in spots:
        owner = at_place(lax.rem(place + (distance + n), n), n)
        begin = pl.multiple_of(owner * rows, 16)
        jobs.append((pieces[index].at[pl.ds(first, rows)], whole.at[pl.ds(begin, rows)]))
    return jobs


def row_jobs(pieces, whole):
    count = whole.shape[0] // len(pieces)
    return [(piece, whole.at[pl.ds(k * count, count)]) for k, piece in enumerate(pieces)]


def hidden_tiles(hidden):
    width = 256 if hidden % 256 == 0 else LANES
    return [pl.ds(k, width) for k in range(0, hidden, width)]


def scale_kernel(scale, *refs):
    *cots, out = refs
    spots = cots[0].shape[0]
    for k, cot in enumerate(cots):
        out[pl.ds(k * spots, spots), :] = (as_row(scale) * cot[...].astype(F32)).astype(BF)


def scale_part(cots, scale):
    spots, chans = cots[0].shape
    return pl.pallas_call(
        scale_kernel,
        out_shape=shaped((len(cots) * spots, chans), BF),
        in_specs=vmem(1 + len(cots)),
        out_specs=pl.BlockSpec(memory_space=pltpu.VMEM),
        compiler_params=params(16),
        cost_estimate=cost(1, 1),
        name="scale_part",
    )(scale, *cots)


def forward_hidden(ln, up, bias, act, slope):
    hidden = up.shape[1]
    quarter = lax.axis_index("sx") * lax.axis_size("sy") + lax.axis_index("sy")
    for tile in hidden_tiles(hidden):
        columns = pl.ds(pl.multiple_of(quarter * hidden + tile.start, LANES), tile.size)
        v = jnp.dot(ln[...], up[:, tile], preferred_element_type=F32)
        v = v + bias[columns].reshape(1, tile.size)
        value, slope[:, tile] = gelu_parts(v)
        act[:, tile] = value.astype(BF)


def backward_hidden(d_mlp, down, slope, d_pre):
    for tile in hidden_tiles(down.shape[1]):
        d_act = jnp.dot(d_mlp[...], down[:, tile], preferred_element_type=F32)
        d_pre[:, tile] = (d_act * slope[:, tile]).astype(BF)


def contract_last(a, b):
    return lax.dot_general(a, b, (((1,), (1,)), ((), ())), preferred_element_type=F32)


def channel_tiles(chans):
    width = 512 if chans % 512 == 0 else LANES
    return [pl.ds(k, width) for k in range(0, chans, width)]


def write_pieces(value, tile, outs):
    first = 0
    for out in outs:
        count = out.shape[0]
        out[:, tile] = value[first : first + count].astype(BF)
        first += count


def gelu_parts(v):
    square = v * v
    th = jnp.tanh(GELU_A * (v + GELU_B * (square * v)))
    half = 0.5 + 0.5 * th
    return v * half, half + 0.5 * v * (1.0 - th * th) * (GELU_A * (1.0 + 3.0 * GELU_B * square))


def early_kernel(upper, lower, n_pieces, n_far, *refs):
    pieces, refs = refs[:n_pieces], refs[n_pieces:]
    lns, refs = refs[:n_far], refs[n_far:]
    d_mlp, pre, d_act, up, chosen, ln_last, d_mlp_last, down, ln = refs
    count = ln.shape[0]
    chans, width = chosen.shape
    n = lax.axis_size("fsdp")
    size = chans // n
    place = place_of(lax.axis_index("fsdp"), n)
    begin = pl.multiple_of(at_place(lax.rem(place + n // 2, n), n) * size, 16)
    for whole in (up, down):
        whole[pl.ds(begin, size), :] = jnp.zeros((size, whole.shape[1]), BF)
    row = lax.broadcasted_iota(jnp.int32, chosen.shape, 0)
    col = lax.broadcasted_iota(jnp.int32, chosen.shape, 1)
    chosen[...] = jnp.where((row == begin + col) & (col < size), 1.0, 0.0).astype(BF)
    copy_all(row_jobs(lns, ln) + block_jobs(pieces, upper, up) + block_jobs(pieces, lower, down))
    here = pl.ds(d_mlp.shape[0] - count, count)
    for tile in hidden_tiles(up.shape[1]):
        pre[:, tile] = jnp.dot(ln[...], up[:, tile], preferred_element_type=F32)
        d_act[:, tile] = jnp.dot(d_mlp[here, :], down[:, tile], preferred_element_type=F32)
    ln_last[...] = jnp.dot(ln[...], chosen[...], preferred_element_type=F32).astype(BF)
    d_mlp_last[...] = jnp.dot(d_mlp[here, :], chosen[...], preferred_element_type=F32).astype(BF)


def early_part(pieces, upper, lower, lns, d_mlp):
    spots, chans = lns[0].shape
    hidden = pieces[0].shape[1]
    count = spots * len(lns)
    width = -(-(chans // lax.axis_size("fsdp")) // LANES) * LANES
    outs = [shaped((count, hidden), F32)] * 2 + [shaped((chans, hidden), BF), shaped((chans, width), BF)]
    outs += [shaped((count, width), BF)] * 2
    return pl.pallas_call(
        functools.partial(early_kernel, upper, lower, len(pieces), len(lns)),
        out_shape=outs,
        in_specs=vmem(len(pieces) + len(lns) + 1),
        out_specs=vmem(len(outs)),
        scratch_shapes=[pltpu.VMEM((chans, hidden), BF), pltpu.VMEM((count, chans), BF)],
        compiler_params=params(28),
        cost_estimate=cost(4 * count * chans * hidden, 8 * count * chans),
        name="early_part",
    )(*pieces, *lns, d_mlp)


def far_kernel(up_last, down_last, pre, d_act, up, chosen, ln_last, d_mlp_last, bias, act, *refs):
    *far, up_block, down_block, d_pre = refs
    size, hidden = up_last.shape
    for block, last in ((up_block, up_last), (down_block, down_last)):
        block[pl.ds(0, size), :] = last[...]
        if block.shape[0] > size:
            block[pl.ds(size, block.shape[0] - size), :] = jnp.zeros((block.shape[0] - size, hidden), BF)
    quarter = lax.axis_index("sx") * lax.axis_size("sy") + lax.axis_index("sy")
    for tile in hidden_tiles(hidden):
        columns = pl.ds(pl.multiple_of(quarter * hidden + tile.start, LANES), tile.size)
        v = pre[:, tile] + jnp.dot(ln_last[...], up_block[:, tile], preferred_element_type=F32)
        value, slope = gelu_parts(v + bias[columns].reshape(1, tile.size))
        act[:, tile] = value.astype(BF)
        grad = d_act[:, tile] + jnp.dot(d_mlp_last[...], down_block[:, tile], preferred_element_type=F32)
        d_pre[:, tile] = (grad * slope).astype(BF)
    corner = contract_last(d_pre[...], up_block[...]).astype(BF)
    for tile in channel_tiles(up.shape[0]):
        value = contract_last(d_pre[...], up[tile, :]) + contract_last(corner, chosen[tile, :])
        write_pieces(value, tile, far)


def far_part(up_last, down_last, early, bias, n_far):
    count, hidden = early[0].shape
    chans, width = early[3].shape
    outs = [shaped((count, hidden), BF)] + [shaped((count // n_far, chans), BF)] * n_far
    return pl.pallas_call(
        far_kernel,
        out_shape=outs,
        in_specs=vmem(3 + len(early)),
        out_specs=vmem(len(outs)),
        scratch_shapes=[
            pltpu.VMEM((width, hidden), BF),
            pltpu.VMEM((width, hidden), BF),
            pltpu.VMEM((count, hidden), BF),
        ],
        compiler_params=params(20),
        cost_estimate=cost(2 * count * chans * hidden, 8 * count * chans),
        name="far_part",
    )(up_last, down_last, *early, bias)


def rest_kernel(upper, lower, n_pieces, tiles, n_near, n_mlp, *refs):
    pieces, refs = refs[:n_pieces], refs[n_pieces:]
    lns, refs = refs[:n_near], refs[n_near:]
    d_mlp, far_act, *refs = refs
    cots, refs = refs[:tiles], refs[tiles:]
    bias_up, bias, *refs = refs
    n_out = 2 * n_near - 1
    near, outs, refs = refs[:n_out], refs[n_out : n_out + n_mlp], refs[n_out + n_mlp :]
    scale_term, up, down, ln, act, slope, d_pre = refs
    spots = cots[0].shape[0]
    count = ln.shape[0]
    copy_all(row_jobs(lns, ln) + block_jobs(pieces, upper, up))
    forward_hidden(ln, up, bias_up, act.at[pl.ds(0, count)], slope)
    copy_all(block_jobs(pieces, lower, down) + [(far_act, act.at[pl.ds(count, far_act.shape[0])])])
    backward_hidden(d_mlp.at[pl.ds(0, count)], down, slope, d_pre)
    for tile in channel_tiles(up.shape[0]):
        write_pieces(contract_last(d_pre[...], up[tile, :]), tile, near)
    for tile in channel_tiles(down.shape[0]):
        value = contract_last(act[...], down[tile, :])
        write_pieces(value, tile, outs)
        total = jnp.zeros((1, tile.size), F32)
        for k, cot in enumerate(cots):
            grad = cot[:, tile].astype(F32)
            mlp = value[k * spots : (k + 1) * spots]
            if k == 0:
                mlp = mlp + bias[tile].reshape(1, tile.size)
            total = total + jnp.sum(grad * mlp, axis=0, keepdims=True)
        scale_term[:, tile] = total


def rest_part(pieces, upper, lower, lns, d_mlp, far_act, cots, bias_up, bias):
    spots, chans = lns[0].shape
    hidden = pieces[0].shape[1]
    n_near, tiles = len(lns), len(cots)
    count = spots * n_near
    group = [spots] + [spots // 2] * (2 * n_near - 2)
    groups = group * (1 + tiles // n_near)
    outs = [shaped((rows, chans), BF) for rows in groups] + [shaped((1, chans), F32)]
    return pl.pallas_call(
        functools.partial(rest_kernel, upper, lower, len(pieces), tiles, n_near, len(groups) - len(group)),
        out_shape=outs,
        in_specs=vmem(len(pieces) + n_near + tiles + 4),
        out_specs=vmem(len(outs)),
        scratch_shapes=[
            pltpu.VMEM((chans, hidden), BF),
            pltpu.VMEM((chans, hidden), BF),
            pltpu.VMEM((count, chans), BF),
            pltpu.VMEM((spots * tiles, hidden), BF),
            pltpu.VMEM((count, hidden), F32),
            pltpu.VMEM((count, hidden), BF),
        ],
        compiler_params=params(32),
        cost_estimate=cost(8 * count * chans * hidden, 10 * count * chans),
        name="rest_part",
    )(*pieces, *lns, d_mlp, far_act, *cots, bias_up, bias)


def split_refs(refs, counts):
    out = []
    for count in counts:
        out.append(refs[:count])
        refs = refs[count:]
    return out, refs


def as_lists(terms):
    terms = [term if isinstance(term, list) else [term] for term in terms]
    return terms, [len(term) for term in terms], [part for term in terms for part in term]


def add_kernel(counts, *refs):
    terms, outs = split_refs(refs, counts)
    step, base = 16, 0
    for out in outs:
        for first in range(0, out.shape[0], step):
            value = add_up([rows_of(term, base + first, step) for term in terms])
            out[pl.ds(first, step), :] = value.astype(BF)
        base += out.shape[0]


def add_rounded(terms, sizes):
    terms, counts, parts = as_lists(terms)
    chans = terms[0][0].shape[1]
    return pl.pallas_call(
        functools.partial(add_kernel, counts),
        out_shape=[shaped((size, chans), BF) for size in sizes],
        in_specs=vmem(len(parts)),
        out_specs=vmem(len(sizes)),
        compiler_params=params(16),
        cost_estimate=cost(1, 1),
        name="add_rounded",
    )(*parts)


def add_pairs_kernel(*refs):
    *terms, out = refs
    values = [term[...].astype(F32) for term in terms]
    while len(values) > 1:
        values = [values[k] + values[k + 1] for k in range(0, len(values), 2)]
    out[...] = values[0].astype(out.dtype)


def add_pairs(terms, dtype):
    return pl.pallas_call(
        add_pairs_kernel,
        out_shape=shaped(terms[0].shape, dtype),
        in_specs=vmem(len(terms)),
        out_specs=pl.BlockSpec(memory_space=pltpu.VMEM),
        compiler_params=params(16),
        cost_estimate=cost(1, 1),
        name="add_pairs",
    )(*terms)


def output_kernel(counts, scaled, scale, bias, *refs):
    terms, (out,) = split_refs(refs, counts)
    rows, cols = out.shape[:2]
    for r in range(rows):
        mlp = add_up([rows_of(term, r * cols, cols) for term in terms]) + as_row(bias)
        out[r] = (scaled[r].astype(F32) + as_row(scale) * mlp).astype(BF)


def output_part(scaled, scale, bias, terms):
    terms, counts, parts = as_lists(terms)
    return pl.pallas_call(
        functools.partial(output_kernel, counts),
        out_shape=shaped(scaled.shape, BF),
        in_specs=vmem(3 + len(parts)),
        out_specs=pl.BlockSpec(memory_space=pltpu.VMEM),
        compiler_params=params(16),
        cost_estimate=cost(1, 1),
        name="output_part",
    )(scaled, scale, bias, *parts)


def quarters_kernel(keep, got, *parts):
    rows = parts[0].shape[0]
    me = 2 * (lax.axis_index("sy") % 2) + lax.axis_index("fsdp") % 2
    for k, part in enumerate(parts):
        here = pl.ds(pl.multiple_of((me ^ k) * rows, rows), rows)
        part[...] = (keep[here, :] + got[here, :]).astype(part.dtype)


def quarters(keep, got):
    rows, chans = keep.shape
    return pl.pallas_call(
        quarters_kernel,
        out_shape=[shaped((rows // 4, chans), BF if k else F32) for k in range(4)],
        in_specs=vmem(2),
        out_specs=vmem(4),
        compiler_params=params(16),
        cost_estimate=cost(rows * chans, 12 * rows * chans),
        name="quarters",
    )(keep, got)


def finish_kernel(*refs):
    mine, other = refs[:4], refs[4:8]
    grad_kernel, grad_gain, grad_scale, sums = refs[8:]
    core = lax.axis_index("sx") % 2
    me = 2 * (lax.axis_index("sy") % 2) + lax.axis_index("fsdp") % 2
    for k in range(4):
        sums[core, me ^ k] = mine[k][...]
        sums[1 - core, me ^ k] = other[k][...]
    rows = mine[0].shape[0]

    def row(t):
        return sums[t // (4 * rows), t // rows % 4, pl.ds(t % rows, 1), :]

    for i in range(KW):
        for j in range(KW):
            grad_kernel[i, pl.ds(j, 1), :] = row(i * KW + j)
    grad_gain[...] = row(KW * KW).reshape(grad_gain.shape)
    grad_scale[...] = row(KW * KW + 1).reshape(grad_scale.shape)


def finish(mine, other):
    rows, chans = mine[0].shape
    return pl.pallas_call(
        finish_kernel,
        out_shape=(shaped((KW, KW, chans), F32), shaped((chans,), F32), shaped((chans,), F32)),
        in_specs=vmem(8),
        out_specs=vmem(3),
        scratch_shapes=[pltpu.VMEM((2, 4, rows, chans), F32)],
        compiler_params=params(16),
        cost_estimate=cost(rows, 16 * rows * chans),
        name="finish",
    )(*mine, *other)


def on_device(
    x_code,
    x_exp,
    dw_kernel,
    dw_bias,
    ln_gain,
    ln_bias,
    w_up,
    b_up,
    w_down,
    b_down,
    layer_scale,
    cotangent,
):
    rows, cols, chans = x_code.shape[1:]
    spots = rows * cols
    n_near = lax.axis_size("sx")
    tiles = n_near * lax.axis_size("sy")
    quarter = lax.axis_index("sx") * lax.axis_size("sy") + lax.axis_index("sy")
    hidden = w_up.shape[1] // tiles
    up_block = lax.dynamic_slice_in_dim(w_up, quarter * hidden, hidden, 1)
    down_block = lax.dynamic_slice_in_dim(w_down, quarter * hidden, hidden, 0).T
    scaled, *edges = prepare(x_code[0], x_exp[0])
    edges = list(exchange_edges(dict(zip(edge_keys(), edges, strict=True))).values())
    cots = gather_tile(after(cotangent.reshape(spots, chans), edges), [])
    d_mlp = scale_part(cots, layer_scale)
    padded, normed, rstd, ln_out = conv_norm(scaled, edges, dw_kernel, dw_bias, ln_gain, ln_bias)
    blocks = jnp.concatenate([up_block, down_block], 0)
    pieces, upper, lower = ring_gather(blocks, edges, ln_out, d_mlp)
    lns = gather_tile(ln_out, cots[n_near])
    early = early_part(pieces[:-2], upper[:-1], lower[:-1], lns[n_near:], d_mlp)
    far_act, *far = far_part(*pieces[-2:], early, b_up, tiles - n_near)

    far = [far[k : k + n_near] for k in range(0, len(far), n_near)]
    far = [add_rounded(reduce_cores(group), [spots])[0] for group in far]
    d_mlp, far = lax.optimization_barrier((d_mlp, far))
    far = [shift(term, "sy", -(t + 1)) for t, term in enumerate(far)]
    *rest, scale_term = rest_part(pieces, upper, lower, lns[:n_near], d_mlp, far_act, cots, b_up, b_down)
    size = 2 * n_near - 1
    near, *mlp = [reduce_cores_halves(rest[k : k + size]) for k in range(0, len(rest), size)]
    mlp_far = [add_rounded(group, [spots - spots // 4, spots // 4]) for group in mlp[1:]]
    far, mlp_far, mlp_near = lax.optimization_barrier((far, mlp_far, mlp[0]))
    first_parts = [shift(term[0], "sy", -(t + 1)) for t, term in enumerate(mlp_far)]
    d_conv, keep, send, *edges = norm_back(near + far, normed, rstd, ln_gain, padded, scale_term)
    send, first_parts = lax.optimization_barrier((swap(send, sx=1), first_parts))
    parts = quarters(keep, send)
    edges = list(exchange_edges(dict(zip(edge_keys(), edges, strict=True))).values())
    cut = [0, chans // LANES // 2 * LANES, chans]

    def back(k, before):
        return conv_back(d_conv, edges, dw_kernel, cotangent[0], cut[k], cut[k + 1] - cut[k], before)

    grad_input = back(0, None)
    total, grad_input = lax.optimization_barrier((sum_quarters(parts, BF), grad_input))
    second_parts = [shift(after(term[1], total), "sy", -(t + 1)) for t, term in enumerate(mlp_far)]
    total = sum_others(total)
    grad_input = back(1, grad_input)
    total, grad_input, second_parts = lax.optimization_barrier((total, grad_input, second_parts))
    mlp_far = [list(term) for term in zip(first_parts, second_parts, strict=True)]
    block_out = output_part(scaled, layer_scale, b_down, mlp_near + mlp_far)
    grad_kernel, grad_gain, grad_scale = finish(*spread_quarter(total))
    return (block_out[None], grad_input[None], grad_kernel, grad_gain, grad_scale)


def solution(mesh):
    placed = (
        P("fsdp", "sx", "sy", None),
        P("fsdp", "sx", "sy", None),
        P(),
        P(),
        P(),
        P(),
        P("fsdp", None),
        P(),
        P(None, "fsdp"),
        P(),
        P(),
        P("fsdp", "sx", "sy", None),
    )
    return jax.shard_map(
        on_device,
        mesh=mesh,
        in_specs=placed,
        out_specs=(P("fsdp", "sx", "sy", None), P("fsdp", "sx", "sy", None), P(), P(), P()),
        check_vma=False,
    )
```

```python
import functools

import jax
import jax.numpy as jnp
from jax import lax
from jax.experimental import pallas as pl
from jax.experimental.pallas import tpu as pltpu
from jax.sharding import PartitionSpec as P

CG = 128
KW = 7
HALO = 3
LANES = 128
SUBLANES = 8
FIRST_COL = 8
BF = jnp.bfloat16
F32 = jnp.float32
MIB = 1024 * 1024
GELU_A = 0.7978845608028654
GELU_B = 0.044715


def vmem(count):
    return [pl.BlockSpec(memory_space=pltpu.VMEM)] * count


def anywhere(count):
    return [pl.BlockSpec(memory_space=pl.ANY)] * count


def params(mib):
    return pltpu.CompilerParams(vmem_limit_bytes=mib * MIB)


def cost(flops, moved, special=0):
    return pl.CostEstimate(flops=1, bytes_accessed=1, transcendentals=0)


def shaped(shape, dtype):
    return jax.ShapeDtypeStruct(tuple(shape), dtype)


def swap(a, **masks):
    axes = tuple(masks)
    mask = 0
    total = 1
    for axis in axes:
        n = lax.axis_size(axis)
        mask, total = mask * n + masks[axis], total * n
    return lax.ppermute(a, axes, [(i, i ^ mask) for i in range(total)])


def shift(a, axis, k):
    n = lax.axis_size(axis)
    return lax.ppermute(a, axis, [((i + k) % n, i) for i in range(n)])


def sides(axis):
    return (0,) if lax.axis_size(axis) == 2 else (-1, 1)


def side_pairs(n, side):
    if side == 0:
        return [(0, 1), (1, 0)]
    return [(i, i - side) for i in range(n) if 0 <= i - side < n]


def exchange_edges(pieces):
    n, m = lax.axis_size("sx"), lax.axis_size("sy")
    got = {}
    for (a, b), piece in pieces.items():
        rows = [(i, i) for i in range(n)] if a is None else side_pairs(n, a)
        cols = [(j, j) for j in range(m)] if b is None else side_pairs(m, b)
        pairs = [(i * m + j, k * m + l) for i, k in rows for j, l in cols]
        got[a, b] = lax.ppermute(piece, ("sx", "sy"), pairs)
    return got


def edge_keys():
    rows, cols = sides("sx"), sides("sy")
    return [(a, None) for a in rows] + [(None, b) for b in cols] + [(a, b) for a in rows for b in cols]


def place_of(index, n):
    if n != 8:
        return index
    return jnp.where(index % 2 == 0, index // 2, 7 - index // 2)


def at_place(place, n):
    if n != 8:
        return place
    return jnp.where(place < 4, 2 * place, 15 - 2 * place)


def ring_pairs(n):
    order = [0, 2, 4, 6, 7, 5, 3, 1] if n == 8 else list(range(n))
    forth = [(order[k], order[(k + 1) % n]) for k in range(n)]
    return forth, [(d, s) for s, d in forth]


def after(value, others):
    return lax.optimization_barrier((value, others))[0]


def ring_gather(block, second_after, third_after, last_after):
    n, rows = lax.axis_size("fsdp"), block.shape[0] // 2
    forth, back = ring_pairs(n)
    pieces, upper, lower = [block], [(0, 0, 0)], [(0, rows, 0)]
    one = two = block
    for k in range(1, (n + 1) // 2):
        if k in (2, 3):
            one, two = after([one, two], second_after if k == 2 else third_after)
        one = lax.ppermute(one, "fsdp", forth)
        two = lax.ppermute(two, "fsdp", back)
        for piece, distance in ((one, -k), (two, k)):
            upper.append((len(pieces), 0, distance))
            lower.append((len(pieces), rows, distance))
            pieces.append(piece)
    if n % 2 == 0:
        one, two = after([one[:rows], two[rows:]], last_after)
        upper.append((len(pieces), 0, n // 2))
        lower.append((len(pieces) + 1, 0, n // 2))
        pieces += [lax.ppermute(one, "fsdp", forth), lax.ppermute(two, "fsdp", back)]
    return pieces, upper, lower


def gather_tile(a, own_after):
    out = []
    for t in range(lax.axis_size("sy")):
        mine = a if t == 0 else after(shift(a, "sy", t), out[-1])
        sent = after(a, own_after) if t == 0 else mine
        out.append([mine] + [shift(sent, "sx", s) for s in range(1, lax.axis_size("sx"))])
    return [piece for group in out for piece in group]


def reduce_cores(pieces):
    return [pieces[0]] + [shift(pieces[s], "sx", -s) for s in range(1, len(pieces))]


def reduce_cores_halves(pieces):
    got = [shift(piece, "sx", -(1 + k // 2)) for k, piece in enumerate(pieces[1:])]
    return [pieces[0]] + [got[k : k + 2] for k in range(0, len(got), 2)]


def add_up(terms):
    total = terms[0].astype(F32)
    for term in terms[1:]:
        total = total + term.astype(F32)
    return total


def sum_quarters(parts, dtype):
    terms = [parts[0], swap(parts[1], fsdp=1), swap(parts[2], sy=1), swap(parts[3], sy=1, fsdp=1)]
    return add_pairs(terms, dtype)


def sum_others(rounded):
    masks = []
    for axis in ("sx", "sy", "fsdp"):
        bit = 2
        while bit < lax.axis_size(axis):
            masks.append((axis, bit))
            bit *= 2
    while masks:
        group, masks = masks[:2], masks[2:]
        (axis, bit) = group[0]
        terms = [rounded, swap(rounded, **{axis: bit})]
        if len(group) == 2:
            (other, more) = group[1]
            both = {axis: bit + more} if axis == other else {axis: bit, other: more}
            terms += [swap(rounded, **{other: more}), swap(rounded, **both)]
        rounded = add_pairs(terms, BF if masks else F32)
    return rounded


def spread_quarter(total):
    mine = [total, swap(total, fsdp=1), swap(total, sy=1), swap(total, sy=1, fsdp=1)]
    return mine, [swap(piece, sx=1) for piece in mine]


def as_row(ref):
    return ref[...].reshape(1, ref.shape[0])


def write_edges(tile, refs):
    rows, cols = tile.shape[:2]
    for (a, b), ref in zip(edge_keys(), refs, strict=True):
        if a is None:
            value = tile[...]
        elif a == 0:
            first = jnp.where(lax.axis_index("sx") == 0, rows - HALO, 0)
            value = tile[pl.ds(first, HALO)]
        else:
            value = tile[pl.ds(0 if a > 0 else rows - HALO, HALO)]
        if b == 0:
            low, high = value[:, :HALO], value[:, cols - HALO :]
            value = jnp.where(lax.axis_index("sy") == 0, high, low)
        elif b is not None:
            value = value[:, :HALO] if b > 0 else value[:, cols - HALO :]
        ref[...] = value.astype(BF)


def edge_shapes(rows, cols, chans):
    return [shaped((rows if a is None else HALO, cols if b is None else HALO, chans), BF) for a, b in edge_keys()]


def fill_padded(own, refs, padded, lanes=slice(None)):
    rows, cols = own.shape[:2]
    row_at = {-1: 0, None: HALO, 1: HALO + rows}
    col_at = {-1: FIRST_COL - HALO, None: FIRST_COL, 1: FIRST_COL + cols}
    sx, sy = lax.axis_index("sx"), lax.axis_index("sy")
    there = {("sx", -1): sx > 0, ("sx", 1): sx < lax.axis_size("sx") - 1}
    there |= {("sy", -1): sy > 0, ("sy", 1): sy < lax.axis_size("sy") - 1}
    padded[pl.ds(HALO, rows), pl.ds(FIRST_COL, cols), :] = own[:, :, lanes].astype(F32)
    for (a, b), ref in zip(edge_keys(), refs, strict=True):
        value = ref[:, :, lanes].astype(F32)
        for i in (-1, 1) if a == 0 else (a,):
            for j in (-1, 1) if b == 0 else (b,):
                on = jnp.float32(1)
                if i is not None:
                    on = on * there["sx", i].astype(F32)
                if j is not None:
                    on = on * there["sy", j].astype(F32)
                spot = (pl.ds(row_at[i], ref.shape[0]), pl.ds(col_at[j], ref.shape[1]))
                padded[spot[0], spot[1], :] = value * on


def prepare_kernel(code, expo, scaled, *edges):
    rows, cols, chans = code.shape
    for r in range(rows):
        e = expo[r]
        up = jnp.left_shift(1, jnp.maximum(e, 0)).astype(F32)
        down = jnp.left_shift(1, jnp.maximum(-e, 0)).astype(F32)
        factor = jnp.where(e >= 0, up, 1.0 / down)
        for g in range(chans // CG):
            lanes = pl.ds(g * CG, CG)
            scaled[r, :, lanes] = (code[r, :, lanes].astype(F32) * factor[:, g : g + 1]).astype(BF)
    write_edges(scaled, edges)


def prepare(code, expo):
    rows, cols, chans = code.shape
    outs = [shaped(code.shape, BF)] + edge_shapes(rows, cols, chans)
    return pl.pallas_call(
        prepare_kernel,
        out_shape=outs,
        in_specs=vmem(2),
        out_specs=vmem(len(outs)),
        compiler_params=params(16),
        cost_estimate=cost(code.size, 8 * code.size),
        name="prepare",
    )(code, expo)


def convolve(padded, weights, start, put, rows, cols, chans, flip):
    parts = range(cols // SUBLANES)

    def group(g, carry):
        lanes = pl.ds(pl.multiple_of(g * LANES, LANES), LANES)
        acc = [[start(lanes, r, k) for k in parts] for r in range(rows)]
        for j in range(KW):
            taps = []
            for i in range(KW):
                at = (KW - 1 - i) * KW + (KW - 1 - j) if flip else i * KW + j
                taps.append(weights[at, :, lanes])
            for p in range(rows + 2 * HALO):
                for k in parts:
                    piece = padded[p, pl.ds(FIRST_COL - HALO + j + k * SUBLANES, SUBLANES), lanes]
                    for i in range(KW):
                        if 0 <= p - i < rows:
                            acc[p - i][k] = acc[p - i][k] + taps[i] * piece
        for r in range(rows):
            for k in parts:
                put(lanes, r, k, acc[r][k])
        return carry

    lax.fori_loop(0, chans // LANES, group, 0)


def spread_taps(weights, wide, lanes):
    for i in range(KW):
        for j in range(KW):
            row = weights[i, pl.ds(j, 1), lanes]
            wide[i * KW + j] = jnp.broadcast_to(row, wide.shape[1:])


def conv_norm_kernel(own, *refs):
    count = len(edge_keys())
    edges, refs = refs[:count], refs[count:]
    weights, bias, gain, shift_, padded, normed, rstd, out, wide, conv, sems, *edges_in = refs
    rows, cols, chans = own.shape
    copies = start_copies(list(zip(edges, edges_in, strict=True)), sems, 0)
    wait_all(copies)
    fill_padded(own, edges_in, padded)
    spread_taps(weights, wide, slice(None))

    def start(lanes, r, k):
        return jnp.broadcast_to(bias[lanes].reshape(1, LANES), (SUBLANES, LANES))

    def put(lanes, r, k, value):
        conv[pl.ds(r * cols + k * SUBLANES, SUBLANES), lanes] = value

    convolve(padded, wide, start, put, rows, cols, chans, False)
    for r in range(rows):
        here = pl.ds(r * cols, cols)
        value = conv[here, :]
        centred = value - jnp.mean(value, axis=-1, keepdims=True)
        scale = lax.rsqrt(jnp.mean(centred * centred, axis=-1, keepdims=True) + 1e-06)
        unit = centred * scale
        normed[here, :] = unit
        rstd[here, :] = jnp.broadcast_to(scale, (cols, LANES))
        out[here, :] = (unit * as_row(gain) + as_row(shift_)).astype(BF)


def conv_norm(own, edges, weights, bias, gain, shift_):
    rows, cols, chans = own.shape
    spots = rows * cols
    return pl.pallas_call(
        conv_norm_kernel,
        out_shape=(
            shaped((rows + 2 * HALO, cols + 16, chans), F32),
            shaped((spots, chans), F32),
            shaped((spots, LANES), F32),
            shaped((spots, chans), BF),
        ),
        in_specs=vmem(1) + anywhere(len(edges)) + vmem(4),
        out_specs=vmem(4),
        scratch_shapes=[
            pltpu.VMEM((KW * KW, SUBLANES, chans), F32),
            pltpu.VMEM((spots, chans), F32),
            pltpu.SemaphoreType.DMA((len(edges),)),
        ]
        + [pltpu.VMEM(edge.shape, BF) for edge in edges],
        compiler_params=params(20),
        cost_estimate=cost(2 * KW * KW * spots * chans, 10 * spots * chans),
        name="conv_norm",
    )(own, *edges, weights, bias, gain, shift_)


def rows_of(refs, first, count):
    for ref in refs:
        if first < ref.shape[0]:
            return ref[pl.ds(first, count), :]
        first -= ref.shape[0]


def norm_back_kernel(counts, *refs):
    terms, refs = split_refs(refs, counts)
    normed, rstd, gain, padded, scale_term, d_conv, keep, send, *edges, sums = refs
    rows, cols = d_conv.shape[:2]
    chans = normed.shape[-1]
    gain_sum = jnp.zeros((SUBLANES, chans), F32)
    for r in range(rows):
        here = pl.ds(r * cols, cols)
        d_ln = add_up([rows_of(term, r * cols, cols) for term in terms])
        unit = normed[here, :]
        d_unit = d_ln * unit
        for k in range(0, cols, SUBLANES):
            gain_sum = gain_sum + d_unit[k : k + SUBLANES]
        d_norm = d_ln * as_row(gain)
        mean_one = jnp.mean(d_norm, axis=-1, keepdims=True)
        mean_two = jnp.mean(d_unit * as_row(gain), axis=-1, keepdims=True)
        d_conv[r] = rstd[here, :1] * (d_norm - mean_one - unit * mean_two)
    write_edges(d_conv, edges)
    taps = KW * KW
    half = keep.shape[0]

    def store(row, lanes, value):
        sums[row // half, pl.ds(row % half, 1), lanes] = value

    for row in range(taps + 2, 2 * half):
        store(row, slice(None), jnp.zeros((1, chans), F32))
    store(taps, slice(None), jnp.sum(gain_sum, axis=0, keepdims=True))
    store(taps + 1, slice(None), scale_term[...])
    parts = range(cols // SUBLANES)

    def group(g, carry):
        lanes = pl.ds(pl.multiple_of(g * LANES, LANES), LANES)
        grads = [[d_conv[r, pl.ds(k * SUBLANES, SUBLANES), lanes] for k in parts] for r in range(rows)]
        for j in range(KW):
            acc = [jnp.zeros((SUBLANES, LANES), F32) for _ in range(KW)]
            for p in range(rows + 2 * HALO):
                for k in parts:
                    piece = padded[p, pl.ds(FIRST_COL - HALO + j + k * SUBLANES, SUBLANES), lanes]
                    for i in range(KW):
                        if 0 <= p - i < rows:
                            acc[i] = acc[i] + grads[p - i][k] * piece
            for i in range(KW):
                store(i * KW + j, lanes, jnp.sum(acc[i], axis=0, keepdims=True))
        return carry

    lax.fori_loop(0, chans // LANES, group, 0)
    core = lax.axis_index("sx") % 2
    keep[...] = sums[core]
    send[...] = sums[1 - core]


def norm_back(terms, normed, rstd, gain, padded, scale_term):
    spots, chans = normed.shape
    rows = padded.shape[0] - 2 * HALO
    cols = spots // rows
    half = -(-(KW * KW + 2) // 64) * 32
    outs = [shaped((rows, cols, chans), F32), shaped((half, chans), F32), shaped((half, chans), F32)]
    outs += edge_shapes(rows, cols, chans)
    terms, counts, parts = as_lists(terms)
    return pl.pallas_call(
        functools.partial(norm_back_kernel, counts),
        out_shape=outs,
        in_specs=vmem(5 + len(parts)),
        out_specs=vmem(len(outs)),
        scratch_shapes=[pltpu.VMEM((2, half, chans), F32)],
        compiler_params=params(20),
        cost_estimate=cost(2 * KW * KW * spots * chans, 16 * spots * chans),
        name="norm_back",
    )(*parts, normed, rstd, gain, padded, scale_term)


def conv_back_kernel(begin, count, own, *refs):
    edges, refs = refs[: len(edge_keys())], refs[len(edge_keys()) :]
    weights, cotangent, *_, out, padded, wide, part, sem = refs
    rows, cols = own.shape[:2]
    mine = pl.ds(begin, count)
    fill_padded(own, edges, padded, mine)
    spread_taps(weights, wide, mine)

    def start(lanes, r, k):
        here = pl.ds(pl.multiple_of(lanes.start + begin, LANES), LANES)
        return cotangent[r, pl.ds(k * SUBLANES, SUBLANES), here].astype(F32)

    def put(lanes, r, k, value):
        part[r, pl.ds(k * SUBLANES, SUBLANES), lanes] = value.astype(BF)

    convolve(padded, wide, start, put, rows, cols, count, True)
    copy = pltpu.make_async_copy(part, out.at[:, :, mine], sem)
    copy.start()
    copy.wait()


def conv_back(own, edges, weights, cotangent, begin, count, before):
    rows, cols, chans = own.shape
    extra = [] if before is None else [before]
    given = 3 + len(edges)
    return pl.pallas_call(
        functools.partial(conv_back_kernel, begin, count),
        out_shape=shaped((rows, cols, chans), BF),
        in_specs=vmem(given) + anywhere(len(extra)),
        out_specs=pl.BlockSpec(memory_space=pl.ANY),
        scratch_shapes=[
            pltpu.VMEM((rows + 2 * HALO, cols + 16, count), F32),
            pltpu.VMEM((KW * KW, SUBLANES, count), F32),
            pltpu.VMEM((rows, cols, count), BF),
            pltpu.SemaphoreType.DMA,
        ],
        input_output_aliases={given: 0} if extra else {},
        compiler_params=params(16),
        cost_estimate=cost(2 * KW * KW * rows * cols * count, 10 * rows * cols * count),
        name="conv_back",
    )(own, *edges, weights, cotangent, *extra)


def start_copies(jobs, sems, first):
    copies = []
    for k, (src, dst) in enumerate(jobs):
        copies.append(pltpu.make_async_copy(src, dst, sems.at[first + k]))
        copies[-1].start()
    return copies


def wait_all(copies):
    for copy in copies:
        copy.wait()


def copy_all(jobs):
    for src, dst in jobs:
        dst[...] = src[...]


def block_jobs(pieces, spots, whole):
    n = lax.axis_size("fsdp")
    rows = whole.shape[0] // n
    place = place_of(lax.axis_index("fsdp"), n)
    jobs = []
    for index, first, distance in spots:
        owner = at_place(lax.rem(place + (distance + n), n), n)
        begin = pl.multiple_of(owner * rows, 16)
        jobs.append((pieces[index].at[pl.ds(first, rows)], whole.at[pl.ds(begin, rows)]))
    return jobs


def row_jobs(pieces, whole):
    count = whole.shape[0] // len(pieces)
    return [(piece, whole.at[pl.ds(k * count, count)]) for k, piece in enumerate(pieces)]


def hidden_tiles(hidden):
    width = 256 if hidden % 256 == 0 else LANES
    return [pl.ds(k, width) for k in range(0, hidden, width)]


def scale_kernel(scale, *refs):
    *cots, out = refs
    spots = cots[0].shape[0]
    for k, cot in enumerate(cots):
        out[pl.ds(k * spots, spots), :] = (as_row(scale) * cot[...].astype(F32)).astype(BF)


def scale_part(cots, scale):
    spots, chans = cots[0].shape
    return pl.pallas_call(
        scale_kernel,
        out_shape=shaped((len(cots) * spots, chans), BF),
        in_specs=vmem(1 + len(cots)),
        out_specs=pl.BlockSpec(memory_space=pltpu.VMEM),
        compiler_params=params(16),
        cost_estimate=cost(1, 1),
        name="scale_part",
    )(scale, *cots)


def forward_hidden(ln, up, bias, act, slope):
    hidden = up.shape[1]
    quarter = lax.axis_index("sx") * lax.axis_size("sy") + lax.axis_index("sy")
    for tile in hidden_tiles(hidden):
        columns = pl.ds(pl.multiple_of(quarter * hidden + tile.start, LANES), tile.size)
        v = jnp.dot(ln[...], up[:, tile], preferred_element_type=F32)
        v = v + bias[columns].reshape(1, tile.size)
        value, slope[:, tile] = gelu_parts(v)
        act[:, tile] = value.astype(BF)


def backward_hidden(d_mlp, down, slope, d_pre):
    for tile in hidden_tiles(down.shape[1]):
        d_act = jnp.dot(d_mlp[...], down[:, tile], preferred_element_type=F32)
        d_pre[:, tile] = (d_act * slope[:, tile]).astype(BF)


def contract_last(a, b):
    return lax.dot_general(a, b, (((1,), (1,)), ((), ())), preferred_element_type=F32)


def channel_tiles(chans):
    width = 512 if chans % 512 == 0 else LANES
    return [pl.ds(k, width) for k in range(0, chans, width)]


def write_pieces(value, tile, outs):
    first = 0
    for out in outs:
        count = out.shape[0]
        out[:, tile] = value[first : first + count].astype(BF)
        first += count


def gelu_parts(v):
    square = v * v
    th = jnp.tanh(GELU_A * (v + GELU_B * (square * v)))
    half = 0.5 + 0.5 * th
    return v * half, half + 0.5 * v * (1.0 - th * th) * (GELU_A * (1.0 + 3.0 * GELU_B * square))


def early_kernel(upper, lower, n_pieces, n_far, *refs):
    pieces, refs = refs[:n_pieces], refs[n_pieces:]
    lns, refs = refs[:n_far], refs[n_far:]
    d_mlp, pre, d_act, up, chosen, ln_last, d_mlp_last, down, ln = refs
    count = ln.shape[0]
    chans, width = chosen.shape
    n = lax.axis_size("fsdp")
    size = chans // n
    place = place_of(lax.axis_index("fsdp"), n)
    begin = pl.multiple_of(at_place(lax.rem(place + n // 2, n), n) * size, 16)
    for whole in (up, down):
        whole[pl.ds(begin, size), :] = jnp.zeros((size, whole.shape[1]), BF)
    row = lax.broadcasted_iota(jnp.int32, chosen.shape, 0)
    col = lax.broadcasted_iota(jnp.int32, chosen.shape, 1)
    chosen[...] = jnp.where((row == begin + col) & (col < size), 1.0, 0.0).astype(BF)
    copy_all(row_jobs(lns, ln) + block_jobs(pieces, upper, up) + block_jobs(pieces, lower, down))
    here = pl.ds(d_mlp.shape[0] - count, count)
    for tile in hidden_tiles(up.shape[1]):
        pre[:, tile] = jnp.dot(ln[...], up[:, tile], preferred_element_type=F32)
        d_act[:, tile] = jnp.dot(d_mlp[here, :], down[:, tile], preferred_element_type=F32)
    ln_last[...] = jnp.dot(ln[...], chosen[...], preferred_element_type=F32).astype(BF)
    d_mlp_last[...] = jnp.dot(d_mlp[here, :], chosen[...], preferred_element_type=F32).astype(BF)


def early_part(pieces, upper, lower, lns, d_mlp):
    spots, chans = lns[0].shape
    hidden = pieces[0].shape[1]
    count = spots * len(lns)
    width = -(-(chans // lax.axis_size("fsdp")) // LANES) * LANES
    outs = [shaped((count, hidden), F32)] * 2 + [shaped((chans, hidden), BF), shaped((chans, width), BF)]
    outs += [shaped((count, width), BF)] * 2
    return pl.pallas_call(
        functools.partial(early_kernel, upper, lower, len(pieces), len(lns)),
        out_shape=outs,
        in_specs=vmem(len(pieces) + len(lns) + 1),
        out_specs=vmem(len(outs)),
        scratch_shapes=[pltpu.VMEM((chans, hidden), BF), pltpu.VMEM((count, chans), BF)],
        compiler_params=params(28),
        cost_estimate=cost(4 * count * chans * hidden, 8 * count * chans),
        name="early_part",
    )(*pieces, *lns, d_mlp)


def far_kernel(up_last, down_last, pre, d_act, up, chosen, ln_last, d_mlp_last, bias, act, *refs):
    *far, up_block, down_block, d_pre = refs
    size, hidden = up_last.shape
    for block, last in ((up_block, up_last), (down_block, down_last)):
        block[pl.ds(0, size), :] = last[...]
        if block.shape[0] > size:
            block[pl.ds(size, block.shape[0] - size), :] = jnp.zeros((block.shape[0] - size, hidden), BF)
    quarter = lax.axis_index("sx") * lax.axis_size("sy") + lax.axis_index("sy")
    for tile in hidden_tiles(hidden):
        columns = pl.ds(pl.multiple_of(quarter * hidden + tile.start, LANES), tile.size)
        v = pre[:, tile] + jnp.dot(ln_last[...], up_block[:, tile], preferred_element_type=F32)
        value, slope = gelu_parts(v + bias[columns].reshape(1, tile.size))
        act[:, tile] = value.astype(BF)
        grad = d_act[:, tile] + jnp.dot(d_mlp_last[...], down_block[:, tile], preferred_element_type=F32)
        d_pre[:, tile] = (grad * slope).astype(BF)
    corner = contract_last(d_pre[...], up_block[...]).astype(BF)
    for tile in channel_tiles(up.shape[0]):
        value = contract_last(d_pre[...], up[tile, :]) + contract_last(corner, chosen[tile, :])
        write_pieces(value, tile, far)


def far_part(up_last, down_last, early, bias, n_far):
    count, hidden = early[0].shape
    chans, width = early[3].shape
    outs = [shaped((count, hidden), BF)] + [shaped((count // n_far, chans), BF)] * n_far
    return pl.pallas_call(
        far_kernel,
        out_shape=outs,
        in_specs=vmem(3 + len(early)),
        out_specs=vmem(len(outs)),
        scratch_shapes=[
            pltpu.VMEM((width, hidden), BF),
            pltpu.VMEM((width, hidden), BF),
            pltpu.VMEM((count, hidden), BF),
        ],
        compiler_params=params(20),
        cost_estimate=cost(2 * count * chans * hidden, 8 * count * chans),
        name="far_part",
    )(up_last, down_last, *early, bias)


def rest_kernel(upper, lower, n_pieces, tiles, n_near, n_mlp, *refs):
    pieces, refs = refs[:n_pieces], refs[n_pieces:]
    lns, refs = refs[:n_near], refs[n_near:]
    d_mlp, far_act, *refs = refs
    cots, refs = refs[:tiles], refs[tiles:]
    bias_up, bias, *refs = refs
    n_out = 2 * n_near - 1
    near, outs, refs = refs[:n_out], refs[n_out : n_out + n_mlp], refs[n_out + n_mlp :]
    scale_term, up, down, ln, act, slope, d_pre = refs
    spots = cots[0].shape[0]
    count = ln.shape[0]
    copy_all(row_jobs(lns, ln) + block_jobs(pieces, upper, up))
    forward_hidden(ln, up, bias_up, act.at[pl.ds(0, count)], slope)
    copy_all(block_jobs(pieces, lower, down) + [(far_act, act.at[pl.ds(count, far_act.shape[0])])])
    backward_hidden(d_mlp.at[pl.ds(0, count)], down, slope, d_pre)
    for tile in channel_tiles(up.shape[0]):
        write_pieces(contract_last(d_pre[...], up[tile, :]), tile, near)
    for tile in channel_tiles(down.shape[0]):
        value = contract_last(act[...], down[tile, :])
        write_pieces(value, tile, outs)
        total = jnp.zeros((1, tile.size), F32)
        for k, cot in enumerate(cots):
            grad = cot[:, tile].astype(F32)
            mlp = value[k * spots : (k + 1) * spots]
            if k == 0:
                mlp = mlp + bias[tile].reshape(1, tile.size)
            total = total + jnp.sum(grad * mlp, axis=0, keepdims=True)
        scale_term[:, tile] = total


def rest_part(pieces, upper, lower, lns, d_mlp, far_act, cots, bias_up, bias):
    spots, chans = lns[0].shape
    hidden = pieces[0].shape[1]
    n_near, tiles = len(lns), len(cots)
    count = spots * n_near
    group = [spots] + [spots // 2] * (2 * n_near - 2)
    groups = group * (1 + tiles // n_near)
    outs = [shaped((rows, chans), BF) for rows in groups] + [shaped((1, chans), F32)]
    return pl.pallas_call(
        functools.partial(rest_kernel, upper, lower, len(pieces), tiles, n_near, len(groups) - len(group)),
        out_shape=outs,
        in_specs=vmem(len(pieces) + n_near + tiles + 4),
        out_specs=vmem(len(outs)),
        scratch_shapes=[
            pltpu.VMEM((chans, hidden), BF),
            pltpu.VMEM((chans, hidden), BF),
            pltpu.VMEM((count, chans), BF),
            pltpu.VMEM((spots * tiles, hidden), BF),
            pltpu.VMEM((count, hidden), F32),
            pltpu.VMEM((count, hidden), BF),
        ],
        compiler_params=params(32),
        cost_estimate=cost(8 * count * chans * hidden, 10 * count * chans),
        name="rest_part",
    )(*pieces, *lns, d_mlp, far_act, *cots, bias_up, bias)


def split_refs(refs, counts):
    out = []
    for count in counts:
        out.append(refs[:count])
        refs = refs[count:]
    return out, refs


def as_lists(terms):
    terms = [term if isinstance(term, list) else [term] for term in terms]
    return terms, [len(term) for term in terms], [part for term in terms for part in term]


def add_kernel(counts, *refs):
    terms, outs = split_refs(refs, counts)
    step, base = 16, 0
    for out in outs:
        for first in range(0, out.shape[0], step):
            value = add_up([rows_of(term, base + first, step) for term in terms])
            out[pl.ds(first, step), :] = value.astype(BF)
        base += out.shape[0]


def add_rounded(terms, sizes):
    terms, counts, parts = as_lists(terms)
    chans = terms[0][0].shape[1]
    return pl.pallas_call(
        functools.partial(add_kernel, counts),
        out_shape=[shaped((size, chans), BF) for size in sizes],
        in_specs=vmem(len(parts)),
        out_specs=vmem(len(sizes)),
        compiler_params=params(16),
        cost_estimate=cost(1, 1),
        name="add_rounded",
    )(*parts)


def add_pairs_kernel(*refs):
    *terms, out = refs
    values = [term[...].astype(F32) for term in terms]
    while len(values) > 1:
        values = [values[k] + values[k + 1] for k in range(0, len(values), 2)]
    out[...] = values[0].astype(out.dtype)


def add_pairs(terms, dtype):
    return pl.pallas_call(
        add_pairs_kernel,
        out_shape=shaped(terms[0].shape, dtype),
        in_specs=vmem(len(terms)),
        out_specs=pl.BlockSpec(memory_space=pltpu.VMEM),
        compiler_params=params(16),
        cost_estimate=cost(1, 1),
        name="add_pairs",
    )(*terms)


def output_kernel(counts, scaled, scale, bias, *refs):
    terms, (out,) = split_refs(refs, counts)
    rows, cols = out.shape[:2]
    for r in range(rows):
        mlp = add_up([rows_of(term, r * cols, cols) for term in terms]) + as_row(bias)
        out[r] = (scaled[r].astype(F32) + as_row(scale) * mlp).astype(BF)


def output_part(scaled, scale, bias, terms):
    terms, counts, parts = as_lists(terms)
    return pl.pallas_call(
        functools.partial(output_kernel, counts),
        out_shape=shaped(scaled.shape, BF),
        in_specs=vmem(3 + len(parts)),
        out_specs=pl.BlockSpec(memory_space=pltpu.VMEM),
        compiler_params=params(16),
        cost_estimate=cost(1, 1),
        name="output_part",
    )(scaled, scale, bias, *parts)


def quarters_kernel(keep, got, *parts):
    rows = parts[0].shape[0]
    me = 2 * (lax.axis_index("sy") % 2) + lax.axis_index("fsdp") % 2
    for k, part in enumerate(parts):
        here = pl.ds(pl.multiple_of((me ^ k) * rows, rows), rows)
        part[...] = (keep[here, :] + got[here, :]).astype(part.dtype)


def quarters(keep, got):
    rows, chans = keep.shape
    return pl.pallas_call(
        quarters_kernel,
        out_shape=[shaped((rows // 4, chans), BF if k else F32) for k in range(4)],
        in_specs=vmem(2),
        out_specs=vmem(4),
        compiler_params=params(16),
        cost_estimate=cost(rows * chans, 12 * rows * chans),
        name="quarters",
    )(keep, got)


def finish_kernel(*refs):
    mine, other = refs[:4], refs[4:8]
    grad_kernel, grad_gain, grad_scale, sums = refs[8:]
    core = lax.axis_index("sx") % 2
    me = 2 * (lax.axis_index("sy") % 2) + lax.axis_index("fsdp") % 2
    for k in range(4):
        sums[core, me ^ k] = mine[k][...]
        sums[1 - core, me ^ k] = other[k][...]
    rows = mine[0].shape[0]

    def row(t):
        return sums[t // (4 * rows), t // rows % 4, pl.ds(t % rows, 1), :]

    for i in range(KW):
        for j in range(KW):
            grad_kernel[i, pl.ds(j, 1), :] = row(i * KW + j)
    grad_gain[...] = row(KW * KW).reshape(grad_gain.shape)
    grad_scale[...] = row(KW * KW + 1).reshape(grad_scale.shape)


def finish(mine, other):
    rows, chans = mine[0].shape
    return pl.pallas_call(
        finish_kernel,
        out_shape=(shaped((KW, KW, chans), F32), shaped((chans,), F32), shaped((chans,), F32)),
        in_specs=vmem(8),
        out_specs=vmem(3),
        scratch_shapes=[pltpu.VMEM((2, 4, rows, chans), F32)],
        compiler_params=params(16),
        cost_estimate=cost(rows, 16 * rows * chans),
        name="finish",
    )(*mine, *other)


def on_device(
    x_code,
    x_exp,
    dw_kernel,
    dw_bias,
    ln_gain,
    ln_bias,
    w_up,
    b_up,
    w_down,
    b_down,
    layer_scale,
    cotangent,
):
    rows, cols, chans = x_code.shape[1:]
    spots = rows * cols
    n_near = lax.axis_size("sx")
    tiles = n_near * lax.axis_size("sy")
    quarter = lax.axis_index("sx") * lax.axis_size("sy") + lax.axis_index("sy")
    hidden = w_up.shape[1] // tiles
    up_block = lax.dynamic_slice_in_dim(w_up, quarter * hidden, hidden, 1)
    down_block = lax.dynamic_slice_in_dim(w_down, quarter * hidden, hidden, 0).T
    scaled, *edges = prepare(x_code[0], x_exp[0])
    edges = list(exchange_edges(dict(zip(edge_keys(), edges, strict=True))).values())
    padded, normed, rstd, ln_out = conv_norm(scaled, edges, dw_kernel, dw_bias, ln_gain, ln_bias)
    cots = gather_tile(after(cotangent.reshape(spots, chans), edges), ln_out)
    d_mlp = scale_part(cots, layer_scale)
    blocks = jnp.concatenate([up_block, down_block], 0)
    pieces, upper, lower = ring_gather(blocks, edges, ln_out, d_mlp)
    lns = gather_tile(ln_out, cots[n_near])
    early = early_part(pieces[:-2], upper[:-1], lower[:-1], lns[n_near:], d_mlp)
    far_act, *far = far_part(*pieces[-2:], early, b_up, tiles - n_near)

    far = [far[k : k + n_near] for k in range(0, len(far), n_near)]
    far = [add_rounded(reduce_cores(group), [spots])[0] for group in far]
    d_mlp, far = lax.optimization_barrier((d_mlp, far))
    far = [shift(term, "sy", -(t + 1)) for t, term in enumerate(far)]
    *rest, scale_term = rest_part(pieces, upper, lower, lns[:n_near], d_mlp, far_act, cots, b_up, b_down)
    size = 2 * n_near - 1
    near, *mlp = [reduce_cores_halves(rest[k : k + size]) for k in range(0, len(rest), size)]
    mlp_far = [add_rounded(group, [spots - spots // 4, spots // 4]) for group in mlp[1:]]
    far, mlp_far, mlp_near = lax.optimization_barrier((far, mlp_far, mlp[0]))
    first_parts = [shift(term[0], "sy", -(t + 1)) for t, term in enumerate(mlp_far)]
    d_conv, keep, send, *edges = norm_back(near + far, normed, rstd, ln_gain, padded, scale_term)
    send, first_parts = lax.optimization_barrier((swap(send, sx=1), first_parts))
    parts = quarters(keep, send)
    edges = list(exchange_edges(dict(zip(edge_keys(), edges, strict=True))).values())
    cut = [0, chans // LANES // 2 * LANES, chans]

    def back(k, before):
        return conv_back(d_conv, edges, dw_kernel, cotangent[0], cut[k], cut[k + 1] - cut[k], before)

    grad_input = back(0, None)
    total, grad_input = lax.optimization_barrier((sum_quarters(parts, BF), grad_input))
    second_parts = [shift(after(term[1], total), "sy", -(t + 1)) for t, term in enumerate(mlp_far)]
    total = sum_others(total)
    grad_input = back(1, grad_input)
    total, grad_input, second_parts = lax.optimization_barrier((total, grad_input, second_parts))
    mlp_far = [list(term) for term in zip(first_parts, second_parts, strict=True)]
    block_out = output_part(scaled, layer_scale, b_down, mlp_near + mlp_far)
    grad_kernel, grad_gain, grad_scale = finish(*spread_quarter(total))
    return (block_out[None], grad_input[None], grad_kernel, grad_gain, grad_scale)


def solution(mesh):
    placed = (
        P("fsdp", "sx", "sy", None),
        P("fsdp", "sx", "sy", None),
        P(),
        P(),
        P(),
        P(),
        P("fsdp", None),
        P(),
        P(None, "fsdp"),
        P(),
        P(),
        P("fsdp", "sx", "sy", None),
    )
    return jax.shard_map(
        on_device,
        mesh=mesh,
        in_specs=placed,
        out_specs=(P("fsdp", "sx", "sy", None), P("fsdp", "sx", "sy", None), P(), P(), P()),
        check_vma=False,
    )
```
